32 devices in a mesh: gene: 4 (over z), cell: 8 (over y, x, core).
Axes of the slice: x: 2, y: 2, z: 4, core: 2. Of those that a mesh axis runs over, the one named last changes fastest.
Arguments:
- counts: int32 [16384, 4096], P('gene', 'cell'), may hold values from 0 to 2047, as said below
- w1: bfloat16 [16384, 512], P(('gene', 'cell')), may hold values from 0.099609375 to 2
- h1: float32 [512, 4096], P(None, 'cell'), may hold values from 0.1 to 2
- w2: float32 [512, 64], replicated, may hold values from 0.1 to 2
- h2: float32 [64, 4096], P(None, 'cell'), may hold values from 0.005 to 0.1
Outputs:
- w1_new: bfloat16 [16384, 512], P(('gene', 'cell'))
- h1_new: float32 [512, 4096], P(None, 'cell')
- w2_new: float32 [512, 64], replicated
- h2_new: float32 [64, 4096], P(None, 'cell')
The draws below stay inside these ranges and needn't reach their ends.
Inputs may be any that keep to these rules, and one draw needn't show every extreme that they name: `counts`: counts are whole numbers; a gene's and a cell's typical depth vary, and cells later in the order run deeper.
All inputs are finite; a program needn't handle non-finite values.
Results may differ from the reference program's by a relative error of at most 0.0013.
The reference program's roundings to bfloat16 on the way count: a program that leaves them out, or rounds other values in their place, can miss the bound.
Values may be sent and summed in bfloat16 or wider, within the bound.
No kernel may reach another device: no remote copies, remote signals or barrier semaphores. Data moves between devices by JAX's collectives and lax.ppermute only.
A program may use at most 64 MiB of HBM per device.

```python
import math
import jax
import jax.numpy as jnp
from jax import lax

G = 16384
K1 = 512
K2 = 64
C = 4096


def draw_counts(key, part):
    key_cell = jax.random.fold_in(key, 11)
    key_gene = jax.random.fold_in(key, 12)
    key_value = jax.random.fold_in(key, 13)
    column = jnp.arange(C, dtype=jnp.int32)
    depth_top = 16 + 48 * (column + 1) // C
    cell_level = jax.random.randint(key_cell, (C,), 1, depth_top + 1)
    gene_level = jax.random.randint(key_gene, (G,), 1, 9)
    ceiling = 4 * gene_level[:, None] * cell_level[None, :] - 1
    return jax.random.randint(key_value, (G, C), 0, ceiling + 1)


def block_scale(own_key, extent, cuts, smallest, largest):
    gain, own = 1.0, jax.random.fold_in(own_key, 6)
    for axis_at, parts in cuts:
        steps = jnp.exp(jax.random.uniform(jax.random.fold_in(own, axis_at), (parts,), jnp.float32, smallest / len(cuts), largest / len(cuts)))
        gain = gain * jnp.repeat(steps, extent[axis_at] // parts).reshape([-1 if axis == axis_at else 1 for axis in range(len(extent))])
    return gain


def setup_inputs(seed: int = 0) -> dict:
    streams_of = jax.random.split(jax.random.key(seed), 6)
    counts = draw_counts(jax.random.fold_in(streams_of[5], 71), 0)
    w1 = jnp.clip(jnp.exp(math.log(2.0) - 2.9996462 * jax.random.uniform(streams_of[1], (G, K1), jnp.float32) ** block_scale(streams_of[1], (G, K1), ((0, 32),), -0.2, 0.2)), 0.099609375, 2.0).astype(jnp.bfloat16)
    h1 = jnp.clip(jnp.exp(math.log(2.0) - 2.9957323 * jax.random.uniform(streams_of[2], (K1, C), jnp.float32) ** block_scale(streams_of[2], (K1, C), ((1, 8),), -0.2, 0.2)), 0.1, 2.0)
    w2 = jnp.clip(jnp.exp(jax.random.uniform(streams_of[3], (K1, K2), jnp.float32, math.log(0.1), math.log(2.0))), 0.1, 2.0)
    h2 = jnp.clip(jnp.exp(math.log(0.1) - 2.9957323 * jax.random.uniform(streams_of[4], (K2, C), jnp.float32) ** block_scale(streams_of[4], (K2, C), ((1, 8),), -0.2, 0.2)), 0.005, 0.1)
    return {"counts": counts, "w1": w1, "h1": h1, "w2": w2, "h2": h2}


def reference(counts, w1, h1, w2, h2):
    hi = lax.Precision.HIGHEST
    block = 512
    nblocks = G // block
    w1_blocks = w1.reshape(nblocks, block, K1)
    v_blocks = counts.reshape(nblocks, block, C)
    h1_low = h1.astype(jnp.bfloat16)
    colsum = jnp.sum(w1.astype(jnp.float32), axis=0)

    def first(acc, pair):
        wb, vb = pair
        approx = jnp.dot(wb, h1_low, preferred_element_type=jnp.float32)
        ratio = (vb.astype(jnp.float32) / approx).astype(jnp.bfloat16)
        return acc + jnp.dot(wb.T, ratio, preferred_element_type=jnp.float32), None

    h1_num, unused = lax.scan(first, jnp.zeros((K1, C), jnp.float32), (w1_blocks, v_blocks))
    h1_new = h1 * h1_num / colsum[:, None]
    h1_low2 = h1_new.astype(jnp.bfloat16)

    def second(pair):
        wb, vb = pair
        approx = jnp.dot(wb, h1_low2, preferred_element_type=jnp.float32)
        ratio = (vb.astype(jnp.float32) / approx).astype(jnp.bfloat16)
        return jnp.dot(ratio, h1_low2.T, preferred_element_type=jnp.float32)

    w1_num = lax.map(second, (w1_blocks, v_blocks)).reshape(G, K1)
    rowsum = jnp.sum(h1_new, axis=1)
    w1_new = (w1.astype(jnp.float32) * w1_num / rowsum[None, :]).astype(jnp.bfloat16)

    ratio3 = h1_new / jnp.dot(w2, h2, precision=hi)
    h2_new = h2 * jnp.dot(w2.T, ratio3, precision=hi) / jnp.sum(w2, axis=0)[:, None]
    ratio4 = h1_new / jnp.dot(w2, h2_new, precision=hi)
    w2_num = jnp.dot(ratio4, h2_new.T, precision=hi)
    w2_new = w2 * w2_num / jnp.sum(h2_new, axis=1)[None, :]
    return w1_new, h1_new, w2_new, h2_new
```

```python
import functools

import jax
import jax.numpy as jnp
from jax import lax
from jax.experimental import pallas as pl
from jax.experimental.pallas import tpu as pltpu
from jax.sharding import PartitionSpec as P

F32 = jnp.float32
BF16 = jnp.bfloat16
PAD = 16
VMEM_LIMIT = 56 * 1024 * 1024


def params():
    return pltpu.CompilerParams(vmem_limit_bytes=VMEM_LIMIT)


def mm(a, b, dims):
    return lax.dot_general(a, b, ((dims[:1], dims[1:]), ((), ())), preferred_element_type=F32)


def encode(x, out_ref):
    rows = x.shape[0]
    top = jnp.maximum(jnp.max(x, axis=0, keepdims=True), 1e-30)
    power = jnp.ceil(jnp.log2(top))
    q = jnp.minimum(x * (jnp.exp2(-power) * 65535.0) + 0.5, 65535.0)
    out_ref[:rows, :] = (q.astype(jnp.int32) - 32768).astype(jnp.int16)
    out_ref[rows:, :] = jnp.broadcast_to(power, (PAD, x.shape[1])).astype(jnp.int32).astype(jnp.int16)


def decode(ref):
    rows = ref.shape[0] - PAD
    power = ref[rows:, :].astype(jnp.int32).astype(F32)[:1]
    unit = jnp.exp2(power) * (1.0 / 65535.0)
    return (ref[:rows, :].astype(jnp.int32) + 32768).astype(F32) * unit


def coded(rows, cols):
    return jax.ShapeDtypeStruct((rows + PAD, cols), jnp.int16)


def whole_spec(shape):
    return pl.BlockSpec(shape, lambda *_: (0,) * len(shape))


def pick(pieces, scratch):
    for k, piece in enumerate(pieces):
        @pl.when(pl.program_id(0) == k)
        def _():
            scratch[...] = piece[...]


def quotient(v_ref, approx):
    return (v_ref[...].astype(jnp.int32).astype(F32) / approx).astype(BF16)


def first_body(n, has_acc, *refs):
    _, _, *pieces = refs[: n + 2]
    ha, hb, va, vb, *rest = refs[n + 2 :]
    if has_acc:
        acc_a_in, acc_b_in, acc_a, acc_b, scratch = rest
    else:
        acc_a, acc_b, scratch = rest
    pick(pieces, scratch)

    @pl.when(pl.program_id(0) == 0)
    def _():
        if has_acc:
            acc_a[...] = acc_a_in[...]
            acc_b[...] = acc_b_in[...]
        else:
            acc_a[...] = jnp.zeros_like(acc_a)
            acc_b[...] = jnp.zeros_like(acc_b)

    w = scratch[...]
    for h, v, acc in ((ha, va, acc_a), (hb, vb, acc_b)):
        ratio = quotient(v, mm(w, h[...], (1, 0)))
        acc[...] += mm(w, ratio, (0, 0))


def first(pieces, at_a, at_b, ha, hb, va, vb, acc=None):
    n, (t, k) = len(pieces), pieces[0].shape
    cells = va.shape[1]
    num = jax.ShapeDtypeStruct((k, cells), F32)
    in_specs = [whole_spec((t, k))] * n + [whole_spec((k, cells))] * 2
    in_specs += [
        pl.BlockSpec((t, cells), lambda i, a, b: (a[i], 0)),
        pl.BlockSpec((t, cells), lambda i, a, b: (b[i], 0)),
    ]
    args = [*pieces, ha, hb, va, vb]
    aliases = {}
    if acc is not None:
        aliases = {2 + len(args): 0, 3 + len(args): 1}
        args += list(acc)
        in_specs += [whole_spec((k, cells))] * 2
    return pl.pallas_call(
        functools.partial(first_body, n, acc is not None),
        out_shape=(num, num),
        grid_spec=pltpu.PrefetchScalarGridSpec(
            num_scalar_prefetch=2,
            grid=(n,),
            in_specs=in_specs,
            out_specs=[whole_spec((k, cells))] * 2,
            scratch_shapes=[pltpu.VMEM((t, k), BF16)],
        ),
        input_output_aliases=aliases,
        compiler_params=params(),
        cost_estimate=pl.CostEstimate(
            flops=8 * n * t * k * cells, bytes_accessed=n * t * cells * 6, transcendentals=0
        ),
        name="first_products",
    )(at_a, at_b, *args)


def second_body(n, code, *refs):
    _, _, *pieces = refs[: n + 2]
    ha, hb, va, vb, *rest = refs[n + 2 :]
    outs, scratch = rest[:n], rest[n]
    pick(pieces, scratch)
    w = scratch[...]
    total = 0.0
    for h, v in ((ha, va), (hb, vb)):
        low = h[...]
        total += mm(quotient(v, mm(w, low, (1, 0))), low, (1, 1))
    for k, out in enumerate(outs):
        @pl.when(pl.program_id(0) == k)
        def _():
            if code:
                encode(total, out)
            else:
                out[...] = total


def second(pieces, at_a, at_b, ha, hb, va, vb, code):
    n, (t, k) = len(pieces), pieces[0].shape
    cells = va.shape[1]
    out = coded(t, k) if code else jax.ShapeDtypeStruct((t, k), F32)
    in_specs = [whole_spec((t, k))] * n + [whole_spec((k, cells))] * 2
    in_specs += [
        pl.BlockSpec((t, cells), lambda i, a, b: (a[i], 0)),
        pl.BlockSpec((t, cells), lambda i, a, b: (b[i], 0)),
    ]
    return pl.pallas_call(
        functools.partial(second_body, n, code),
        out_shape=(out,) * n,
        grid_spec=pltpu.PrefetchScalarGridSpec(
            num_scalar_prefetch=2,
            grid=(n,),
            in_specs=in_specs,
            out_specs=[whole_spec(out.shape)] * n,
            scratch_shapes=[pltpu.VMEM((t, k), BF16)],
        ),
        compiler_params=params(),
        cost_estimate=pl.CostEstimate(
            flops=8 * n * t * k * cells, bytes_accessed=n * t * cells * 6, transcendentals=0
        ),
        name="second_products",
    )(at_a, at_b, *pieces, ha, hb, va, vb)


def plain(body, outs, *args, name):
    return pl.pallas_call(body, out_shape=outs, compiler_params=params(), name=name)(*args)


def flip(x, axis, size, bit):
    return lax.ppermute(x, axis, [(i, i ^ bit) for i in range(size)])


def add_core_and_encode(a_ref, b_ref, lo_ref, hi_ref):
    half = a_ref.shape[0] // 2
    encode(a_ref[:half, :] + b_ref[:half, :], lo_ref)
    encode(a_ref[half:, :] + b_ref[half:, :], hi_ref)


def add_and_encode(lo, lo_in, hi, hi_in, lo_ref, hi_ref):
    encode(decode(lo) + decode(lo_in), lo_ref)
    encode(decode(hi) + decode(hi_in), hi_ref)


def h1_update(lo, lo_in, hi, hi_in, h1_ref, col_ref, new_ref, low_ref):
    half = h1_ref.shape[0] // 2
    for at, one, other in ((0, lo, lo_in), (half, hi, hi_in)):
        rows = pl.ds(at, half)
        new = h1_ref[rows, :] * (decode(one) + decode(other)) / col_ref[rows, :1]
        new_ref[rows, :] = new
        low_ref[rows, :] = new.astype(BF16)


def h1_update_plain(num, h1_ref, col_ref, new_ref, low_ref):
    new = h1_ref[...] * num[...] / col_ref[:, :1]
    new_ref[...] = new
    low_ref[...] = new.astype(BF16)


def relay_add(x, x_in, y, y_in, x_ref, y_ref):
    encode(x[...] + decode(x_in), x_ref)
    encode(y[...] + decode(y_in), y_ref)


def w1_update(own0, own1, x0, x1, y0, y1, w_ref, row_ref, out_ref):
    t = own0.shape[0]
    row = row_ref[:1, :]
    for at, parts in ((0, (own0, x0, y0)), (t, (own1, x1, y1))):
        total = parts[0][...] + decode(parts[1]) + decode(parts[2])
        w = w_ref[pl.ds(at, t), :].astype(F32)
        out_ref[pl.ds(at, t), :] = (w * total / row).astype(BF16)


def layer_two(h1_new, w2, h2):
    hi = lax.Precision.HIGHEST
    ratio3 = h1_new / jnp.dot(w2, h2, precision=hi)
    h2_new = h2 * jnp.dot(w2.T, ratio3, precision=hi) / jnp.sum(w2, axis=0)[:, None]
    ratio4 = h1_new / jnp.dot(w2, h2_new, precision=hi)
    w2_part = lax.dot_general(h2_new, ratio4, (((1,), (1,)), ((), ())), precision=hi)
    return h2_new, w2_part, jnp.sum(h2_new, axis=1)


def on_device(n_gene, n_cell, counts, w1, h1, w2, h2):
    genes, cells = counts.shape
    rows, k1 = w1.shape
    k2 = w2.shape[1]
    chips = n_cell // 2
    me = lax.axis_index("cell")
    core, chip = me % 2, me // 2
    rings = n_cell == 8 and n_gene == 4
    cell = functools.partial(flip, axis="cell", size=n_cell)
    gene = functools.partial(flip, axis="gene", size=n_gene)

    col = jnp.sum(w1.astype(F32), axis=0)[None, :]
    if rings:
        col = jnp.broadcast_to(col, (8, k1))
        for bit in (1, 2, 4):
            col = col + cell(col, bit=bit)
        for bit in (1, 3):
            col = col + gene(col, bit=bit)
        col = col[0]
    else:
        col = lax.psum(col, ("gene", "cell"))[0]
    col = jnp.broadcast_to(col[:, None], (k1, 128))

    h1_low = h1.astype(BF16)
    pairs = counts.reshape(chips, 2, rows, cells)
    theirs = lax.dynamic_index_in_dim(pairs, 1 - core, axis=1, keepdims=False)
    v_other = cell(theirs.astype(jnp.int16), bit=1).reshape(chips * rows, cells)
    h1_low_other = cell(h1_low, bit=1)

    if rings:
        t = rows // 2
        w_lo, w_hi = w1[:t], w1[t:]
        x_hi, y_lo = cell(w_hi, bit=2), cell(w_lo, bit=4)
        x_lo, y_hi = cell(w_lo, bit=2), cell(w_hi, bit=4)
        d_lo, d_hi = cell(y_lo, bit=2), cell(x_hi, bit=4)

        def places(*which):
            chip_at = jnp.stack([chip ^ d for d, _ in which])
            half = jnp.array([h for _, h in which], jnp.int32)
            return (chip_at * 2 + core) * 2 + half, chip_at * 2 + half

        own, near = places((0, 0), (0, 1)), places((1, 0), (1, 1), (2, 0), (2, 1))
        far = places((3, 0), (3, 1))
        data = (h1_low, h1_low_other, counts, v_other)
        acc = first((w_lo, w_hi), *own, *data)
        acc = first((x_lo, x_hi, y_lo, y_hi), *near, *data, acc)
        num, num_other = first((d_lo, d_hi), *far, *data, acc)
        num_in = cell(num_other, bit=1)
        half = coded(k1 // 2, cells)
        lo, hi = plain(add_core_and_encode, (half, half), num, num_in, name="encode_h1_num")
        lo_in, hi_in = gene(lo, bit=1), gene(hi, bit=3)
        lo, hi = plain(add_and_encode, (half, half), lo, lo_in, hi, hi_in, name="add_h1_num")
        lo_in, hi_in = gene(lo, bit=3), gene(hi, bit=1)
        h1_new, h1_low2 = plain(
            h1_update,
            (jax.ShapeDtypeStruct((k1, cells), F32), jax.ShapeDtypeStruct((k1, cells), BF16)),
            lo, lo_in, hi, hi_in, h1, col, name="h1_update",
        )
        h1_low2_other = cell(h1_low2, bit=1)

        data = (h1_low2, h1_low2_other, counts, v_other)
        d_lo, d_hi = second((d_lo, d_hi), *far, *data, True)
        y_in, x_in = cell(d_lo, bit=2), cell(d_hi, bit=4)
        x_lo2, y_hi2 = second((x_lo, y_hi), *places((1, 0), (2, 1)), *data, True)
        x_lo_in, y_hi_in = cell(x_lo2, bit=2), cell(y_hi2, bit=4)
        x_hi2, y_lo2 = second((x_hi, y_lo), *places((1, 1), (2, 0)), *data, False)
        piece = coded(t, k1)
        x_hi2, y_lo2 = plain(relay_add, (piece, piece), x_hi2, x_in, y_lo2, y_in, name="relay_add")
        x_hi_in, y_lo_in = cell(x_hi2, bit=2), cell(y_lo2, bit=4)
        own0, own1 = second((w_lo, w_hi), *own, *data, False)
    else:
        groups = [list(range(c, n_cell, 2)) for c in (0, 1)]
        w_all = lax.all_gather(w1, "cell", axis=0, tiled=True, axis_index_groups=groups)
        pieces = [w_all[i * rows : (i + 1) * rows] for i in range(chips)]
        at = jnp.arange(chips, dtype=jnp.int32)
        at = (at * 2 + core, at)
        num, num_other = first(pieces, *at, h1_low, h1_low_other, counts, v_other)
        num = lax.psum(num + cell(num_other, bit=1), "gene")
        h1_new, h1_low2 = plain(
            h1_update_plain,
            (jax.ShapeDtypeStruct((k1, cells), F32), jax.ShapeDtypeStruct((k1, cells), BF16)),
            num, h1, col, name="h1_update",
        )
        h1_low2_other = cell(h1_low2, bit=1)
        parts = second(pieces, *at, h1_low2, h1_low2_other, counts, v_other, False)
        w1_num = lax.psum_scatter(
            jnp.concatenate(parts), "cell", scatter_dimension=0, tiled=True, axis_index_groups=groups
        )

    h2_new, w2_part, h2_part = layer_two(h1_new, w2, h2)
    small = jnp.concatenate(
        [w2_part, jnp.sum(h1_new, axis=1)[None, :], jnp.pad(h2_part, (0, k1 - k2))[None, :], jnp.zeros((6, k1), F32)]
    )
    if rings:
        for bit in (1, 2, 4):
            small = small + cell(small, bit=bit)
    else:
        small = lax.psum(small, "cell")
    w2_num, rowsum, h2_rows = small[:k2], small[k2 : k2 + 1], small[k2 + 1, :k2]
    w2_new = w2 * w2_num.T / h2_rows[None, :]
    if rings:
        w1_new = plain(
            w1_update, jax.ShapeDtypeStruct((rows, k1), BF16),
            own0, own1, x_lo_in, x_hi_in, y_lo_in, y_hi_in, w1, rowsum, name="w1_update",
        )
    else:
        w1_new = (w1.astype(F32) * w1_num / rowsum).astype(BF16)
    return (w1_new, h1_new, w2_new, h2_new)


def solution(mesh):
    placed = (P("gene", "cell"), P(("gene", "cell"), None), P(None, "cell"), P(), P(None, "cell"))
    return jax.shard_map(
        functools.partial(on_device, mesh.shape["gene"], mesh.shape["cell"]),
        mesh=mesh,
        in_specs=placed,
        out_specs=(P(("gene", "cell"), None), P(None, "cell"), P(), P(None, "cell")),
        check_vma=False,
    )
```

```python
import functools

import jax
import jax.numpy as jnp
from jax import lax
from jax.experimental import pallas as pl
from jax.experimental.pallas import tpu as pltpu
from jax.sharding import PartitionSpec as P

F32 = jnp.float32
BF16 = jnp.bfloat16
PAD = 16
CHUNKS = 2


def params(mib=16):
    return pltpu.CompilerParams(vmem_limit_bytes=mib * 1024 * 1024)


def mm(a, b, dims):
    return lax.dot_general(a, b, ((dims[:1], dims[1:]), ((), ())), preferred_element_type=F32)


def encode(x, out_ref, extra=None):
    rows, cols = x.shape
    top = jnp.maximum(jnp.max(x, axis=0, keepdims=True), 1e-30)
    power = jnp.ceil(jnp.log2(top))
    q = jnp.minimum(x * (jnp.exp2(-power) * 65535.0) + 0.5, 65535.0)
    out_ref[:rows, :] = (q.astype(jnp.int32) - 32768).astype(jnp.int16)
    lines = [power]
    if extra is not None:
        whole = jnp.floor(extra)
        for y in (whole, jnp.floor((extra - whole) * 32768.0 + 0.25)):
            lines += [y[:, i : i + cols] for i in range(0, y.shape[1], cols)]
    lines.append(jnp.zeros((PAD - len(lines), cols), F32))
    out_ref[rows:, :] = jnp.concatenate(lines, axis=0).astype(jnp.int32).astype(jnp.int16)


def decode_extra(ref, width):
    rows, cols = ref.shape[0] - PAD, ref.shape[1]
    n = width // cols
    lines = ref[rows:, :].astype(jnp.int32).astype(F32)
    lines = [lines[1 + i : 2 + i] for i in range(2 * n)]
    return jnp.concatenate(lines[:n], axis=1) + jnp.concatenate(lines[n:], axis=1) * (1.0 / 32768.0)


def decode(ref):
    rows = ref.shape[0] - PAD
    power = ref[rows:, :].astype(jnp.int32).astype(F32)[:1]
    unit = jnp.exp2(power) * (1.0 / 65535.0)
    return (ref[:rows, :].astype(jnp.int32) + 32768).astype(F32) * unit


def coded(rows, cols):
    return jax.ShapeDtypeStruct((rows + PAD, cols), jnp.int16)


def quotient(v, approx):
    return (v.astype(jnp.int32).astype(F32) / approx).astype(BF16)


def counts_body(chips, rows, at, v, *refs):
    outs, held, low, sems = refs[: 2 * chips], *refs[2 * chips :]
    copies = []
    for q in range(chips):
        start = pl.multiple_of((at[0] ^ q) * 2 * rows, 2 * rows)
        both = pl.ds(q * 2 * rows, 2 * rows)
        copies.append(pltpu.make_async_copy(v.at[pl.ds(start, 2 * rows), :], held.at[both, :], sems.at[q]))
        copies[-1].start()
    for q in range(chips):
        copies[q].wait()
        for slot, core in ((q, at[1]), (chips + q, 1 - at[1])):
            some = held[pl.ds(pl.multiple_of((2 * q + core) * rows, rows), rows), :]
            low[slot] = some.astype(jnp.int16)
            copies.append(pltpu.make_async_copy(low.at[slot], outs[slot], sems.at[chips + slot]))
            copies[-1].start()
    for copy in copies[chips:]:
        copy.wait()


def split_counts(at, counts, chips, rows):
    cells = counts.shape[1]
    out = pltpu.HBM((rows, cells), jnp.int16)
    smem, hbm = pl.BlockSpec(memory_space=pltpu.SMEM), pl.BlockSpec(memory_space=pltpu.HBM)
    outs = pl.pallas_call(
        functools.partial(counts_body, chips, rows),
        out_shape=(out,) * (2 * chips),
        in_specs=[smem, hbm],
        out_specs=[hbm] * (2 * chips),
        scratch_shapes=[
            pltpu.VMEM(counts.shape, counts.dtype),
            pltpu.VMEM((2 * chips, rows, cells), jnp.int16),
            pltpu.SemaphoreType.DMA((3 * chips,)),
        ],
        compiler_params=params(),
        name="split_counts",
    )(at, pltpu.with_memory_space_constraint(counts, pltpu.HBM))
    return outs[:chips], outs[chips:]


class Later:
    def __init__(self, array):
        self.array = array


def fetching(refs, later, scratch):
    sems, slots, found = scratch[-1] if later else None, iter(scratch), []
    for i, ref in enumerate(refs):
        copy = None
        if i in later:
            slot = next(slots)
            copy = pltpu.make_async_copy(ref, slot, sems.at[later.index(i)])
            copy.start()
            ref = slot
        found.append((ref, copy))
    return found


def ready(operand):
    ref, copy = operand
    if copy is not None:
        copy.wait()
    return ref[...]


def joined(operands):
    return jnp.concatenate([ready(x) for x in operands], axis=0) if len(operands) > 1 else ready(operands[0])


def ahead(sources, outs, sems):
    copies = [pltpu.make_async_copy(x, out, sems.at[i]) for i, (x, out) in enumerate(zip(sources, outs))]
    for copy in copies:
        copy.start()
    return copies


def fetch_body(n, *refs):
    for copy in ahead(refs[:n], refs[n : 2 * n], refs[-1]):
        copy.wait()


def plain_fetch(arrays):
    n = len(arrays)
    vmem, hbm = pl.BlockSpec(memory_space=pltpu.VMEM), pl.BlockSpec(memory_space=pltpu.HBM)
    return pl.pallas_call(
        functools.partial(fetch_body, n),
        out_shape=[jax.ShapeDtypeStruct(x.shape, x.dtype) for x in arrays],
        in_specs=[hbm] * n,
        out_specs=[vmem] * n,
        scratch_shapes=[pltpu.SemaphoreType.DMA((n,))],
        compiler_params=params(),
        name="fetch",
    )(*(pltpu.with_memory_space_constraint(x, pltpu.HBM) for x in arrays))


def first_body(groups, later, n_ahead, has_acc, h, *refs):
    n, n_later = sum(groups) + len(groups), len(later)
    refs, sems = (refs[:-1], refs[-1:]) if n_ahead else (refs, ())
    refs, scratch = (refs[:-n_later - 1] + sems, refs[-n_later - 1 :]) if later else (refs + sems, ())
    operands = fetching(refs[:n], later, scratch)
    copies, refs = (), refs[n:]
    if n_ahead:
        copies, refs = ahead(refs[:n_ahead], refs[-1 - n_ahead : -1], refs[-1]), refs[n_ahead : -1 - n_ahead]
    num_ref, col_ref = refs[-2:]
    total, col = (refs[0][...], refs[1][...]) if has_acc else (0.0, 0.0)
    for n in groups:
        w, v = joined(operands[:n]), operands[n]
        operands = operands[n + 1 :]
        approx = mm(w, h[...], (1, 0))
        total += mm(w, quotient(ready(v), approx), (0, 0))
        col += jnp.sum(w.astype(F32), axis=0, keepdims=True)
    num_ref[...] = total
    col_ref[...] = jnp.broadcast_to(col, col_ref.shape)
    for copy in copies:
        copy.wait()


def second_body(groups, later, n_ahead, code, ha, hb, *refs):
    n, n_later = sum(groups) + 2 * len(groups), len(later)
    refs, scratch = (refs[:-n_later - 1], refs[-n_later - 1 :]) if later else (refs, ())
    operands, outs = fetching(refs[:n], later, scratch), refs[n:]
    for n in groups:
        pieces, v, operands = operands[:n], operands[n : n + 2], operands[n + 2 :]
        w, t = joined(pieces), pieces[0][0].shape[0]
        total = 0.0
        for h, some in ((hb, v[1]), (ha, v[0])):
            low = h[...]
            approx = mm(w, low, (1, 0))
            total += mm(quotient(ready(some), approx), low, (1, 1))
        for k in range(n):
            out, outs = outs[0], outs[1:]
            part = total[k * t : (k + 1) * t]
            if code:
                encode(part, out)
            else:
                out[...] = part


def products(body, flag, outs, groups, h, acc, name, fetch=()):
    n_h = len(h)
    sizes = tuple(len(g) - n_h for g in groups)
    flat = [x for g in groups for x in g]
    later = tuple(i for i, x in enumerate(flat) if isinstance(x, Later))
    vmem, hbm = pl.BlockSpec(memory_space=pltpu.VMEM), pl.BlockSpec(memory_space=pltpu.HBM)
    specs = [hbm if i in later else vmem for i in range(len(flat))]
    flat = [pltpu.with_memory_space_constraint(x.array, pltpu.HBM) if isinstance(x, Later) else x for x in flat]
    scratch = [pltpu.VMEM(flat[i].shape, flat[i].dtype) for i in later]
    if later:
        scratch.append(pltpu.SemaphoreType.DMA((len(later),)))
    fetch = [pltpu.with_memory_space_constraint(x, pltpu.HBM) for x in fetch]
    if fetch:
        scratch.append(pltpu.SemaphoreType.DMA((len(fetch),)))
    outs = (*outs, *(jax.ShapeDtypeStruct(x.shape, x.dtype) for x in fetch))
    args = [*h, *flat, *fetch, *acc]
    work = 2 * sum(x.shape[0] for x in flat) * h[0].shape[1]
    return pl.pallas_call(
        functools.partial(body, sizes, later, len(fetch), flag),
        out_shape=outs,
        in_specs=[vmem] * n_h + specs + [hbm] * len(fetch) + [vmem] * len(acc),
        out_specs=[vmem] * len(outs),
        scratch_shapes=scratch,
        input_output_aliases={len(args) - len(acc) + i: i for i in range(len(acc))},
        compiler_params=params(),
        cost_estimate=pl.CostEstimate(flops=2 * work * h[0].shape[0], bytes_accessed=work, transcendentals=0),
        name=name,
    )(*args)


def first(groups, h, acc=(), fetch=()):
    k1, cells = h.shape
    outs = (jax.ShapeDtypeStruct((k1, cells), F32), jax.ShapeDtypeStruct((8, k1), F32))
    return products(first_body, bool(acc), outs, groups, (h,), acc, "first_products", fetch)


def second(groups, t, h, code):
    k1 = h[0].shape[0]
    out = coded(t, k1) if code else jax.ShapeDtypeStruct((t, k1), F32)
    outs = (out,) * sum(len(g) - 2 for g in groups)
    return products(second_body, code, outs, groups, h, (), "second_products")


def plain(body, outs, *args, name, flag=None):
    vmem = pl.BlockSpec(memory_space=pltpu.VMEM)
    specs = [vmem] * len(args)
    if flag is not None:
        specs, args = [pl.BlockSpec(memory_space=pltpu.SMEM)] + specs, (flag, *args)
    out_specs = (vmem,) * len(outs) if isinstance(outs, tuple) else vmem
    return pl.pallas_call(
        body, out_shape=outs, in_specs=specs, out_specs=out_specs, compiler_params=params(), name=name
    )(*args)


def flip(x, axis, size, bit):
    return lax.ppermute(x, axis, [(i, i ^ bit) for i in range(size)])


def split_num(flag, num, col, keep_ref, *sends):
    inner = flag[0] == 1
    half = num.shape[1] // 2
    keep_ref[...] = jnp.where(inner, num[:, half:], num[:, :half])
    width = half // len(sends)
    for i, send in enumerate(sends):
        lo = num[:, i * width : (i + 1) * width]
        hi = num[:, half + i * width : half + (i + 1) * width]
        encode(jnp.where(inner, lo, hi), send, None if i else col[:1, :])


def add_kept(i, keep, other, *refs):
    width, k1 = other.shape[1], keep.shape[0]
    extra = None if i else decode_extra(refs[0], k1) + decode_extra(other, k1)
    encode(keep[:, i * width : (i + 1) * width] + decode(other), refs[-1], extra)


def add_coded(one, other, out_ref, *col_ref):
    encode(decode(one) + decode(other), out_ref)
    for ref in col_ref:
        k1 = ref.shape[1]
        ref[...] = jnp.broadcast_to(decode_extra(one, k1) + decode_extra(other, k1), ref.shape)


def h1_update(n, flag, *refs):
    mine, theirs, (h1_ref, col_ref, new_ref, low_ref, late_ref) = refs[:n], refs[n : 2 * n], refs[2 * n :]
    inner = flag[0] == 1
    half = h1_ref.shape[1] // 2
    width = half // n
    col = col_ref[...].T[:, :1]
    for i in range(n):
        a, b = decode(mine[i]), decode(theirs[i])
        for at, num in ((i * width, jnp.where(inner, b, a)), (half + i * width, jnp.where(inner, a, b))):
            new = h1_ref[:, at : at + width] * num / col
            new_ref[:, at : at + width] = new
            late_ref[:, at : at + width] = new
            low_ref[:, at : at + width] = new.astype(BF16)


def h1_update_plain(num, h1_ref, col_ref, new_ref, low_ref):
    new = h1_ref[...] * num[...] / col_ref[:, :1]
    new_ref[...] = new
    low_ref[...] = new.astype(BF16)


def relay_add(x, x_in, y, y_in, x_ref, y_ref):
    half = x.shape[0] // 2
    encode(jnp.concatenate([x[:half, :], x[half:, :] + decode(x_in)], axis=0), x_ref)
    encode(jnp.concatenate([y[:half, :] + decode(y_in), y[half:, :]], axis=0), y_ref)


def half_sum(core, a_ref, b_ref, out_ref):
    half = out_ref.shape[0]
    total = a_ref[...] + b_ref[...]
    out_ref[...] = jnp.where(core[0] == 0, total[:half], total[half:])


def add_two(a_ref, b_ref, out_ref):
    out_ref[...] = a_ref[...] + b_ref[...]


def w1_update(own, x, y, w_ref, row_ref, out_ref):
    total = own[...] + decode(x) + decode(y)
    out_ref[...] = (w_ref[...].astype(F32) * total / row_ref[:1, :]).astype(BF16)


def parts(x):
    hi = x.astype(BF16)
    return hi, (x - hi.astype(F32)).astype(BF16)


def mm3(a, b, dims):
    (ah, al), (bh, bl) = a, b
    return mm(ah, bh, dims) + (mm(ah, bl, dims) + mm(al, bh, dims))


def layer_two(h1_ref, w2t_ref, h2_ref, v, new_ref, sums_ref, v_out, sem):
    copy = pltpu.make_async_copy(v, v_out, sem)
    copy.start()
    h1, w2t, h2 = h1_ref[...], w2t_ref[...], h2_ref[...]
    k2, k1 = w2t.shape
    w2p = parts(w2t)
    ratio3 = h1 / mm3(w2p, parts(h2), (0, 0))
    h2_new = h2 * mm3(w2p, parts(ratio3), (1, 0)) / jnp.sum(w2t, axis=1, keepdims=True)
    new_ref[...] = h2_new
    h2p = parts(h2_new)
    ratio4 = h1 / mm3(w2p, h2p, (0, 0))
    sums_ref[:k2, :] = mm3(h2p, parts(ratio4), (1, 1))
    cells = h1.shape[1]
    row = (jnp.ones((8, cells), BF16), jnp.zeros((8, cells), BF16))
    sums_ref[k2 : k2 + 8, :] = mm3(row, parts(h1), (1, 1))
    sums_ref[k2 + 8 :, :] = jnp.zeros((8, k1), F32)
    sums_ref[k2 + 8 :, :k2] = mm3(row, h2p, (1, 1))
    copy.wait()


def on_device(n_gene, n_cell, counts, w1, h1, w2, h2):
    genes, cells = counts.shape
    rows, k1 = w1.shape
    k2 = w2.shape[1]
    chips = n_cell // 2
    me = lax.axis_index("cell")
    core, chip = me % 2, me // 2
    line = n_cell == 8 and n_gene == 4 and genes * 4 < 32768
    cell = functools.partial(flip, axis="cell", size=n_cell)
    gene = functools.partial(flip, axis="gene", size=n_gene)
    after = lax.optimization_barrier
    at = jnp.stack([chip, core]).astype(jnp.int32)

    h1_low = h1.astype(BF16)
    new_shapes = (jax.ShapeDtypeStruct((k1, cells), F32), jax.ShapeDtypeStruct((k1, cells), BF16))
    if line:
        t = rows // 2
        w_x, w_y = cell(w1, bit=2), cell(w1, bit=4)
        w_0 = cell(w1, bit=1)

        v_mine, v_theirs = split_counts(at, counts, chips, rows)
        v_other = [cell(v, bit=1) for v in v_theirs]
        on_mine, on_theirs = ([Later(v) for v in some] for some in (v_mine, v_theirs))
        acc = first(((Later(w1), on_mine[0]), (w_0, on_theirs[0])), h1_low)
        w_x, w_y, *acc = after((w_x, w_y, *acc))
        d_lo, d_hi = cell(w_y[:t], bit=2), cell(w_x[t:], bit=4)
        x_0, y_0 = cell(w_x, bit=1), cell(w_y, bit=1)
        near = ((Later(w_x), on_mine[1]), (Later(w_y), on_mine[2]), (x_0, on_theirs[1]), (y_0, on_theirs[2]))
        acc = first(near, h1_low, acc)
        d_lo, d_hi, *acc = after((d_lo, d_hi, *acc))
        v_far = after((v_mine[3], v_theirs[3], *acc))[:2]
        v_far = plain_fetch(v_far)
        far = cell(d_lo, bit=1), cell(d_hi, bit=1)
        acc = first(((d_lo, d_hi, v_far[0]),), h1_low, acc)
        num, col = first(((*far, v_far[1]),), h1_low, acc)

        z = lax.axis_index("gene")
        inner = jnp.where((z == 1) | (z == 2), 1, 0).astype(jnp.int32)[None]
        chunks = tuple(range(CHUNKS))
        piece = coded(k1, cells // 2 // CHUNKS)
        keep, *sent = plain(
            split_num, (jax.ShapeDtypeStruct((k1, cells // 2), F32),) + (piece,) * CHUNKS,
            num, col, flag=inner, name="split_num",
        )

        pair = []
        for i, x in enumerate(sent):
            got = gene(after((x, *pair))[0], bit=1)
            extra = () if i else (x,)
            pair.append(plain(functools.partial(add_kept, i), piece, keep, got, *extra, name="add_pair"))
        mine = []
        for i, x in enumerate(pair):
            outs = piece if i else (piece, jax.ShapeDtypeStruct((8, k1), F32))
            mine.append(plain(add_coded, outs, x, gene(x, bit=3), name="add_cross"))
        (first_mine, col), *mine = mine
        mine = [first_mine, *mine]
        theirs = [gene(x, bit=1) for x in mine]
        h1_new, h1_low2, h1_late = plain(
            functools.partial(h1_update, CHUNKS), new_shapes + new_shapes[:1], *mine, *theirs, h1, col,
            flag=inner, name="h1_update",
        )
        h1_low2_other = cell(h1_low2, bit=1)
    else:
        col = None
        groups = [list(range(c, n_cell, 2)) for c in (0, 1)]
        w_half = lax.all_gather(w1, "cell", axis=0, tiled=True, axis_index_groups=groups)
        v_mine, v_theirs = split_counts(at * jnp.array([0, 1], jnp.int32), counts, chips, rows)
        v_other = [cell(v, bit=1) for v in v_theirs]
        halves = [[w[j * rows : (j + 1) * rows] for j in range(chips)] for w in (w_half, cell(w_half, bit=1))]
        each = min(chips, max(1, 512 // rows))
        acc = ()
        for i in range(0, chips, each):
            for w, v in zip(halves, (v_mine, v_theirs)):
                acc = first(tuple((w[j], v[j]) for j in range(i, i + each)), h1_low, acc)
        num, col = lax.psum(tuple(acc), "gene")
        col = jnp.broadcast_to(col[0][:, None], (k1, 128))
        h1_new, h1_low2 = plain(h1_update_plain, new_shapes, num, h1, col, name="h1_update")
        h1_low2_other, h1_late = cell(h1_low2, bit=1), h1_new

    w2t = w2.T
    vmem, hbm = pl.BlockSpec(memory_space=pltpu.VMEM), pl.BlockSpec(memory_space=pltpu.HBM)
    h2_new, sums, v_far = pl.pallas_call(
        layer_two,
        out_shape=(
            jax.ShapeDtypeStruct((k2, cells), F32),
            jax.ShapeDtypeStruct((k2 + 16, k1), F32),
            jax.ShapeDtypeStruct(v_mine[-1].shape, jnp.int16),
        ),
        in_specs=[vmem] * 3 + [hbm],
        out_specs=[vmem] * 3,
        scratch_shapes=[pltpu.SemaphoreType.DMA(())],
        compiler_params=params(),
        name="layer_two",
    )(h1_late, w2t, h2, pltpu.with_memory_space_constraint(v_mine[-1], pltpu.HBM))
    low2 = (h1_low2, h1_low2_other)
    if line:
        sums_in = cell(sums, bit=1)
        d_lo, d_hi = second(((d_lo, d_hi, v_far, v_other[3]),), t, low2, True)
        half = jax.ShapeDtypeStruct(((k2 + 16) // 2, k1), F32)
        sums, sums_in, d_lo = after((sums, sums_in, d_lo))
        part = plain(half_sum, half, sums, sums_in, flag=core.astype(jnp.int32)[None], name="half_sum")
        part, d_lo, d_hi = after((part, d_lo, d_hi))
        part_in = cell(part, bit=2)
        y_in, x_in = cell(d_lo, bit=2), cell(d_hi, bit=4)
        part = plain(add_two, half, part, part_in, name="add_two")
        w_x, part = after((w_x, part))
        part_in = cell(part, bit=4)
        near = ((Later(w_x), on_mine[1], v_other[1]), (Later(w_y), on_mine[2], v_other[2]))
        x_num, y_num = second(near, rows, low2, False)
        part, x_num = after((part, x_num))
        w1_late, part = after((w1, part))
        (own,) = second(((Later(w1_late), on_mine[0], v_other[0]),), rows, low2, False)
        piece = coded(rows, k1)
        x_num, part_in, own = after((x_num, part_in, own))
        x_num, y_num = plain(relay_add, (piece, piece), x_num, x_in, y_num, y_in, name="relay_add")
        x_num_in, y_num_in = cell(x_num, bit=2), cell(y_num, bit=4)
        part = plain(add_two, half, part, part_in, name="add_two")
        rest = cell(part, bit=1)
        sums = jnp.where(core == 0, jnp.concatenate([part, rest]), jnp.concatenate([rest, part]))
    else:
        found = []
        for i in range(0, chips, each):
            some = tuple((halves[0][j], v_mine[j], v_other[j]) for j in range(i, i + each))
            found += second(some, rows, low2, False)
        w1_num = lax.psum_scatter(
            jnp.concatenate(found), "cell", scatter_dimension=0, tiled=True, axis_index_groups=groups
        )
        sums = lax.psum(sums, "cell")
    w2_num, rowsum, h2_rows = sums[:k2], sums[k2 : k2 + 8], sums[k2 + 8, :k2]
    w2_new = (w2t * w2_num / h2_rows[:, None]).T
    if line:
        w1_new = plain(
            w1_update, jax.ShapeDtypeStruct((rows, k1), BF16), own, x_num_in, y_num_in, w1, rowsum, name="w1_update"
        )
    else:
        w1_new = (w1.astype(F32) * w1_num / rowsum[:1]).astype(BF16)
    return (w1_new, h1_new, w2_new, h2_new)


def solution(mesh):
    placed = (P("gene", "cell"), P(("gene", "cell"), None), P(None, "cell"), P(), P(None, "cell"))
    return jax.shard_map(
        functools.partial(on_device, mesh.shape["gene"], mesh.shape["cell"]),
        mesh=mesh,
        in_specs=placed,
        out_specs=(P(("gene", "cell"), None), P(None, "cell"), P(), P(None, "cell")),
        check_vma=False,
    )
```

```python
import functools

import jax
import jax.numpy as jnp
from jax import lax
from jax.experimental import pallas as pl
from jax.experimental.pallas import tpu as pltpu
from jax.sharding import PartitionSpec as P

F32 = jnp.float32
BF16 = jnp.bfloat16
PAD = 16
CHUNKS = 2


def params(mib=16):
    return pltpu.CompilerParams(vmem_limit_bytes=mib * 1024 * 1024)


def mm(a, b, dims):
    return lax.dot_general(a, b, ((dims[:1], dims[1:]), ((), ())), preferred_element_type=F32)


def power_of(x):
    return jnp.ceil(jnp.log2(jnp.maximum(x, 1e-30)))


def encode(x, out_ref, extra=None, singles=(), at=0):
    rows, cols = x.shape
    power = power_of(jnp.max(x, axis=0, keepdims=True))
    q = jnp.minimum(x * (jnp.exp2(-power) * 65535.0) + 0.5, 65535.0)
    out_ref[at : at + rows, :] = (q.astype(jnp.int32) - 32768).astype(jnp.int16)
    lines = [power]
    if extra is not None:
        whole = jnp.floor(extra)
        for y in (whole, jnp.floor((extra - whole) * 32768.0 + 0.25)):
            lines += [y[:, i : i + cols] for i in range(0, y.shape[1], cols)]
    for y in singles:
        own = power_of(y)
        y = y * (jnp.exp2(-own) * 32767.0)
        whole = jnp.floor(y)
        lines += [own, whole, jnp.floor((y - whole) * 32768.0)]
    lines.append(jnp.zeros((PAD - len(lines), cols), F32))
    out_ref[at + rows : at + rows + PAD, :] = jnp.concatenate(lines, axis=0).astype(jnp.int32).astype(jnp.int16)


def pad_rows(ref, end):
    return ref[end - PAD : end, :].astype(jnp.int32).astype(F32)


def decode_extra(ref, width):
    n = width // ref.shape[1]
    lines = pad_rows(ref, ref.shape[0])
    lines = [lines[1 + i : 2 + i] for i in range(2 * n)]
    return jnp.concatenate(lines[:n], axis=1) + jnp.concatenate(lines[n:], axis=1) * (1.0 / 32768.0)


def decode_singles(ref, n, end):
    lines = pad_rows(ref, end)
    found = []
    for i in range(1, 1 + 3 * n, 3):
        unit = jnp.exp2(lines[i : i + 1]) * (1.0 / 32767.0)
        found.append((lines[i + 1 : i + 2] + lines[i + 2 : i + 3] * (1.0 / 32768.0)) * unit)
    return found


def decode(ref, rows=None, at=0):
    rows = ref.shape[0] - PAD if rows is None else rows
    unit = jnp.exp2(pad_rows(ref, at + rows + PAD)[:1]) * (1.0 / 65535.0)
    return (ref[at : at + rows, :].astype(jnp.int32) + 32768).astype(F32) * unit


def coded(rows, cols):
    return jax.ShapeDtypeStruct((rows + PAD, cols), jnp.int16)


def quotient(v, approx):
    return (v.astype(jnp.int32).astype(F32) / approx).astype(BF16)


def counts_body(chips, rows, at, v, *refs):
    outs, held, low, sems = refs[: 2 * chips], *refs[2 * chips :]
    copies = []
    for q in range(chips):
        start = pl.multiple_of((at[0] ^ q) * 2 * rows, 2 * rows)
        both = pl.ds(q * 2 * rows, 2 * rows)
        copies.append(pltpu.make_async_copy(v.at[pl.ds(start, 2 * rows), :], held.at[both, :], sems.at[q]))
        copies[-1].start()
    for q in range(chips):
        copies[q].wait()
        for slot, core in ((q, at[1]), (chips + q, 1 - at[1])):
            some = held[pl.ds(pl.multiple_of((2 * q + core) * rows, rows), rows), :]
            low[slot] = some.astype(jnp.int16)
            copies.append(pltpu.make_async_copy(low.at[slot], outs[slot], sems.at[chips + slot]))
            copies[-1].start()
    for copy in copies[chips:]:
        copy.wait()


def split_counts(at, counts, chips, rows):
    cells = counts.shape[1]
    out = pltpu.HBM((rows, cells), jnp.int16)
    smem, hbm = pl.BlockSpec(memory_space=pltpu.SMEM), pl.BlockSpec(memory_space=pltpu.HBM)
    outs = pl.pallas_call(
        functools.partial(counts_body, chips, rows),
        out_shape=(out,) * (2 * chips),
        in_specs=[smem, hbm],
        out_specs=[hbm] * (2 * chips),
        scratch_shapes=[
            pltpu.VMEM(counts.shape, counts.dtype),
            pltpu.VMEM((2 * chips, rows, cells), jnp.int16),
            pltpu.SemaphoreType.DMA((3 * chips,)),
        ],
        compiler_params=params(),
        name="split_counts",
    )(at, pltpu.with_memory_space_constraint(counts, pltpu.HBM))
    return outs[:chips], outs[chips:]


class Later:
    def __init__(self, array):
        self.array = array


def fetching(refs, later, scratch):
    sems, slots, found = scratch[-1] if later else None, iter(scratch), []
    for i, ref in enumerate(refs):
        copy = None
        if i in later:
            slot = next(slots)
            copy = pltpu.make_async_copy(ref, slot, sems.at[later.index(i)])
            copy.start()
            ref = slot
        found.append((ref, copy))
    return found


def ready(operand):
    ref, copy = operand
    if copy is not None:
        copy.wait()
    return ref[...]


def joined(operands):
    return jnp.concatenate([ready(x) for x in operands], axis=0) if len(operands) > 1 else ready(operands[0])


def ahead(sources, outs, sems):
    copies = [pltpu.make_async_copy(x, out, sems.at[i]) for i, (x, out) in enumerate(zip(sources, outs))]
    for copy in copies:
        copy.start()
    return copies


def fetch_body(n, *refs):
    for copy in ahead(refs[:n], refs[n : 2 * n], refs[-1]):
        copy.wait()


def plain_fetch(arrays):
    n = len(arrays)
    vmem, hbm = pl.BlockSpec(memory_space=pltpu.VMEM), pl.BlockSpec(memory_space=pltpu.HBM)
    return pl.pallas_call(
        functools.partial(fetch_body, n),
        out_shape=[jax.ShapeDtypeStruct(x.shape, x.dtype) for x in arrays],
        in_specs=[hbm] * n,
        out_specs=[vmem] * n,
        scratch_shapes=[pltpu.SemaphoreType.DMA((n,))],
        compiler_params=params(),
        name="fetch",
    )(*(pltpu.with_memory_space_constraint(x, pltpu.HBM) for x in arrays))


def first_body(groups, later, n_ahead, has_acc, h, *refs):
    n, n_later = sum(groups) + len(groups), len(later)
    refs, sems = (refs[:-1], refs[-1:]) if n_ahead else (refs, ())
    refs, scratch = (refs[:-n_later - 1] + sems, refs[-n_later - 1 :]) if later else (refs + sems, ())
    operands = fetching(refs[:n], later, scratch)
    copies, refs = (), refs[n:]
    if n_ahead:
        copies, refs = ahead(refs[:n_ahead], refs[-1 - n_ahead : -1], refs[-1]), refs[n_ahead : -1 - n_ahead]
    num_ref, col_ref = refs[-2:]
    total, col = (refs[0][...], refs[1][...]) if has_acc else (0.0, 0.0)
    for n in groups:
        w, v = joined(operands[:n]), operands[n]
        operands = operands[n + 1 :]
        approx = mm(w, h[...], (1, 0))
        total += mm(w, quotient(ready(v), approx), (0, 0))
        col += jnp.sum(w.astype(F32), axis=0, keepdims=True)
    num_ref[...] = total
    col_ref[...] = jnp.broadcast_to(col, col_ref.shape)
    for copy in copies:
        copy.wait()


def second_body(groups, later, n_ahead, code, ha, hb, *refs):
    n, n_later = sum(groups) + 2 * len(groups), len(later)
    refs, scratch = (refs[:-n_later - 1], refs[-n_later - 1 :]) if later else (refs, ())
    operands, outs = fetching(refs[:n], later, scratch), refs[n:]
    for n in groups:
        pieces, v, operands = operands[:n], operands[n : n + 2], operands[n + 2 :]
        w, t = joined(pieces), pieces[0][0].shape[0]
        total = 0.0
        for h, some in ((hb, v[1]), (ha, v[0])):
            low = h[...]
            approx = mm(w, low, (1, 0))
            total += mm(quotient(ready(some), approx), low, (1, 1))
        for k in range(n):
            out, outs = outs[0], outs[1:]
            part = total[k * t : (k + 1) * t]
            if code:
                encode(part, out)
            else:
                out[...] = part


def products(body, flag, outs, groups, h, acc, name, fetch=()):
    n_h = len(h)
    sizes = tuple(len(g) - n_h for g in groups)
    flat = [x for g in groups for x in g]
    later = tuple(i for i, x in enumerate(flat) if isinstance(x, Later))
    vmem, hbm = pl.BlockSpec(memory_space=pltpu.VMEM), pl.BlockSpec(memory_space=pltpu.HBM)
    specs = [hbm if i in later else vmem for i in range(len(flat))]
    flat = [pltpu.with_memory_space_constraint(x.array, pltpu.HBM) if isinstance(x, Later) else x for x in flat]
    scratch = [pltpu.VMEM(flat[i].shape, flat[i].dtype) for i in later]
    if later:
        scratch.append(pltpu.SemaphoreType.DMA((len(later),)))
    fetch = [pltpu.with_memory_space_constraint(x, pltpu.HBM) for x in fetch]
    if fetch:
        scratch.append(pltpu.SemaphoreType.DMA((len(fetch),)))
    outs = (*outs, *(jax.ShapeDtypeStruct(x.shape, x.dtype) for x in fetch))
    args = [*h, *flat, *fetch, *acc]
    work = 2 * sum(x.shape[0] for x in flat) * h[0].shape[1]
    return pl.pallas_call(
        functools.partial(body, sizes, later, len(fetch), flag),
        out_shape=outs,
        in_specs=[vmem] * n_h + specs + [hbm] * len(fetch) + [vmem] * len(acc),
        out_specs=[vmem] * len(outs),
        scratch_shapes=scratch,
        input_output_aliases={len(args) - len(acc) + i: i for i in range(len(acc))},
        compiler_params=params(),
        cost_estimate=pl.CostEstimate(flops=2 * work * h[0].shape[0], bytes_accessed=work, transcendentals=0),
        name=name,
    )(*args)


def first(groups, h, acc=(), fetch=()):
    k1, cells = h.shape
    outs = (jax.ShapeDtypeStruct((k1, cells), F32), jax.ShapeDtypeStruct((8, k1), F32))
    return products(first_body, bool(acc), outs, groups, (h,), acc, "first_products", fetch)


def second(groups, t, h, code):
    k1 = h[0].shape[0]
    out = coded(t, k1) if code else jax.ShapeDtypeStruct((t, k1), F32)
    outs = (out,) * sum(len(g) - 2 for g in groups)
    return products(second_body, code, outs, groups, h, (), "second_products")


def plain(body, outs, *args, name, flag=None):
    vmem = pl.BlockSpec(memory_space=pltpu.VMEM)
    specs = [vmem] * len(args)
    if flag is not None:
        specs, args = [pl.BlockSpec(memory_space=pltpu.SMEM)] + specs, (flag, *args)
    out_specs = (vmem,) * len(outs) if isinstance(outs, tuple) else vmem
    return pl.pallas_call(
        body, out_shape=outs, in_specs=specs, out_specs=out_specs, compiler_params=params(), name=name
    )(*args)


def flip(x, axis, size, bit):
    return lax.ppermute(x, axis, [(i, i ^ bit) for i in range(size)])


def split_num(flag, num, col, keep_ref, *sends):
    inner = flag[0] == 1
    half = num.shape[1] // 2
    keep_ref[...] = jnp.where(inner, num[:, half:], num[:, :half])
    width = half // len(sends)
    for i, send in enumerate(sends):
        lo = num[:, i * width : (i + 1) * width]
        hi = num[:, half + i * width : half + (i + 1) * width]
        encode(jnp.where(inner, lo, hi), send, None if i else col[:1, :])


def add_kept(i, keep, other, *refs):
    width, k1 = other.shape[1], keep.shape[0]
    extra = None if i else decode_extra(refs[0], k1) + decode_extra(other, k1)
    encode(keep[:, i * width : (i + 1) * width] + decode(other), refs[-1], extra)


def add_coded(one, other, out_ref, *col_ref):
    encode(decode(one) + decode(other), out_ref)
    for ref in col_ref:
        k1 = ref.shape[1]
        ref[...] = jnp.broadcast_to(decode_extra(one, k1) + decode_extra(other, k1), ref.shape)


def h1_update(n, flag, *refs):
    mine, theirs, (h1_ref, col_ref, new_ref, low_ref, late_ref) = refs[:n], refs[n : 2 * n], refs[2 * n :]
    inner = flag[0] == 1
    half = h1_ref.shape[1] // 2
    width = half // n
    col = col_ref[...].T[:, :1]
    for i in range(n):
        a, b = decode(mine[i]), decode(theirs[i])
        for at, num in ((i * width, jnp.where(inner, b, a)), (half + i * width, jnp.where(inner, a, b))):
            new = h1_ref[:, at : at + width] * num / col
            new_ref[:, at : at + width] = new
            late_ref[:, at : at + width] = new
            low_ref[:, at : at + width] = new.astype(BF16)


def h1_update_plain(num, h1_ref, col_ref, new_ref, low_ref):
    new = h1_ref[...] * num[...] / col_ref[:, :1]
    new_ref[...] = new
    low_ref[...] = new.astype(BF16)


def pack(k2, lo, hi, sums, sums_in, lo_ref, hi_ref):
    total = sums[...] + sums_in[...]
    t, half = lo.shape[0], k2 // 2
    encode(lo[...], lo_ref)
    encode(total[:half], lo_ref, singles=(total[k2 : k2 + 1], total[k2 + 8 : k2 + 9]), at=t + PAD)
    encode(hi[...], hi_ref)
    encode(total[half:k2], hi_ref, at=t + PAD)


def relay_add(k2, x, x_in, y, y_in, lo, hi, x_ref, y_ref, x_sums, y_sums):
    rows, half = x.shape[0], x.shape[0] // 2
    encode(jnp.concatenate([x[:half, :], x[half:, :] + decode(x_in, half)], axis=0), x_ref)
    encode(jnp.concatenate([y[:half, :] + decode(y_in, half), y[half:, :]], axis=0), y_ref)
    at, few = half + PAD, k2 // 2
    one = [a + b for a, b in zip(decode_singles(lo, 2, lo.shape[0]), decode_singles(y_in, 2, lo.shape[0]))]
    encode(decode(lo, few, at) + decode(y_in, few, at), y_sums, singles=one)
    encode(decode(hi, few, at) + decode(x_in, few, at), x_sums)
    x_ref[rows + PAD :, :] = x_sums[...]
    y_ref[rows + PAD :, :] = y_sums[...]


def last_update(own, x, y, x_sums, y_sums, w_ref, w2t_ref, w1_ref, w2_ref):
    rows, few = own.shape[0], x_sums.shape[0] - PAD
    total = own[...] + decode(x, rows) + decode(y, rows)
    singles = zip(decode_singles(y_sums, 2, few + PAD), decode_singles(y, 2, y.shape[0]))
    row, h2_row = [a + b for a, b in singles]
    w1_ref[...] = (w_ref[...].astype(F32) * total / row).astype(BF16)
    h2_col = jnp.broadcast_to(h2_row, (8, h2_row.shape[1])).T[: 2 * few, :1]
    at = rows + PAD
    low = decode(y_sums, few) + decode(y, few, at)
    high = decode(x_sums, few) + decode(x, few, at)
    w2_ref[...] = w2t_ref[...] * jnp.concatenate([low, high], axis=0) / h2_col


def parts(x):
    hi = x.astype(BF16)
    return hi, (x - hi.astype(F32)).astype(BF16)


def mm3(a, b, dims):
    (ah, al), (bh, bl) = a, b
    return mm(ah, bh, dims) + (mm(ah, bl, dims) + mm(al, bh, dims))


def layer_two(h1_ref, w2t_ref, h2_ref, v, new_ref, sums_ref, v_out, sem):
    copy = pltpu.make_async_copy(v, v_out, sem)
    copy.start()
    h1, w2t, h2 = h1_ref[...], w2t_ref[...], h2_ref[...]
    k2, k1 = w2t.shape
    w2p = parts(w2t)
    ratio3 = h1 / mm3(w2p, parts(h2), (0, 0))
    h2_new = h2 * mm3(w2p, parts(ratio3), (1, 0)) / jnp.sum(w2t, axis=1, keepdims=True)
    new_ref[...] = h2_new
    h2p = parts(h2_new)
    ratio4 = h1 / mm3(w2p, h2p, (0, 0))
    sums_ref[:k2, :] = mm3(h2p, parts(ratio4), (1, 1))
    cells = h1.shape[1]
    row = (jnp.ones((8, cells), BF16), jnp.zeros((8, cells), BF16))
    sums_ref[k2 : k2 + 8, :] = mm3(row, parts(h1), (1, 1))
    sums_ref[k2 + 8 :, :] = jnp.zeros((8, k1), F32)
    sums_ref[k2 + 8 :, :k2] = mm3(row, h2p, (1, 1))
    copy.wait()


def on_device(n_gene, n_cell, counts, w1, h1, w2, h2):
    genes, cells = counts.shape
    rows, k1 = w1.shape
    k2 = w2.shape[1]
    chips = n_cell // 2
    me = lax.axis_index("cell")
    core, chip = me % 2, me // 2
    line = n_cell == 8 and n_gene == 4 and genes * 4 < 32768
    cell = functools.partial(flip, axis="cell", size=n_cell)
    gene = functools.partial(flip, axis="gene", size=n_gene)
    after = lax.optimization_barrier
    at = jnp.stack([chip, core]).astype(jnp.int32)

    h1_low = h1.astype(BF16)
    new_shapes = (jax.ShapeDtypeStruct((k1, cells), F32), jax.ShapeDtypeStruct((k1, cells), BF16))
    if line:
        t = rows // 2
        w_x, w_y = cell(w1, bit=2), cell(w1, bit=4)
        w_0 = cell(w1, bit=1)

        v_mine, v_theirs = split_counts(at, counts, chips, rows)
        v_other = [cell(v, bit=1) for v in v_theirs]
        on_mine, on_theirs = ([Later(v) for v in some] for some in (v_mine, v_theirs))
        acc = first(((Later(w1), on_mine[0]), (w_0, on_theirs[0])), h1_low)
        w_x, w_y, *acc = after((w_x, w_y, *acc))
        d_lo, d_hi = cell(w_y[:t], bit=2), cell(w_x[t:], bit=4)
        x_0, y_0 = cell(w_x, bit=1), cell(w_y, bit=1)
        near = ((Later(w_x), on_mine[1]), (Later(w_y), on_mine[2]), (x_0, on_theirs[1]), (y_0, on_theirs[2]))
        acc = first(near, h1_low, acc)
        d_lo, d_hi, *acc = after((d_lo, d_hi, *acc))
        v_far = after((v_mine[3], v_theirs[3], *acc))[:2]
        v_far = plain_fetch(v_far)
        far = cell(d_lo, bit=1), cell(d_hi, bit=1)
        acc = first(((d_lo, d_hi, v_far[0]),), h1_low, acc)
        num, col = first(((*far, v_far[1]),), h1_low, acc)

        z = lax.axis_index("gene")
        inner = jnp.where((z == 1) | (z == 2), 1, 0).astype(jnp.int32)[None]
        chunks = tuple(range(CHUNKS))
        piece = coded(k1, cells // 2 // CHUNKS)
        keep, *sent = plain(
            split_num, (jax.ShapeDtypeStruct((k1, cells // 2), F32),) + (piece,) * CHUNKS,
            num, col, flag=inner, name="split_num",
        )

        pair = []
        for i, x in enumerate(sent):
            got = gene(after((x, *pair))[0], bit=1)
            extra = () if i else (x,)
            pair.append(plain(functools.partial(add_kept, i), piece, keep, got, *extra, name="add_pair"))
        mine = []
        for i, x in enumerate(pair):
            outs = piece if i else (piece, jax.ShapeDtypeStruct((8, k1), F32))
            mine.append(plain(add_coded, outs, x, gene(x, bit=3), name="add_cross"))
        (first_mine, col), *mine = mine
        mine = [first_mine, *mine]
        theirs = [gene(x, bit=1) for x in mine]
        h1_new, h1_low2, h1_late = plain(
            functools.partial(h1_update, CHUNKS), new_shapes + new_shapes[:1], *mine, *theirs, h1, col,
            flag=inner, name="h1_update",
        )
        h1_low2_other = cell(h1_low2, bit=1)
    else:
        col = None
        groups = [list(range(c, n_cell, 2)) for c in (0, 1)]
        w_half = lax.all_gather(w1, "cell", axis=0, tiled=True, axis_index_groups=groups)
        v_mine, v_theirs = split_counts(at * jnp.array([0, 1], jnp.int32), counts, chips, rows)
        v_other = [cell(v, bit=1) for v in v_theirs]
        halves = [[w[j * rows : (j + 1) * rows] for j in range(chips)] for w in (w_half, cell(w_half, bit=1))]
        each = min(chips, max(1, 512 // rows))
        acc = ()
        for i in range(0, chips, each):
            for w, v in zip(halves, (v_mine, v_theirs)):
                acc = first(tuple((w[j], v[j]) for j in range(i, i + each)), h1_low, acc)
        num, col = lax.psum(tuple(acc), "gene")
        col = jnp.broadcast_to(col[0][:, None], (k1, 128))
        h1_new, h1_low2 = plain(h1_update_plain, new_shapes, num, h1, col, name="h1_update")
        h1_low2_other, h1_late = cell(h1_low2, bit=1), h1_new

    w2t = w2.T
    vmem, hbm = pl.BlockSpec(memory_space=pltpu.VMEM), pl.BlockSpec(memory_space=pltpu.HBM)
    h2_new, sums, v_far = pl.pallas_call(
        layer_two,
        out_shape=(
            jax.ShapeDtypeStruct((k2, cells), F32),
            jax.ShapeDtypeStruct((k2 + 16, k1), F32),
            jax.ShapeDtypeStruct(v_mine[-1].shape, jnp.int16),
        ),
        in_specs=[vmem] * 3 + [hbm],
        out_specs=[vmem] * 3,
        scratch_shapes=[pltpu.SemaphoreType.DMA(())],
        compiler_params=params(),
        name="layer_two",
    )(h1_late, w2t, h2, pltpu.with_memory_space_constraint(v_mine[-1], pltpu.HBM))
    low2 = (h1_low2, h1_low2_other)
    if line:
        sums_in = cell(sums, bit=1)
        d_lo, d_hi = second(((d_lo, d_hi, v_far, v_other[3]),), t, low2, False)
        sums, sums_in, d_lo = after((sums, sums_in, d_lo))
        few = k2 // 2 + PAD
        with_sums = coded(t + few, k1)
        d_lo, d_hi = plain(
            functools.partial(pack, k2), (with_sums, with_sums), d_lo, d_hi, sums, sums_in, name="pack"
        )
        y_in, x_in = cell(d_lo, bit=2), cell(d_hi, bit=4)
        w_x, d_lo = after((w_x, d_lo))
        near = ((Later(w_x), on_mine[1], v_other[1]), (Later(w_y), on_mine[2], v_other[2]))
        x_num, y_num = second(near, rows, low2, False)
        with_sums = coded(rows + few, k1)
        sums_only = jax.ShapeDtypeStruct((few, k1), jnp.int16)
        x_num, y_num, x_sums, y_sums = plain(
            functools.partial(relay_add, k2), (with_sums, with_sums, sums_only, sums_only),
            x_num, x_in, y_num, y_in, d_lo, d_hi, name="relay_add",
        )
        x_num_in, y_num_in = cell(x_num, bit=2), cell(y_num, bit=4)
        w1_late, x_num = after((w1, x_num))
        (own,) = second(((Later(w1_late), on_mine[0], v_other[0]),), rows, low2, False)
        w1_new, w2_new = plain(
            last_update, (jax.ShapeDtypeStruct((rows, k1), BF16), jax.ShapeDtypeStruct((k2, k1), F32)),
            own, x_num_in, y_num_in, x_sums, y_sums, w1, w2t, name="last_update",
        )
        w2_new = w2_new.T
    else:
        found = []
        for i in range(0, chips, each):
            some = tuple((halves[0][j], v_mine[j], v_other[j]) for j in range(i, i + each))
            found += second(some, rows, low2, False)
        w1_num = lax.psum_scatter(
            jnp.concatenate(found), "cell", scatter_dimension=0, tiled=True, axis_index_groups=groups
        )
        sums = lax.psum(sums, "cell")
        w2_new = (w2t * sums[:k2] / sums[k2 + 8, :k2, None]).T
        w1_new = (w1.astype(F32) * w1_num / sums[k2 : k2 + 1]).astype(BF16)
    return (w1_new, h1_new, w2_new, h2_new)


def solution(mesh):
    placed = (P("gene", "cell"), P(("gene", "cell"), None), P(None, "cell"), P(), P(None, "cell"))
    return jax.shard_map(
        functools.partial(on_device, mesh.shape["gene"], mesh.shape["cell"]),
        mesh=mesh,
        in_specs=placed,
        out_specs=(P(("gene", "cell"), None), P(None, "cell"), P(), P(None, "cell")),
        check_vma=False,
    )
```

```python
import functools

import jax
import jax.numpy as jnp
from jax import lax
from jax.experimental import pallas as pl
from jax.experimental.pallas import tpu as pltpu
from jax.sharding import PartitionSpec as P

F32 = jnp.float32
BF16 = jnp.bfloat16
PAD = 16
CHUNKS = 2


def params(mib=16):
    return pltpu.CompilerParams(vmem_limit_bytes=mib * 1024 * 1024)


def mm(a, b, dims):
    return lax.dot_general(a, b, ((dims[:1], dims[1:]), ((), ())), preferred_element_type=F32)


def power_of(x):
    return jnp.ceil(jnp.log2(jnp.maximum(x, 1e-30)))


def encode(x, out_ref, extra=None, singles=(), at=0):
    rows, cols = x.shape
    power = power_of(jnp.max(x, axis=0, keepdims=True))
    q = jnp.minimum(x * (jnp.exp2(-power) * 65535.0) + 0.5, 65535.0)
    out_ref[at : at + rows, :] = (q.astype(jnp.int32) - 32768).astype(jnp.int16)
    lines = [power]
    if extra is not None:
        whole = jnp.floor(extra)
        for y in (whole, jnp.floor((extra - whole) * 32768.0 + 0.25)):
            lines += [y[:, i : i + cols] for i in range(0, y.shape[1], cols)]
    for y in singles:
        own = power_of(y)
        y = y * (jnp.exp2(-own) * 32767.0)
        whole = jnp.floor(y)
        lines += [own, whole, jnp.floor((y - whole) * 32768.0)]
    lines.append(jnp.zeros((PAD - len(lines), cols), F32))
    out_ref[at + rows : at + rows + PAD, :] = jnp.concatenate(lines, axis=0).astype(jnp.int32).astype(jnp.int16)


def pad_rows(ref, end):
    return ref[end - PAD : end, :].astype(jnp.int32).astype(F32)


def decode_extra(ref, width):
    n = width // ref.shape[1]
    lines = pad_rows(ref, ref.shape[0])
    lines = [lines[1 + i : 2 + i] for i in range(2 * n)]
    return jnp.concatenate(lines[:n], axis=1) + jnp.concatenate(lines[n:], axis=1) * (1.0 / 32768.0)


def decode_singles(ref, n, end):
    lines = pad_rows(ref, end)
    found = []
    for i in range(1, 1 + 3 * n, 3):
        unit = jnp.exp2(lines[i : i + 1]) * (1.0 / 32767.0)
        found.append((lines[i + 1 : i + 2] + lines[i + 2 : i + 3] * (1.0 / 32768.0)) * unit)
    return found


def decode(ref, rows=None, at=0):
    rows = ref.shape[0] - PAD if rows is None else rows
    unit = jnp.exp2(pad_rows(ref, at + rows + PAD)[:1]) * (1.0 / 65535.0)
    return (ref[at : at + rows, :].astype(jnp.int32) + 32768).astype(F32) * unit


def coded(rows, cols):
    return jax.ShapeDtypeStruct((rows + PAD, cols), jnp.int16)


def quotient(v, approx):
    return (v.astype(jnp.int32).astype(F32) / approx).astype(BF16)


def counts_body(chips, rows, at, v, *refs):
    outs, held, low, sems = refs[: 2 * chips], *refs[2 * chips :]
    copies = []
    for q in range(chips):
        start = pl.multiple_of((at[0] ^ q) * 2 * rows, 2 * rows)
        both = pl.ds(q * 2 * rows, 2 * rows)
        copies.append(pltpu.make_async_copy(v.at[pl.ds(start, 2 * rows), :], held.at[both, :], sems.at[q]))
        copies[-1].start()
    for q in range(chips):
        copies[q].wait()
        for slot, core in ((q, at[1]), (chips + q, 1 - at[1])):
            some = held[pl.ds(pl.multiple_of((2 * q + core) * rows, rows), rows), :]
            low[slot] = some.astype(jnp.int16)
            copies.append(pltpu.make_async_copy(low.at[slot], outs[slot], sems.at[chips + slot]))
            copies[-1].start()
    for copy in copies[chips:]:
        copy.wait()


def split_counts(at, counts, chips, rows):
    cells = counts.shape[1]
    out = pltpu.HBM((rows, cells), jnp.int16)
    smem, hbm = pl.BlockSpec(memory_space=pltpu.SMEM), pl.BlockSpec(memory_space=pltpu.HBM)
    outs = pl.pallas_call(
        functools.partial(counts_body, chips, rows),
        out_shape=(out,) * (2 * chips),
        in_specs=[smem, hbm],
        out_specs=[hbm] * (2 * chips),
        scratch_shapes=[
            pltpu.VMEM(counts.shape, counts.dtype),
            pltpu.VMEM((2 * chips, rows, cells), jnp.int16),
            pltpu.SemaphoreType.DMA((3 * chips,)),
        ],
        compiler_params=params(),
        name="split_counts",
    )(at, pltpu.with_memory_space_constraint(counts, pltpu.HBM))
    return outs[:chips], outs[chips:]


class Later:
    def __init__(self, array):
        self.array = array


def fetching(refs, later, scratch):
    sems, slots, found = scratch[-1] if later else None, iter(scratch), []
    for i, ref in enumerate(refs):
        copy = None
        if i in later:
            slot = next(slots)
            copy = pltpu.make_async_copy(ref, slot, sems.at[later.index(i)])
            copy.start()
            ref = slot
        found.append((ref, copy))
    return found


def ready(operand):
    ref, copy = operand
    if copy is not None:
        copy.wait()
    return ref[...]


def joined(operands):
    return jnp.concatenate([ready(x) for x in operands], axis=0) if len(operands) > 1 else ready(operands[0])


def ahead(sources, outs, sems):
    copies = [pltpu.make_async_copy(x, out, sems.at[i]) for i, (x, out) in enumerate(zip(sources, outs))]
    for copy in copies:
        copy.start()
    return copies


def fetch_body(n, *refs):
    for copy in ahead(refs[:n], refs[n : 2 * n], refs[-1]):
        copy.wait()


def plain_fetch(arrays):
    n = len(arrays)
    vmem, hbm = pl.BlockSpec(memory_space=pltpu.VMEM), pl.BlockSpec(memory_space=pltpu.HBM)
    return pl.pallas_call(
        functools.partial(fetch_body, n),
        out_shape=[jax.ShapeDtypeStruct(x.shape, x.dtype) for x in arrays],
        in_specs=[hbm] * n,
        out_specs=[vmem] * n,
        scratch_shapes=[pltpu.SemaphoreType.DMA((n,))],
        compiler_params=params(),
        name="fetch",
    )(*(pltpu.with_memory_space_constraint(x, pltpu.HBM) for x in arrays))


def first_body(groups, later, n_ahead, has_acc, h, *refs):
    n, n_later = sum(groups) + len(groups), len(later)
    refs, sems = (refs[:-1], refs[-1:]) if n_ahead else (refs, ())
    refs, scratch = (refs[:-n_later - 1] + sems, refs[-n_later - 1 :]) if later else (refs + sems, ())
    operands = fetching(refs[:n], later, scratch)
    copies, refs = (), refs[n:]
    if n_ahead:
        copies, refs = ahead(refs[:n_ahead], refs[-1 - n_ahead : -1], refs[-1]), refs[n_ahead : -1 - n_ahead]
    num_ref, col_ref = refs[-2:]
    total, col = (refs[0][...], refs[1][...]) if has_acc else (0.0, 0.0)
    for n in groups:
        w, v = joined(operands[:n]), operands[n]
        operands = operands[n + 1 :]
        approx = mm(w, h[...], (1, 0))
        total += mm(w, quotient(ready(v), approx), (0, 0))
        col += jnp.sum(w.astype(F32), axis=0, keepdims=True)
    num_ref[...] = total
    col_ref[...] = jnp.broadcast_to(col, col_ref.shape)
    for copy in copies:
        copy.wait()


def second_body(groups, later, n_ahead, codes, ha, hb, *refs):
    n, n_later = sum(groups) + 2 * len(groups), len(later)
    refs, scratch = (refs[:-n_later - 1], refs[-n_later - 1 :]) if later else (refs, ())
    operands, outs = fetching(refs[:n], later, scratch), refs[n:]
    for n, code in zip(groups, codes):
        pieces, v, operands = operands[:n], operands[n : n + 2], operands[n + 2 :]
        w = joined(pieces)
        total = 0.0
        for h, some in ((hb, v[1]), (ha, v[0])):
            low = h[...]
            approx = mm(w, low, (1, 0))
            total += mm(quotient(ready(some), approx), low, (1, 1))
        t = w.shape[0] // len(code)
        for k, coding in enumerate(code):
            out, outs = outs[0], outs[1:]
            part = total[k * t : (k + 1) * t]
            if coding:
                encode(part, out)
            else:
                out[...] = part


def products(body, flag, outs, groups, h, acc, name, fetch=()):
    n_h = len(h)
    sizes = tuple(len(g) - n_h for g in groups)
    flat = [x for g in groups for x in g]
    later = tuple(i for i, x in enumerate(flat) if isinstance(x, Later))
    vmem, hbm = pl.BlockSpec(memory_space=pltpu.VMEM), pl.BlockSpec(memory_space=pltpu.HBM)
    specs = [hbm if i in later else vmem for i in range(len(flat))]
    flat = [pltpu.with_memory_space_constraint(x.array, pltpu.HBM) if isinstance(x, Later) else x for x in flat]
    scratch = [pltpu.VMEM(flat[i].shape, flat[i].dtype) for i in later]
    if later:
        scratch.append(pltpu.SemaphoreType.DMA((len(later),)))
    fetch = [pltpu.with_memory_space_constraint(x, pltpu.HBM) for x in fetch]
    if fetch:
        scratch.append(pltpu.SemaphoreType.DMA((len(fetch),)))
    outs = (*outs, *(jax.ShapeDtypeStruct(x.shape, x.dtype) for x in fetch))
    args = [*h, *flat, *fetch, *acc]
    work = 2 * sum(x.shape[0] for x in flat) * h[0].shape[1]
    return pl.pallas_call(
        functools.partial(body, sizes, later, len(fetch), flag),
        out_shape=outs,
        in_specs=[vmem] * n_h + specs + [hbm] * len(fetch) + [vmem] * len(acc),
        out_specs=[vmem] * len(outs),
        scratch_shapes=scratch,
        input_output_aliases={len(args) - len(acc) + i: i for i in range(len(acc))},
        compiler_params=params(),
        cost_estimate=pl.CostEstimate(flops=2 * work * h[0].shape[0], bytes_accessed=work, transcendentals=0),
        name=name,
    )(*args)


def first(groups, h, acc=(), fetch=()):
    k1, cells = h.shape
    outs = (jax.ShapeDtypeStruct((k1, cells), F32), jax.ShapeDtypeStruct((8, k1), F32))
    return products(first_body, bool(acc), outs, groups, (h,), acc, "first_products", fetch)


def second(groups, rows, h, codes):
    k1 = h[0].shape[0]
    outs = []
    for code in codes:
        t = rows // len(code)
        outs += [coded(t, k1) if c else jax.ShapeDtypeStruct((t, k1), F32) for c in code]
    return products(second_body, codes, tuple(outs), groups, h, (), "second_products")


def plain(body, outs, *args, name, flag=None):
    vmem = pl.BlockSpec(memory_space=pltpu.VMEM)
    specs = [vmem] * len(args)
    if flag is not None:
        specs, args = [pl.BlockSpec(memory_space=pltpu.SMEM)] + specs, (flag, *args)
    out_specs = (vmem,) * len(outs) if isinstance(outs, tuple) else vmem
    return pl.pallas_call(
        body, out_shape=outs, in_specs=specs, out_specs=out_specs, compiler_params=params(), name=name
    )(*args)


def flip(x, axis, size, bit):
    return lax.ppermute(x, axis, [(i, i ^ bit) for i in range(size)])


def split_num(flag, num, col, keep_ref, *sends):
    inner = flag[0] == 1
    half = num.shape[1] // 2
    keep_ref[...] = jnp.where(inner, num[:, half:], num[:, :half])
    width = half // len(sends)
    for i, send in enumerate(sends):
        lo = num[:, i * width : (i + 1) * width]
        hi = num[:, half + i * width : half + (i + 1) * width]
        encode(jnp.where(inner, lo, hi), send, None if i else col[:1, :])


def add_kept(i, keep, other, *refs):
    width, k1 = other.shape[1], keep.shape[0]
    extra = None if i else decode_extra(refs[0], k1) + decode_extra(other, k1)
    encode(keep[:, i * width : (i + 1) * width] + decode(other), refs[-1], extra)


def add_coded(one, other, out_ref, *col_ref):
    encode(decode(one) + decode(other), out_ref)
    for ref in col_ref:
        k1 = ref.shape[1]
        ref[...] = jnp.broadcast_to(decode_extra(one, k1) + decode_extra(other, k1), ref.shape)


def h1_update(n, flag, *refs):
    mine, theirs, (h1_ref, col_ref, new_ref, low_ref, late_ref) = refs[:n], refs[n : 2 * n], refs[2 * n :]
    inner = flag[0] == 1
    half = h1_ref.shape[1] // 2
    width = half // n
    col = col_ref[...].T[:, :1]
    for i in range(n):
        a, b = decode(mine[i]), decode(theirs[i])
        for at, num in ((i * width, jnp.where(inner, b, a)), (half + i * width, jnp.where(inner, a, b))):
            new = h1_ref[:, at : at + width] * num / col
            new_ref[:, at : at + width] = new
            late_ref[:, at : at + width] = new
            low_ref[:, at : at + width] = new.astype(BF16)


def h1_update_plain(num, h1_ref, col_ref, new_ref, low_ref):
    new = h1_ref[...] * num[...] / col_ref[:, :1]
    new_ref[...] = new
    low_ref[...] = new.astype(BF16)


def pack(k2, lo, hi, sums, sums_in, lo_ref, hi_ref):
    total = sums[...] + sums_in[...]
    t, half = lo.shape[0], k2 // 2
    encode(lo[...], lo_ref)
    encode(total[:half], lo_ref, singles=(total[k2 : k2 + 1], total[k2 + 8 : k2 + 9]), at=t + PAD)
    encode(hi[...], hi_ref)
    encode(total[half:k2], hi_ref, at=t + PAD)


def relay_add(k2, x, x_in, y, y_in, lo, hi, x_ref, y_ref, x_sums, y_sums):
    rows = x.shape[0]
    at, few = rows + PAD, k2 // 2
    encode(x[...] + decode(x_in, rows), x_ref)
    encode(y[...] + decode(y_in, rows), y_ref)
    one = [a + b for a, b in zip(decode_singles(lo, 2, lo.shape[0]), decode_singles(y_in, 2, lo.shape[0]))]
    encode(decode(lo, few, at) + decode(y_in, few, at), y_sums, singles=one)
    encode(decode(hi, few, at) + decode(x_in, few, at), x_sums)
    x_ref[at:, :] = x_sums[...]
    y_ref[at:, :] = y_sums[...]


def last_update(own, x_lo, x_hi, y_lo, y_hi, x_sums, y_sums, w_ref, w2t_ref, w1_ref, w2_ref):
    t, few = x_lo.shape[0] - PAD, x_sums.shape[0] - PAD
    singles = zip(decode_singles(y_sums, 2, few + PAD), decode_singles(y_lo, 2, y_lo.shape[0]))
    row, h2_row = [a + b for a, b in singles]
    for at, x, y in ((0, x_lo, y_lo), (t, x_hi, y_hi)):
        rows = slice(at, at + t)
        total = own[rows, :] + decode(x, t) + decode(y, t)
        w1_ref[rows, :] = (w_ref[rows, :].astype(F32) * total / row).astype(BF16)
    h2_col = jnp.broadcast_to(h2_row, (8, h2_row.shape[1])).T[: 2 * few, :1]
    low = decode(y_sums, few) + decode(y_lo, few, t + PAD)
    high = decode(x_sums, few) + decode(x_hi, few, t + PAD)
    w2_ref[...] = w2t_ref[...] * jnp.concatenate([low, high], axis=0) / h2_col


def parts(x):
    hi = x.astype(BF16)
    return hi, (x - hi.astype(F32)).astype(BF16)


def mm3(a, b, dims):
    (ah, al), (bh, bl) = a, b
    return mm(ah, bh, dims) + (mm(ah, bl, dims) + mm(al, bh, dims))


def layer_two(h1_ref, w2t_ref, h2_ref, v, new_ref, sums_ref, v_out, sem):
    copy = pltpu.make_async_copy(v, v_out, sem)
    copy.start()
    h1, w2t, h2 = h1_ref[...], w2t_ref[...], h2_ref[...]
    k2, k1 = w2t.shape
    w2p = parts(w2t)
    ratio3 = h1 / mm3(w2p, parts(h2), (0, 0))
    h2_new = h2 * mm3(w2p, parts(ratio3), (1, 0)) / jnp.sum(w2t, axis=1, keepdims=True)
    new_ref[...] = h2_new
    h2p = parts(h2_new)
    ratio4 = h1 / mm3(w2p, h2p, (0, 0))
    sums_ref[:k2, :] = mm3(h2p, parts(ratio4), (1, 1))
    cells = h1.shape[1]
    row = (jnp.ones((8, cells), BF16), jnp.zeros((8, cells), BF16))
    sums_ref[k2 : k2 + 8, :] = mm3(row, parts(h1), (1, 1))
    sums_ref[k2 + 8 :, :] = jnp.zeros((8, k1), F32)
    sums_ref[k2 + 8 :, :k2] = mm3(row, h2p, (1, 1))
    copy.wait()


def on_device(n_gene, n_cell, counts, w1, h1, w2, h2):
    genes, cells = counts.shape
    rows, k1 = w1.shape
    k2 = w2.shape[1]
    chips = n_cell // 2
    me = lax.axis_index("cell")
    core, chip = me % 2, me // 2
    line = n_cell == 8 and n_gene == 4 and genes * 4 < 32768
    cell = functools.partial(flip, axis="cell", size=n_cell)
    gene = functools.partial(flip, axis="gene", size=n_gene)
    after = lax.optimization_barrier
    at = jnp.stack([chip, core]).astype(jnp.int32)

    h1_low = h1.astype(BF16)
    new_shapes = (jax.ShapeDtypeStruct((k1, cells), F32), jax.ShapeDtypeStruct((k1, cells), BF16))
    if line:
        t = rows // 2
        w_x, w_y = cell(w1, bit=2), cell(w1, bit=4)
        w_0 = cell(w1, bit=1)

        v_mine, v_theirs = split_counts(at, counts, chips, rows)
        v_other = [cell(v, bit=1) for v in v_theirs]
        on_mine, on_theirs = ([Later(v) for v in some] for some in (v_mine, v_theirs))
        acc = first(((Later(w1), on_mine[0]), (w_0, on_theirs[0])), h1_low)
        w_x, w_y, *acc = after((w_x, w_y, *acc))
        d_lo, d_hi = cell(w_y[:t], bit=2), cell(w_x[t:], bit=4)
        x_0, y_0 = cell(w_x, bit=1), cell(w_y, bit=1)
        near = ((Later(w_x), on_mine[1]), (Later(w_y), on_mine[2]), (x_0, on_theirs[1]), (y_0, on_theirs[2]))
        acc = first(near, h1_low, acc)
        d_lo, d_hi, *acc = after((d_lo, d_hi, *acc))
        v_far = after((v_mine[3], v_theirs[3], *acc))[:2]
        v_far = plain_fetch(v_far)
        far = cell(d_lo, bit=1), cell(d_hi, bit=1)
        acc = first(((d_lo, d_hi, v_far[0]),), h1_low, acc)
        num, col = first(((*far, v_far[1]),), h1_low, acc)

        z = lax.axis_index("gene")
        inner = jnp.where((z == 1) | (z == 2), 1, 0).astype(jnp.int32)[None]
        chunks = tuple(range(CHUNKS))
        piece = coded(k1, cells // 2 // CHUNKS)
        keep, *sent = plain(
            split_num, (jax.ShapeDtypeStruct((k1, cells // 2), F32),) + (piece,) * CHUNKS,
            num, col, flag=inner, name="split_num",
        )

        pair = []
        for i, x in enumerate(sent):
            got = gene(after((x, *pair))[0], bit=1)
            extra = () if i else (x,)
            pair.append(plain(functools.partial(add_kept, i), piece, keep, got, *extra, name="add_pair"))
        mine = []
        for i, x in enumerate(pair):
            outs = piece if i else (piece, jax.ShapeDtypeStruct((8, k1), F32))
            mine.append(plain(add_coded, outs, x, gene(x, bit=3), name="add_cross"))
        (first_mine, col), *mine = mine
        mine = [first_mine, *mine]
        theirs = [gene(x, bit=1) for x in mine]
        h1_new, h1_low2, h1_late = plain(
            functools.partial(h1_update, CHUNKS), new_shapes + new_shapes[:1], *mine, *theirs, h1, col,
            flag=inner, name="h1_update",
        )
        h1_low2_other = cell(h1_low2, bit=1)
    else:
        col = None
        groups = [list(range(c, n_cell, 2)) for c in (0, 1)]
        w_half = lax.all_gather(w1, "cell", axis=0, tiled=True, axis_index_groups=groups)
        v_mine, v_theirs = split_counts(at * jnp.array([0, 1], jnp.int32), counts, chips, rows)
        v_other = [cell(v, bit=1) for v in v_theirs]
        halves = [[w[j * rows : (j + 1) * rows] for j in range(chips)] for w in (w_half, cell(w_half, bit=1))]
        each = min(chips, max(1, 512 // rows))
        acc = ()
        for i in range(0, chips, each):
            for w, v in zip(halves, (v_mine, v_theirs)):
                acc = first(tuple((w[j], v[j]) for j in range(i, i + each)), h1_low, acc)
        num, col = lax.psum(tuple(acc), "gene")
        col = jnp.broadcast_to(col[0][:, None], (k1, 128))
        h1_new, h1_low2 = plain(h1_update_plain, new_shapes, num, h1, col, name="h1_update")
        h1_low2_other, h1_late = cell(h1_low2, bit=1), h1_new

    w2t = w2.T
    vmem, hbm = pl.BlockSpec(memory_space=pltpu.VMEM), pl.BlockSpec(memory_space=pltpu.HBM)
    h2_new, sums, v_far = pl.pallas_call(
        layer_two,
        out_shape=(
            jax.ShapeDtypeStruct((k2, cells), F32),
            jax.ShapeDtypeStruct((k2 + 16, k1), F32),
            jax.ShapeDtypeStruct(v_mine[-1].shape, jnp.int16),
        ),
        in_specs=[vmem] * 3 + [hbm],
        out_specs=[vmem] * 3,
        scratch_shapes=[pltpu.SemaphoreType.DMA(())],
        compiler_params=params(),
        name="layer_two",
    )(h1_late, w2t, h2, pltpu.with_memory_space_constraint(v_mine[-1], pltpu.HBM))
    low2 = (h1_low2, h1_low2_other)
    if line:
        sums_in = cell(sums, bit=1)
        d_lo, d_hi = second(((d_lo, d_hi, v_far, v_other[3]),), rows, low2, ((False, False),))
        sums, sums_in, d_lo = after((sums, sums_in, d_lo))
        few = k2 // 2 + PAD
        with_sums = coded(t + few, k1)
        d_lo, d_hi = plain(
            functools.partial(pack, k2), (with_sums, with_sums), d_lo, d_hi, sums, sums_in, name="pack"
        )
        y_in, x_in = cell(d_lo, bit=2), cell(d_hi, bit=4)
        w_x, d_lo = after((w_x, d_lo))
        near = ((Later(w_x), on_mine[1], v_other[1]), (Later(w_y), on_mine[2], v_other[2]))
        x_lo, x_hi, y_lo, y_hi = second(near, rows, low2, ((True, False), (False, True)))
        x_lo_in, y_hi_in = cell(x_lo, bit=2), cell(y_hi, bit=4)
        sums_only = jax.ShapeDtypeStruct((few, k1), jnp.int16)
        x_hi, y_lo, x_sums, y_sums = plain(
            functools.partial(relay_add, k2), (with_sums, with_sums, sums_only, sums_only),
            x_hi, x_in, y_lo, y_in, d_lo, d_hi, name="relay_add",
        )
        x_hi_in, y_lo_in = cell(x_hi, bit=2), cell(y_lo, bit=4)
        w1_late, x_hi, x_lo_in, y_hi_in = after((w1, x_hi, x_lo_in, y_hi_in))
        (own,) = second(((Later(w1_late), on_mine[0], v_other[0]),), rows, low2, ((False,),))
        w1_new, w2_new = plain(
            last_update, (jax.ShapeDtypeStruct((rows, k1), BF16), jax.ShapeDtypeStruct((k2, k1), F32)),
            own, x_lo_in, x_hi_in, y_lo_in, y_hi_in, x_sums, y_sums, w1, w2t, name="last_update",
        )
        w2_new = w2_new.T
    else:
        found = []
        for i in range(0, chips, each):
            some = tuple((halves[0][j], v_mine[j], v_other[j]) for j in range(i, i + each))
            found += second(some, rows, low2, ((False,),) * each)
        w1_num = lax.psum_scatter(
            jnp.concatenate(found), "cell", scatter_dimension=0, tiled=True, axis_index_groups=groups
        )
        sums = lax.psum(sums, "cell")
        w2_new = (w2t * sums[:k2] / sums[k2 + 8, :k2, None]).T
        w1_new = (w1.astype(F32) * w1_num / sums[k2 : k2 + 1]).astype(BF16)
    return (w1_new, h1_new, w2_new, h2_new)


def solution(mesh):
    placed = (P("gene", "cell"), P(("gene", "cell"), None), P(None, "cell"), P(), P(None, "cell"))
    return jax.shard_map(
        functools.partial(on_device, mesh.shape["gene"], mesh.shape["cell"]),
        mesh=mesh,
        in_specs=placed,
        out_specs=(P(("gene", "cell"), None), P(None, "cell"), P(), P(None, "cell")),
        check_vma=False,
    )
```

```python
import functools

import jax
import jax.numpy as jnp
from jax import lax
from jax.experimental import pallas as pl
from jax.experimental.pallas import tpu as pltpu
from jax.sharding import PartitionSpec as P

F32 = jnp.float32
BF16 = jnp.bfloat16
PAD = 16
CHUNKS = 2


def params(mib=16):
    return pltpu.CompilerParams(vmem_limit_bytes=mib * 1024 * 1024)


def mm(a, b, dims):
    return lax.dot_general(a, b, ((dims[:1], dims[1:]), ((), ())), preferred_element_type=F32)


def power_of(x):
    return jnp.ceil(jnp.log2(jnp.maximum(x, 1e-30)))


def encode(x, out_ref, extra=None, singles=(), at=0):
    rows, cols = x.shape
    power = power_of(jnp.max(x, axis=0, keepdims=True))
    q = jnp.minimum(x * (jnp.exp2(-power) * 65535.0) + 0.5, 65535.0)
    out_ref[at : at + rows, :] = (q.astype(jnp.int32) - 32768).astype(jnp.int16)
    lines = [power]
    if extra is not None:
        whole = jnp.floor(extra)
        for y in (whole, jnp.floor((extra - whole) * 32768.0 + 0.25)):
            lines += [y[:, i : i + cols] for i in range(0, y.shape[1], cols)]
    for y in singles:
        own = power_of(y)
        y = y * (jnp.exp2(-own) * 32767.0)
        whole = jnp.floor(y)
        lines += [own, whole, jnp.floor((y - whole) * 32768.0)]
    lines.append(jnp.zeros((PAD - len(lines), cols), F32))
    out_ref[at + rows : at + rows + PAD, :] = jnp.concatenate(lines, axis=0).astype(jnp.int32).astype(jnp.int16)


def pad_rows(ref, end):
    return ref[end - PAD : end, :].astype(jnp.int32).astype(F32)


def decode_extra(ref, width):
    n = width // ref.shape[1]
    lines = pad_rows(ref, ref.shape[0])
    lines = [lines[1 + i : 2 + i] for i in range(2 * n)]
    return jnp.concatenate(lines[:n], axis=1) + jnp.concatenate(lines[n:], axis=1) * (1.0 / 32768.0)


def decode_singles(ref, n, end):
    lines = pad_rows(ref, end)
    found = []
    for i in range(1, 1 + 3 * n, 3):
        unit = jnp.exp2(lines[i : i + 1]) * (1.0 / 32767.0)
        found.append((lines[i + 1 : i + 2] + lines[i + 2 : i + 3] * (1.0 / 32768.0)) * unit)
    return found


def decode(ref, rows=None, at=0):
    rows = ref.shape[0] - PAD if rows is None else rows
    unit = jnp.exp2(pad_rows(ref, at + rows + PAD)[:1]) * (1.0 / 65535.0)
    return (ref[at : at + rows, :].astype(jnp.int32) + 32768).astype(F32) * unit


def coded(rows, cols):
    return jax.ShapeDtypeStruct((rows + PAD, cols), jnp.int16)


def quotient(v, approx):
    return (v.astype(jnp.int32).astype(F32) / approx).astype(BF16)


def counts_body(chips, rows, at, v, *refs):
    outs, held, low, sems = refs[: 2 * chips], *refs[2 * chips :]
    copies = []
    for q in range(chips):
        start = pl.multiple_of((at[0] ^ q) * 2 * rows, 2 * rows)
        both = pl.ds(q * 2 * rows, 2 * rows)
        copies.append(pltpu.make_async_copy(v.at[pl.ds(start, 2 * rows), :], held.at[both, :], sems.at[q]))
        copies[-1].start()
    for q in range(chips):
        copies[q].wait()
        for slot, core in ((q, at[1]), (chips + q, 1 - at[1])):
            some = held[pl.ds(pl.multiple_of((2 * q + core) * rows, rows), rows), :]
            low[slot] = some.astype(jnp.int16)
            copies.append(pltpu.make_async_copy(low.at[slot], outs[slot], sems.at[chips + slot]))
            copies[-1].start()
    for copy in copies[chips:]:
        copy.wait()


def split_counts(at, counts, chips, rows):
    cells = counts.shape[1]
    out = pltpu.HBM((rows, cells), jnp.int16)
    smem, hbm = pl.BlockSpec(memory_space=pltpu.SMEM), pl.BlockSpec(memory_space=pltpu.HBM)
    outs = pl.pallas_call(
        functools.partial(counts_body, chips, rows),
        out_shape=(out,) * (2 * chips),
        in_specs=[smem, hbm],
        out_specs=[hbm] * (2 * chips),
        scratch_shapes=[
            pltpu.VMEM(counts.shape, counts.dtype),
            pltpu.VMEM((2 * chips, rows, cells), jnp.int16),
            pltpu.SemaphoreType.DMA((3 * chips,)),
        ],
        compiler_params=params(),
        name="split_counts",
    )(at, pltpu.with_memory_space_constraint(counts, pltpu.HBM))
    return outs[:chips], outs[chips:]


class Later:
    def __init__(self, array):
        self.array = array


def fetching(refs, later, scratch):
    sems, slots, found = scratch[-1] if later else None, iter(scratch), []
    for i, ref in enumerate(refs):
        copy = None
        if i in later:
            slot = next(slots)
            copy = pltpu.make_async_copy(ref, slot, sems.at[later.index(i)])
            copy.start()
            ref = slot
        found.append((ref, copy))
    return found


def ready(operand):
    ref, copy = operand
    if copy is not None:
        copy.wait()
    return ref[...]


def joined(operands):
    return jnp.concatenate([ready(x) for x in operands], axis=0) if len(operands) > 1 else ready(operands[0])


def ahead(sources, outs, sems):
    copies = [pltpu.make_async_copy(x, out, sems.at[i]) for i, (x, out) in enumerate(zip(sources, outs))]
    for copy in copies:
        copy.start()
    return copies


def fetch_body(n, *refs):
    for copy in ahead(refs[:n], refs[n : 2 * n], refs[-1]):
        copy.wait()


def plain_fetch(arrays):
    n = len(arrays)
    vmem, hbm = pl.BlockSpec(memory_space=pltpu.VMEM), pl.BlockSpec(memory_space=pltpu.HBM)
    return pl.pallas_call(
        functools.partial(fetch_body, n),
        out_shape=[jax.ShapeDtypeStruct(x.shape, x.dtype) for x in arrays],
        in_specs=[hbm] * n,
        out_specs=[vmem] * n,
        scratch_shapes=[pltpu.SemaphoreType.DMA((n,))],
        compiler_params=params(),
        name="fetch",
    )(*(pltpu.with_memory_space_constraint(x, pltpu.HBM) for x in arrays))


def first_body(groups, later, n_ahead, has_acc, h, *refs):
    n, n_later = sum(groups) + len(groups), len(later)
    refs, sems = (refs[:-1], refs[-1:]) if n_ahead else (refs, ())
    refs, scratch = (refs[:-n_later - 1] + sems, refs[-n_later - 1 :]) if later else (refs + sems, ())
    operands = fetching(refs[:n], later, scratch)
    copies, refs = (), refs[n:]
    if n_ahead:
        copies, refs = ahead(refs[:n_ahead], refs[-1 - n_ahead : -1], refs[-1]), refs[n_ahead : -1 - n_ahead]
    num_ref, col_ref = refs[-2:]
    total, col = (refs[0][...], refs[1][...]) if has_acc else (0.0, 0.0)
    for n in groups:
        w, v = joined(operands[:n]), operands[n]
        operands = operands[n + 1 :]
        approx = mm(w, h[...], (1, 0))
        total += mm(w, quotient(ready(v), approx), (0, 0))
        col += jnp.sum(w.astype(F32), axis=0, keepdims=True)
    num_ref[...] = total
    col_ref[...] = jnp.broadcast_to(col, col_ref.shape)
    for copy in copies:
        copy.wait()


def second_body(groups, later, n_ahead, codes, ha, hb, *refs):
    n, n_later = sum(groups) + 2 * len(groups), len(later)
    refs, scratch = (refs[:-n_later - 1], refs[-n_later - 1 :]) if later else (refs, ())
    operands, outs = fetching(refs[:n], later, scratch), refs[n:]
    for n, code in zip(groups, codes):
        pieces, v, operands = operands[:n], operands[n : n + 2], operands[n + 2 :]
        w = joined(pieces)
        total = 0.0
        for h, some in ((hb, v[1]), (ha, v[0])):
            low = h[...]
            approx = mm(w, low, (1, 0))
            total += mm(quotient(ready(some), approx), low, (1, 1))
        t = w.shape[0] // len(code)
        for k, coding in enumerate(code):
            out, outs = outs[0], outs[1:]
            part = total[k * t : (k + 1) * t]
            if coding:
                encode(part, out)
            else:
                out[...] = part


def products(body, flag, outs, groups, h, acc, name, fetch=()):
    n_h = len(h)
    sizes = tuple(len(g) - n_h for g in groups)
    flat = [x for g in groups for x in g]
    later = tuple(i for i, x in enumerate(flat) if isinstance(x, Later))
    vmem, hbm = pl.BlockSpec(memory_space=pltpu.VMEM), pl.BlockSpec(memory_space=pltpu.HBM)
    specs = [hbm if i in later else vmem for i in range(len(flat))]
    flat = [pltpu.with_memory_space_constraint(x.array, pltpu.HBM) if isinstance(x, Later) else x for x in flat]
    scratch = [pltpu.VMEM(flat[i].shape, flat[i].dtype) for i in later]
    if later:
        scratch.append(pltpu.SemaphoreType.DMA((len(later),)))
    fetch = [pltpu.with_memory_space_constraint(x, pltpu.HBM) for x in fetch]
    if fetch:
        scratch.append(pltpu.SemaphoreType.DMA((len(fetch),)))
    outs = (*outs, *(jax.ShapeDtypeStruct(x.shape, x.dtype) for x in fetch))
    args = [*h, *flat, *fetch, *acc]
    work = 2 * sum(x.shape[0] for x in flat) * h[0].shape[1]
    return pl.pallas_call(
        functools.partial(body, sizes, later, len(fetch), flag),
        out_shape=outs,
        in_specs=[vmem] * n_h + specs + [hbm] * len(fetch) + [vmem] * len(acc),
        out_specs=[vmem] * len(outs),
        scratch_shapes=scratch,
        input_output_aliases={len(args) - len(acc) + i: i for i in range(len(acc))},
        compiler_params=params(),
        cost_estimate=pl.CostEstimate(flops=2 * work * h[0].shape[0], bytes_accessed=work, transcendentals=0),
        name=name,
    )(*args)


def first(groups, h, acc=(), fetch=()):
    k1, cells = h.shape
    outs = (jax.ShapeDtypeStruct((k1, cells), F32), jax.ShapeDtypeStruct((8, k1), F32))
    return products(first_body, bool(acc), outs, groups, (h,), acc, "first_products", fetch)


def second(groups, rows, h, codes):
    k1 = h[0].shape[0]
    outs = []
    for code in codes:
        t = rows // len(code)
        outs += [coded(t, k1) if c else jax.ShapeDtypeStruct((t, k1), F32) for c in code]
    return products(second_body, codes, tuple(outs), groups, h, (), "second_products")


def plain(body, outs, *args, name, flag=None):
    vmem = pl.BlockSpec(memory_space=pltpu.VMEM)
    specs = [vmem] * len(args)
    if flag is not None:
        specs, args = [pl.BlockSpec(memory_space=pltpu.SMEM)] + specs, (flag, *args)
    out_specs = (vmem,) * len(outs) if isinstance(outs, tuple) else vmem
    return pl.pallas_call(
        body, out_shape=outs, in_specs=specs, out_specs=out_specs, compiler_params=params(), name=name
    )(*args)


def flip(x, axis, size, bit):
    return lax.ppermute(x, axis, [(i, i ^ bit) for i in range(size)])


def split_num(flag, num, col, keep_ref, *sends):
    inner = flag[0] == 1
    half = num.shape[1] // 2
    keep_ref[...] = jnp.where(inner, num[:, half:], num[:, :half])
    width = half // len(sends)
    for i, send in enumerate(sends):
        lo = num[:, i * width : (i + 1) * width]
        hi = num[:, half + i * width : half + (i + 1) * width]
        encode(jnp.where(inner, lo, hi), send, None if i else col[:1, :])


def add_kept(i, keep, other, *refs):
    width, k1 = other.shape[1], keep.shape[0]
    extra = None if i else decode_extra(refs[0], k1) + decode_extra(other, k1)
    encode(keep[:, i * width : (i + 1) * width] + decode(other), refs[-1], extra)


def add_coded(one, other, out_ref, *col_ref):
    encode(decode(one) + decode(other), out_ref)
    for ref in col_ref:
        k1 = ref.shape[1]
        ref[...] = jnp.broadcast_to(decode_extra(one, k1) + decode_extra(other, k1), ref.shape)


def h1_update(n, flag, *refs):
    mine, theirs, (h1_ref, col_ref, new_ref, low_ref, late_ref) = refs[:n], refs[n : 2 * n], refs[2 * n :]
    inner = flag[0] == 1
    half = h1_ref.shape[1] // 2
    width = half // n
    col = col_ref[...].T[:, :1]
    for i in range(n):
        a, b = decode(mine[i]), decode(theirs[i])
        for at, num in ((i * width, jnp.where(inner, b, a)), (half + i * width, jnp.where(inner, a, b))):
            new = h1_ref[:, at : at + width] * num / col
            new_ref[:, at : at + width] = new
            late_ref[:, at : at + width] = new
            low_ref[:, at : at + width] = new.astype(BF16)


def h1_update_plain(num, h1_ref, col_ref, new_ref, low_ref):
    new = h1_ref[...] * num[...] / col_ref[:, :1]
    new_ref[...] = new
    low_ref[...] = new.astype(BF16)


def cut_halves(a_ref, b_ref, lo_ref, hi_ref):
    t = lo_ref.shape[0]
    lo_ref[...] = a_ref[:t, :]
    hi_ref[...] = b_ref[t:, :]


def pack(k2, lo, hi, sums, sums_in, lo_ref, hi_ref):
    total = sums[...] + sums_in[...]
    t, half = lo.shape[0], k2 // 2
    encode(lo[...], lo_ref)
    encode(total[:half], lo_ref, singles=(total[k2 : k2 + 1], total[k2 + 8 : k2 + 9]), at=t + PAD)
    encode(hi[...], hi_ref)
    encode(total[half:k2], hi_ref, at=t + PAD)


def relay_add(k2, x, x_in, y, y_in, lo, hi, x_ref, y_ref, x_sums, y_sums):
    rows = x.shape[0]
    at, few = rows + PAD, k2 // 2
    encode(x[...] + decode(x_in, rows), x_ref)
    encode(y[...] + decode(y_in, rows), y_ref)
    one = [a + b for a, b in zip(decode_singles(lo, 2, lo.shape[0]), decode_singles(y_in, 2, lo.shape[0]))]
    encode(decode(lo, few, at) + decode(y_in, few, at), y_sums, singles=one)
    encode(decode(hi, few, at) + decode(x_in, few, at), x_sums)
    x_ref[at:, :] = x_sums[...]
    y_ref[at:, :] = y_sums[...]


def early_sum(own, x_lo, y_hi, out_ref):
    t = x_lo.shape[0] - PAD
    out_ref[:t, :] = own[:t, :] + decode(x_lo)
    out_ref[t:, :] = own[t:, :] + decode(y_hi)


def last_update(base, x_hi, y_lo, x_sums, y_sums, w_ref, w2t_ref, w1_ref, w2_ref):
    t, few = base.shape[0] // 2, x_sums.shape[0] - PAD
    singles = zip(decode_singles(y_sums, 2, few + PAD), decode_singles(y_lo, 2, y_lo.shape[0]))
    row, h2_row = [a + b for a, b in singles]
    for at, late in ((0, y_lo), (t, x_hi)):
        rows = slice(at, at + t)
        total = base[rows, :] + decode(late, t)
        w1_ref[rows, :] = (w_ref[rows, :].astype(F32) * total / row).astype(BF16)
    h2_col = jnp.broadcast_to(h2_row, (8, h2_row.shape[1])).T[: 2 * few, :1]
    low = decode(y_sums, few) + decode(y_lo, few, t + PAD)
    high = decode(x_sums, few) + decode(x_hi, few, t + PAD)
    w2_ref[...] = w2t_ref[...] * jnp.concatenate([low, high], axis=0) / h2_col


def parts(x):
    hi = x.astype(BF16)
    return hi, (x - hi.astype(F32)).astype(BF16)


def mm3(a, b, dims):
    (ah, al), (bh, bl) = a, b
    if ah.shape[dims[0]] <= 64:
        one, other = (jnp.concatenate(x, axis=d) for x, d in (((ah, ah, al), dims[0]), ((bh, bl, bh), dims[1])))
        return mm(one, other, dims)
    return mm(ah, bh, dims) + (mm(ah, bl, dims) + mm(al, bh, dims))


def layer_two(n_ahead, h1_ref, w2t_ref, h2_ref, *refs):
    new_ref, sums_ref = refs[n_ahead : n_ahead + 2]
    copies = ahead(refs[:n_ahead], refs[n_ahead + 2 : -1], refs[-1])
    h1, w2t, h2 = h1_ref[...], w2t_ref[...], h2_ref[...]
    k2, k1 = w2t.shape
    w2p = parts(w2t)
    ratio3 = h1 / mm3(w2p, parts(h2), (0, 0))
    h2_new = h2 * mm3(w2p, parts(ratio3), (1, 0)) / jnp.sum(w2t, axis=1, keepdims=True)
    new_ref[...] = h2_new
    h2p = parts(h2_new)
    ratio4 = h1 / mm3(w2p, h2p, (0, 0))
    sums_ref[:k2, :] = mm3(h2p, parts(ratio4), (1, 1))
    cells = h1.shape[1]
    row = (jnp.ones((8, cells), BF16), jnp.zeros((8, cells), BF16))
    sums_ref[k2 : k2 + 8, :] = mm3(row, parts(h1), (1, 1))
    sums_ref[k2 + 8 :, :] = jnp.zeros((8, k1), F32)
    sums_ref[k2 + 8 :, :k2] = mm3(row, h2p, (1, 1))
    for copy in copies:
        copy.wait()


def on_device(n_gene, n_cell, counts, w1, h1, w2, h2):
    genes, cells = counts.shape
    rows, k1 = w1.shape
    k2 = w2.shape[1]
    chips = n_cell // 2
    me = lax.axis_index("cell")
    core, chip = me % 2, me // 2
    line = n_cell == 8 and n_gene == 4 and genes * 4 < 32768
    cell = functools.partial(flip, axis="cell", size=n_cell)
    gene = functools.partial(flip, axis="gene", size=n_gene)
    after = lax.optimization_barrier
    at = jnp.stack([chip, core]).astype(jnp.int32)

    h1_low = h1.astype(BF16)
    new_shapes = (jax.ShapeDtypeStruct((k1, cells), F32), jax.ShapeDtypeStruct((k1, cells), BF16))
    if line:
        t = rows // 2
        w_x, w_y = cell(w1, bit=2), cell(w1, bit=4)
        w_0 = cell(w1, bit=1)

        v_mine, v_theirs = split_counts(at, counts, chips, rows)
        v_other = [cell(v, bit=1) for v in v_theirs]
        on_mine, on_theirs = ([Later(v) for v in some] for some in (v_mine, v_theirs))
        acc = first(((Later(w1), on_mine[0]), (w_0, on_theirs[0])), h1_low)
        w_x, w_y, *acc = after((w_x, w_y, *acc))
        half = jax.ShapeDtypeStruct((t, k1), BF16)
        y_lo, x_hi = plain(cut_halves, (half, half), w_y, w_x, name="cut_halves")
        d_lo, d_hi = cell(y_lo, bit=2), cell(x_hi, bit=4)
        x_0, y_0 = cell(w_x, bit=1), cell(w_y, bit=1)
        near = ((w_x, on_mine[1]), (w_y, on_mine[2]), (x_0, on_theirs[1]), (y_0, on_theirs[2]))
        acc = first(near, h1_low, acc)
        d_lo, d_hi, *acc = after((d_lo, d_hi, *acc))
        far = [Later(cell(d, bit=1)) for d in (d_lo, d_hi)]
        *v_far, own_lo, own_hi = plain_fetch(after((v_mine[3], v_theirs[3], d_lo, d_hi, *acc))[:4])
        num, col = first(((own_lo, own_hi, v_far[0]), (*far, v_far[1])), h1_low, acc)

        z = lax.axis_index("gene")
        inner = jnp.where((z == 1) | (z == 2), 1, 0).astype(jnp.int32)[None]
        chunks = tuple(range(CHUNKS))
        piece = coded(k1, cells // 2 // CHUNKS)
        keep, *sent = plain(
            split_num, (jax.ShapeDtypeStruct((k1, cells // 2), F32),) + (piece,) * CHUNKS,
            num, col, flag=inner, name="split_num",
        )

        pair = []
        for i, x in enumerate(sent):
            got = gene(after((x, *pair))[0], bit=1)
            extra = () if i else (x,)
            pair.append(plain(functools.partial(add_kept, i), piece, keep, got, *extra, name="add_pair"))
        mine = []
        for i, x in enumerate(pair):
            outs = piece if i else (piece, jax.ShapeDtypeStruct((8, k1), F32))
            mine.append(plain(add_coded, outs, x, gene(x, bit=3), name="add_cross"))
        (first_mine, col), *mine = mine
        mine = [first_mine, *mine]
        theirs = [gene(x, bit=1) for x in mine]
        h1_new, h1_low2, h1_late = plain(
            functools.partial(h1_update, CHUNKS), new_shapes + new_shapes[:1], *mine, *theirs, h1, col,
            flag=inner, name="h1_update",
        )
        h1_low2_other = cell(h1_low2, bit=1)
    else:
        col = None
        groups = [list(range(c, n_cell, 2)) for c in (0, 1)]
        w_half = lax.all_gather(w1, "cell", axis=0, tiled=True, axis_index_groups=groups)
        v_mine, v_theirs = split_counts(at * jnp.array([0, 1], jnp.int32), counts, chips, rows)
        v_other = [cell(v, bit=1) for v in v_theirs]
        halves = [[w[j * rows : (j + 1) * rows] for j in range(chips)] for w in (w_half, cell(w_half, bit=1))]
        each = min(chips, max(1, 512 // rows))
        acc = ()
        for i in range(0, chips, each):
            for w, v in zip(halves, (v_mine, v_theirs)):
                acc = first(tuple((w[j], v[j]) for j in range(i, i + each)), h1_low, acc)
        num, col = lax.psum(tuple(acc), "gene")
        col = jnp.broadcast_to(col[0][:, None], (k1, 128))
        h1_new, h1_low2 = plain(h1_update_plain, new_shapes, num, h1, col, name="h1_update")
        h1_low2_other, h1_late = cell(h1_low2, bit=1), h1_new

    w2t = w2.T
    vmem, hbm = pl.BlockSpec(memory_space=pltpu.VMEM), pl.BlockSpec(memory_space=pltpu.HBM)
    soon = [pltpu.with_memory_space_constraint(x, pltpu.HBM) for x in ((v_mine[3], d_lo, d_hi) if line else v_mine[:1])]
    h2_new, sums, *soon = pl.pallas_call(
        functools.partial(layer_two, len(soon)),
        out_shape=(
            jax.ShapeDtypeStruct((k2, cells), F32),
            jax.ShapeDtypeStruct((k2 + 16, k1), F32),
            *(jax.ShapeDtypeStruct(x.shape, x.dtype) for x in soon),
        ),
        in_specs=[vmem] * 3 + [hbm] * len(soon),
        out_specs=[vmem] * (2 + len(soon)),
        scratch_shapes=[pltpu.SemaphoreType.DMA((len(soon),))],
        compiler_params=params(),
        name="layer_two",
    )(h1_late, w2t, h2, *soon)
    low2 = (h1_low2, h1_low2_other)
    if line:
        sums_in = cell(sums, bit=1)
        v_far, d_lo, d_hi = soon
        d_lo, d_hi = second(((d_lo, d_hi, v_far, v_other[3]),), rows, low2, ((False, False),))
        sums, sums_in, d_lo = after((sums, sums_in, d_lo))
        few = k2 // 2 + PAD
        with_sums = coded(t + few, k1)
        d_lo, d_hi = plain(
            functools.partial(pack, k2), (with_sums, with_sums), d_lo, d_hi, sums, sums_in, name="pack"
        )
        y_in, x_in = cell(d_lo, bit=2), cell(d_hi, bit=4)
        w_x, d_lo = after((w_x, d_lo))
        near = ((Later(w_x), on_mine[1], v_other[1]), (Later(w_y), on_mine[2], v_other[2]))
        x_lo, x_hi, y_lo, y_hi = second(near, rows, low2, ((True, False), (False, True)))
        x_lo_in, y_hi_in = cell(x_lo, bit=2), cell(y_hi, bit=4)
        sums_only = jax.ShapeDtypeStruct((few, k1), jnp.int16)
        x_hi, y_lo, x_sums, y_sums = plain(
            functools.partial(relay_add, k2), (with_sums, with_sums, sums_only, sums_only),
            x_hi, x_in, y_lo, y_in, d_lo, d_hi, name="relay_add",
        )
        x_hi_in, y_lo_in = cell(x_hi, bit=2), cell(y_lo, bit=4)
        w1_late, x_hi, x_lo_in, y_hi_in = after((w1, x_hi, x_lo_in, y_hi_in))
        (own,) = second(((Later(w1_late), on_mine[0], v_other[0]),), rows, low2, ((False,),))
        base = plain(
            early_sum, jax.ShapeDtypeStruct((rows, k1), F32), own, x_lo_in, y_hi_in, name="early_sum"
        )
        w1_new, w2_new = plain(
            last_update, (jax.ShapeDtypeStruct((rows, k1), BF16), jax.ShapeDtypeStruct((k2, k1), F32)),
            base, x_hi_in, y_lo_in, x_sums, y_sums, w1, w2t, name="last_update",
        )
        w2_new = w2_new.T
    else:
        found = []
        for i in range(0, chips, each):
            some = tuple((halves[0][j], v_mine[j], v_other[j]) for j in range(i, i + each))
            found += second(some, rows, low2, ((False,),) * each)
        w1_num = lax.psum_scatter(
            jnp.concatenate(found), "cell", scatter_dimension=0, tiled=True, axis_index_groups=groups
        )
        sums = lax.psum(sums, "cell")
        w2_new = (w2t * sums[:k2] / sums[k2 + 8, :k2, None]).T
        w1_new = (w1.astype(F32) * w1_num / sums[k2 : k2 + 1]).astype(BF16)
    return (w1_new, h1_new, w2_new, h2_new)


def solution(mesh):
    placed = (P("gene", "cell"), P(("gene", "cell"), None), P(None, "cell"), P(), P(None, "cell"))
    return jax.shard_map(
        functools.partial(on_device, mesh.shape["gene"], mesh.shape["cell"]),
        mesh=mesh,
        in_specs=placed,
        out_specs=(P(("gene", "cell"), None), P(None, "cell"), P(), P(None, "cell")),
        check_vma=False,
    )
```

```python
import functools

import jax
import jax.numpy as jnp
from jax import lax
from jax.experimental import pallas as pl
from jax.experimental.pallas import tpu as pltpu
from jax.sharding import PartitionSpec as P

F32 = jnp.float32
BF16 = jnp.bfloat16
PAD = 16
CHUNKS = 2


def params(mib=16):
    return pltpu.CompilerParams(vmem_limit_bytes=mib * 1024 * 1024)


def mm(a, b, dims):
    return lax.dot_general(a, b, ((dims[:1], dims[1:]), ((), ())), preferred_element_type=F32)


def power_of(x):
    return jnp.ceil(jnp.log2(jnp.maximum(x, 1e-30)))


def encode(x, out_ref, extra=None, singles=(), at=0):
    rows, cols = x.shape
    power = power_of(jnp.max(x, axis=0, keepdims=True))
    q = jnp.minimum(x * (jnp.exp2(-power) * 65535.0) + 0.5, 65535.0)
    out_ref[at : at + rows, :] = (q.astype(jnp.int32) - 32768).astype(jnp.int16)
    lines = [power]
    if extra is not None:
        whole = jnp.floor(extra)
        for y in (whole, jnp.floor((extra - whole) * 32768.0 + 0.25)):
            lines += [y[:, i : i + cols] for i in range(0, y.shape[1], cols)]
    for y in singles:
        own = power_of(y)
        y = y * (jnp.exp2(-own) * 32767.0)
        whole = jnp.floor(y)
        lines += [own, whole, jnp.floor((y - whole) * 32768.0)]
    lines.append(jnp.zeros((PAD - len(lines), cols), F32))
    out_ref[at + rows : at + rows + PAD, :] = jnp.concatenate(lines, axis=0).astype(jnp.int32).astype(jnp.int16)


def pad_rows(ref, end):
    return ref[end - PAD : end, :].astype(jnp.int32).astype(F32)


def decode_extra(ref, width):
    n = width // ref.shape[1]
    lines = pad_rows(ref, ref.shape[0])
    lines = [lines[1 + i : 2 + i] for i in range(2 * n)]
    return jnp.concatenate(lines[:n], axis=1) + jnp.concatenate(lines[n:], axis=1) * (1.0 / 32768.0)


def decode_singles(ref, n, end):
    lines = pad_rows(ref, end)
    found = []
    for i in range(1, 1 + 3 * n, 3):
        unit = jnp.exp2(lines[i : i + 1]) * (1.0 / 32767.0)
        found.append((lines[i + 1 : i + 2] + lines[i + 2 : i + 3] * (1.0 / 32768.0)) * unit)
    return found


def decode(ref, rows=None, at=0):
    rows = ref.shape[0] - PAD if rows is None else rows
    unit = jnp.exp2(pad_rows(ref, at + rows + PAD)[:1]) * (1.0 / 65535.0)
    return (ref[at : at + rows, :].astype(jnp.int32) + 32768).astype(F32) * unit


def coded(rows, cols):
    return jax.ShapeDtypeStruct((rows + PAD, cols), jnp.int16)


def quotient(v, approx):
    return (v.astype(jnp.int32).astype(F32) / approx).astype(BF16)


def counts_body(chips, rows, at, v, *refs):
    outs, held, low, sems = refs[: 2 * chips], *refs[2 * chips :]
    copies = []
    for q in range(chips):
        start = pl.multiple_of((at[0] ^ q) * 2 * rows, 2 * rows)
        both = pl.ds(q * 2 * rows, 2 * rows)
        copies.append(pltpu.make_async_copy(v.at[pl.ds(start, 2 * rows), :], held.at[both, :], sems.at[q]))
        copies[-1].start()
    for q in range(chips):
        copies[q].wait()
        for slot, core in ((q, at[1]), (chips + q, 1 - at[1])):
            some = held[pl.ds(pl.multiple_of((2 * q + core) * rows, rows), rows), :]
            low[slot] = some.astype(jnp.int16)
            copies.append(pltpu.make_async_copy(low.at[slot], outs[slot], sems.at[chips + slot]))
            copies[-1].start()
    for copy in copies[chips:]:
        copy.wait()


def split_counts(at, counts, chips, rows):
    cells = counts.shape[1]
    out = pltpu.HBM((rows, cells), jnp.int16)
    smem, hbm = pl.BlockSpec(memory_space=pltpu.SMEM), pl.BlockSpec(memory_space=pltpu.HBM)
    outs = pl.pallas_call(
        functools.partial(counts_body, chips, rows),
        out_shape=(out,) * (2 * chips),
        in_specs=[smem, hbm],
        out_specs=[hbm] * (2 * chips),
        scratch_shapes=[
            pltpu.VMEM(counts.shape, counts.dtype),
            pltpu.VMEM((2 * chips, rows, cells), jnp.int16),
            pltpu.SemaphoreType.DMA((3 * chips,)),
        ],
        compiler_params=params(),
        name="split_counts",
    )(at, pltpu.with_memory_space_constraint(counts, pltpu.HBM))
    return outs[:chips], outs[chips:]


class Later:
    def __init__(self, array):
        self.array = array


def fetching(refs, later, scratch):
    sems, slots, found = scratch[-1] if later else None, iter(scratch), []
    for i, ref in enumerate(refs):
        copy = None
        if i in later:
            slot = next(slots)
            copy = pltpu.make_async_copy(ref, slot, sems.at[later.index(i)])
            copy.start()
            ref = slot
        found.append((ref, copy))
    return found


def ready(operand):
    ref, copy = operand
    if copy is not None:
        copy.wait()
    return ref[...]


def joined(operands):
    return jnp.concatenate([ready(x) for x in operands], axis=0) if len(operands) > 1 else ready(operands[0])


def ahead(sources, outs, sems):
    copies = [pltpu.make_async_copy(x, out, sems.at[i]) for i, (x, out) in enumerate(zip(sources, outs))]
    for copy in copies:
        copy.start()
    return copies


def fetch_body(n, *refs):
    for copy in ahead(refs[:n], refs[n : 2 * n], refs[-1]):
        copy.wait()


def plain_fetch(arrays):
    n = len(arrays)
    vmem, hbm = pl.BlockSpec(memory_space=pltpu.VMEM), pl.BlockSpec(memory_space=pltpu.HBM)
    return pl.pallas_call(
        functools.partial(fetch_body, n),
        out_shape=[jax.ShapeDtypeStruct(x.shape, x.dtype) for x in arrays],
        in_specs=[hbm] * n,
        out_specs=[vmem] * n,
        scratch_shapes=[pltpu.SemaphoreType.DMA((n,))],
        compiler_params=params(),
        name="fetch",
    )(*(pltpu.with_memory_space_constraint(x, pltpu.HBM) for x in arrays))


def first_body(groups, later, n_ahead, has_acc, h, *refs):
    n, n_later = sum(groups) + len(groups), len(later)
    refs, sems = (refs[:-1], refs[-1:]) if n_ahead else (refs, ())
    refs, scratch = (refs[:-n_later - 1] + sems, refs[-n_later - 1 :]) if later else (refs + sems, ())
    operands = fetching(refs[:n], later, scratch)
    copies, refs = (), refs[n:]
    if n_ahead:
        copies, refs = ahead(refs[:n_ahead], refs[-1 - n_ahead : -1], refs[-1]), refs[n_ahead : -1 - n_ahead]
    num_ref, col_ref = refs[-2:]
    total, col = (refs[0][...], refs[1][...]) if has_acc else (0.0, 0.0)
    for n in groups:
        w, v = joined(operands[:n]), operands[n]
        operands = operands[n + 1 :]
        approx = mm(w, h[...], (1, 0))
        total += mm(w, quotient(ready(v), approx), (0, 0))
        col += jnp.sum(w.astype(F32), axis=0, keepdims=True)
    num_ref[...] = total
    col_ref[...] = jnp.broadcast_to(col, col_ref.shape)
    for copy in copies:
        copy.wait()


def second_body(groups, later, n_ahead, codes, ha, hb, *refs):
    n, n_later = sum(groups) + 2 * len(groups), len(later)
    refs, scratch = (refs[:-n_later - 1], refs[-n_later - 1 :]) if later else (refs, ())
    operands, outs = fetching(refs[:n], later, scratch), refs[n:]
    for n, code in zip(groups, codes):
        pieces, v, operands = operands[:n], operands[n : n + 2], operands[n + 2 :]
        w = joined(pieces)
        total = 0.0
        for h, some in ((hb, v[1]), (ha, v[0])):
            low = h[...]
            approx = mm(w, low, (1, 0))
            total += mm(quotient(ready(some), approx), low, (1, 1))
        t = w.shape[0] // len(code)
        for k, coding in enumerate(code):
            out, outs = outs[0], outs[1:]
            part = total[k * t : (k + 1) * t]
            if coding:
                encode(part, out)
            else:
                out[...] = part


def products(body, flag, outs, groups, h, acc, name, fetch=()):
    n_h = len(h)
    sizes = tuple(len(g) - n_h for g in groups)
    flat = [x for g in groups for x in g]
    later = tuple(i for i, x in enumerate(flat) if isinstance(x, Later))
    vmem, hbm = pl.BlockSpec(memory_space=pltpu.VMEM), pl.BlockSpec(memory_space=pltpu.HBM)
    specs = [hbm if i in later else vmem for i in range(len(flat))]
    flat = [pltpu.with_memory_space_constraint(x.array, pltpu.HBM) if isinstance(x, Later) else x for x in flat]
    scratch = [pltpu.VMEM(flat[i].shape, flat[i].dtype) for i in later]
    if later:
        scratch.append(pltpu.SemaphoreType.DMA((len(later),)))
    fetch = [pltpu.with_memory_space_constraint(x, pltpu.HBM) for x in fetch]
    if fetch:
        scratch.append(pltpu.SemaphoreType.DMA((len(fetch),)))
    outs = (*outs, *(jax.ShapeDtypeStruct(x.shape, x.dtype) for x in fetch))
    args = [*h, *flat, *fetch, *acc]
    work = 2 * sum(x.shape[0] for x in flat) * h[0].shape[1]
    return pl.pallas_call(
        functools.partial(body, sizes, later, len(fetch), flag),
        out_shape=outs,
        in_specs=[vmem] * n_h + specs + [hbm] * len(fetch) + [vmem] * len(acc),
        out_specs=[vmem] * len(outs),
        scratch_shapes=scratch,
        input_output_aliases={len(args) - len(acc) + i: i for i in range(len(acc))},
        compiler_params=params(),
        cost_estimate=pl.CostEstimate(flops=2 * work * h[0].shape[0], bytes_accessed=work, transcendentals=0),
        name=name,
    )(*args)


def first(groups, h, acc=(), fetch=()):
    k1, cells = h.shape
    outs = (jax.ShapeDtypeStruct((k1, cells), F32), jax.ShapeDtypeStruct((8, k1), F32))
    return products(first_body, bool(acc), outs, groups, (h,), acc, "first_products", fetch)


def second(groups, rows, h, codes):
    k1 = h[0].shape[0]
    outs = []
    for code in codes:
        t = rows // len(code)
        outs += [coded(t, k1) if c else jax.ShapeDtypeStruct((t, k1), F32) for c in code]
    return products(second_body, codes, tuple(outs), groups, h, (), "second_products")


def plain(body, outs, *args, name, flag=None):
    vmem = pl.BlockSpec(memory_space=pltpu.VMEM)
    specs = [vmem] * len(args)
    if flag is not None:
        specs, args = [pl.BlockSpec(memory_space=pltpu.SMEM)] + specs, (flag, *args)
    out_specs = (vmem,) * len(outs) if isinstance(outs, tuple) else vmem
    return pl.pallas_call(
        body, out_shape=outs, in_specs=specs, out_specs=out_specs, compiler_params=params(), name=name
    )(*args)


def flip(x, axis, size, bit):
    return lax.ppermute(x, axis, [(i, i ^ bit) for i in range(size)])


def split_num(flag, num, col, keep_ref, *sends):
    inner = flag[0] == 1
    half = num.shape[1] // 2
    keep_ref[...] = jnp.where(inner, num[:, half:], num[:, :half])
    width = half // len(sends)
    for i, send in enumerate(sends):
        lo = num[:, i * width : (i + 1) * width]
        hi = num[:, half + i * width : half + (i + 1) * width]
        encode(jnp.where(inner, lo, hi), send, None if i else col[:1, :])


def add_kept(i, keep, other, *refs):
    width, k1 = other.shape[1], keep.shape[0]
    extra = None if i else decode_extra(refs[0], k1) + decode_extra(other, k1)
    encode(keep[:, i * width : (i + 1) * width] + decode(other), refs[-1], extra)


def add_coded(one, other, out_ref, *col_ref):
    encode(decode(one) + decode(other), out_ref)
    for ref in col_ref:
        k1 = ref.shape[1]
        ref[...] = jnp.broadcast_to(decode_extra(one, k1) + decode_extra(other, k1), ref.shape)


def h1_update(n, flag, *refs):
    mine, theirs, (h1_ref, col_ref, low_ref, late_ref) = refs[:n], refs[n : 2 * n], refs[2 * n :]
    inner = flag[0] == 1
    half = h1_ref.shape[1] // 2
    width = half // n
    col = col_ref[...].T[:, :1]
    for i in range(n):
        a, b = decode(mine[i]), decode(theirs[i])
        for at, num in ((i * width, jnp.where(inner, b, a)), (half + i * width, jnp.where(inner, a, b))):
            new = h1_ref[:, at : at + width] * num / col
            late_ref[:, at : at + width] = new
            low_ref[:, at : at + width] = new.astype(BF16)


def h1_update_plain(num, h1_ref, col_ref, new_ref, low_ref):
    new = h1_ref[...] * num[...] / col_ref[:, :1]
    new_ref[...] = new
    low_ref[...] = new.astype(BF16)


def cut_halves(a_ref, b_ref, lo_ref, hi_ref):
    t = lo_ref.shape[0]
    lo_ref[...] = a_ref[:t, :]
    hi_ref[...] = b_ref[t:, :]


def pack(k2, lo, hi, sums, sums_in, lo_ref, hi_ref):
    total = sums[...] + sums_in[...]
    t, half = lo.shape[0], k2 // 2
    encode(lo[...], lo_ref)
    encode(total[:half], lo_ref, singles=(total[k2 : k2 + 1], total[k2 + 8 : k2 + 9]), at=t + PAD)
    encode(hi[...], hi_ref)
    encode(total[half:k2], hi_ref, at=t + PAD)


def relay_add(k2, x, x_in, y, y_in, lo, hi, x_ref, y_ref, x_sums, y_sums):
    rows = x.shape[0]
    at, few = rows + PAD, k2 // 2
    encode(x[...] + decode(x_in, rows), x_ref)
    encode(y[...] + decode(y_in, rows), y_ref)
    one = [a + b for a, b in zip(decode_singles(lo, 2, lo.shape[0]), decode_singles(y_in, 2, lo.shape[0]))]
    encode(decode(lo, few, at) + decode(y_in, few, at), y_sums, singles=one)
    encode(decode(hi, few, at) + decode(x_in, few, at), x_sums)
    x_ref[at:, :] = x_sums[...]
    y_ref[at:, :] = y_sums[...]


def early_sum(own, x_lo, y_hi, w_ref, w2t_ref, out_ref, w_out, w2t_out):
    w_out[...], w2t_out[...] = w_ref[...], w2t_ref[...]
    t = x_lo.shape[0] - PAD
    out_ref[:t, :] = own[:t, :] + decode(x_lo)
    out_ref[t:, :] = own[t:, :] + decode(y_hi)


def last_update(base, x_hi, y_lo, x_sums, y_sums, w_ref, w2t_ref, w1_ref, w2_ref):
    t, few = base.shape[0] // 2, x_sums.shape[0] - PAD
    singles = zip(decode_singles(y_sums, 2, few + PAD), decode_singles(y_lo, 2, y_lo.shape[0]))
    row, h2_row = [a + b for a, b in singles]
    for at, late in ((0, y_lo), (t, x_hi)):
        rows = slice(at, at + t)
        total = base[rows, :] + decode(late, t)
        w1_ref[rows, :] = (w_ref[rows, :].astype(F32) * total / row).astype(BF16)
    h2_col = jnp.broadcast_to(h2_row, (8, h2_row.shape[1])).T[: 2 * few, :1]
    low = decode(y_sums, few) + decode(y_lo, few, t + PAD)
    high = decode(x_sums, few) + decode(x_hi, few, t + PAD)
    w2_ref[...] = w2t_ref[...] * jnp.concatenate([low, high], axis=0) / h2_col


def parts(x):
    hi = x.astype(BF16)
    return hi, (x - hi.astype(F32)).astype(BF16)


def mm3(a, b, dims):
    (ah, al), (bh, bl) = a, b
    if ah.shape[dims[0]] <= 64:
        one, other = (jnp.concatenate(x, axis=d) for x, d in (((ah, ah, al), dims[0]), ((bh, bl, bh), dims[1])))
        return mm(one, other, dims)
    m = ah.shape[1 - dims[0]]
    if m <= 64:
        both = mm(jnp.concatenate((ah, al), axis=1 - dims[0]), bh, dims)
        return both[:m] + (both[m:] + mm(ah, bl, dims))
    return mm(ah, bh, dims) + (mm(ah, bl, dims) + mm(al, bh, dims))


def layer_two(n_ahead, h1_ref, w2t_ref, h2_ref, *refs):
    new_ref, sums_ref = refs[n_ahead : n_ahead + 2]
    copies = ahead((*refs[:n_ahead], h1_ref), refs[n_ahead + 2 : -1], refs[-1])
    h1, w2t, h2 = h1_ref[...], w2t_ref[...], h2_ref[...]
    k2, k1 = w2t.shape
    w2p = parts(w2t)
    ratio3 = h1 / mm3(w2p, parts(h2), (0, 0))
    h2_new = h2 * mm3(w2p, parts(ratio3), (1, 0)) / jnp.sum(w2t, axis=1, keepdims=True)
    new_ref[...] = h2_new
    h2p = parts(h2_new)
    ratio4 = h1 / mm3(w2p, h2p, (0, 0))
    sums_ref[:k2, :] = mm3(h2p, parts(ratio4), (1, 1))
    cells = h1.shape[1]
    row = jnp.ones((8, cells), BF16)
    sums_ref[k2 : k2 + 8, :] = sum(mm(row, x, (1, 1)) for x in parts(h1))
    sums_ref[k2 + 8 :, :] = jnp.zeros((8, k1), F32)
    sums_ref[k2 + 8 :, :k2] = sum(mm(row, x, (1, 1)) for x in h2p)
    for copy in copies:
        copy.wait()


def on_device(n_gene, n_cell, counts, w1, h1, w2, h2):
    genes, cells = counts.shape
    rows, k1 = w1.shape
    k2 = w2.shape[1]
    chips = n_cell // 2
    me = lax.axis_index("cell")
    core, chip = me % 2, me // 2
    line = n_cell == 8 and n_gene == 4 and genes * 4 < 32768
    cell = functools.partial(flip, axis="cell", size=n_cell)
    gene = functools.partial(flip, axis="gene", size=n_gene)
    after = lax.optimization_barrier
    at = jnp.stack([chip, core]).astype(jnp.int32)

    h1_low = h1.astype(BF16)
    new_shapes = (jax.ShapeDtypeStruct((k1, cells), F32), jax.ShapeDtypeStruct((k1, cells), BF16))
    if line:
        t = rows // 2
        w_x, w_y = cell(w1, bit=2), cell(w1, bit=4)
        w_0 = cell(w1, bit=1)

        v_mine, v_theirs = split_counts(at, counts, chips, rows)
        v_other = [cell(v, bit=1) for v in v_theirs]
        on_mine, on_theirs = ([Later(v) for v in some] for some in (v_mine, v_theirs))
        acc = first(((Later(w1), on_mine[0]), (w_0, on_theirs[0])), h1_low)
        w_x, w_y, *acc = after((w_x, w_y, *acc))
        half = jax.ShapeDtypeStruct((t, k1), BF16)
        y_lo, x_hi = plain(cut_halves, (half, half), w_y, w_x, name="cut_halves")
        d_lo, d_hi = cell(y_lo, bit=2), cell(x_hi, bit=4)
        x_0, y_0 = cell(w_x, bit=1), cell(w_y, bit=1)
        near = ((w_x, on_mine[1]), (w_y, on_mine[2]), (x_0, on_theirs[1]), (y_0, on_theirs[2]))
        acc = first(near, h1_low, acc)
        d_lo, d_hi, *acc = after((d_lo, d_hi, *acc))
        far = [Later(cell(d, bit=1)) for d in (d_lo, d_hi)]
        *v_far, own_lo, own_hi = plain_fetch(after((v_mine[3], v_theirs[3], d_lo, d_hi, *acc))[:4])
        num, col = first(((own_lo, own_hi, v_far[0]), (*far, v_far[1])), h1_low, acc)

        z = lax.axis_index("gene")
        inner = jnp.where((z == 1) | (z == 2), 1, 0).astype(jnp.int32)[None]
        chunks = tuple(range(CHUNKS))
        piece = coded(k1, cells // 2 // CHUNKS)
        keep, *sent = plain(
            split_num, (jax.ShapeDtypeStruct((k1, cells // 2), F32),) + (piece,) * CHUNKS,
            num, col, flag=inner, name="split_num",
        )

        pair = []
        for i, x in enumerate(sent):
            got = gene(after((x, *pair))[0], bit=1)
            extra = () if i else (x,)
            pair.append(plain(functools.partial(add_kept, i), piece, keep, got, *extra, name="add_pair"))
        mine = []
        for i, x in enumerate(pair):
            outs = piece if i else (piece, jax.ShapeDtypeStruct((8, k1), F32))
            mine.append(plain(add_coded, outs, x, gene(x, bit=3), name="add_cross"))
        (first_mine, col), *mine = mine
        mine = [first_mine, *mine]
        theirs = [gene(x, bit=1) for x in mine]
        h1_low2, h1_late = plain(
            functools.partial(h1_update, CHUNKS), new_shapes[::-1], *mine, *theirs, h1, col,
            flag=inner, name="h1_update",
        )
        h1_low2_other = cell(h1_low2, bit=1)
    else:
        col = None
        groups = [list(range(c, n_cell, 2)) for c in (0, 1)]
        w_half = lax.all_gather(w1, "cell", axis=0, tiled=True, axis_index_groups=groups)
        v_mine, v_theirs = split_counts(at * jnp.array([0, 1], jnp.int32), counts, chips, rows)
        v_other = [cell(v, bit=1) for v in v_theirs]
        halves = [[w[j * rows : (j + 1) * rows] for j in range(chips)] for w in (w_half, cell(w_half, bit=1))]
        each = min(chips, max(1, 512 // rows))
        acc = ()
        for i in range(0, chips, each):
            for w, v in zip(halves, (v_mine, v_theirs)):
                acc = first(tuple((w[j], v[j]) for j in range(i, i + each)), h1_low, acc)
        num, col = lax.psum(tuple(acc), "gene")
        col = jnp.broadcast_to(col[0][:, None], (k1, 128))
        h1_new, h1_low2 = plain(h1_update_plain, new_shapes, num, h1, col, name="h1_update")
        h1_low2_other, h1_late = cell(h1_low2, bit=1), h1_new

    w2t = w2.T
    vmem, hbm = pl.BlockSpec(memory_space=pltpu.VMEM), pl.BlockSpec(memory_space=pltpu.HBM)
    soon = [pltpu.with_memory_space_constraint(x, pltpu.HBM) for x in ((v_mine[3], d_lo, d_hi) if line else v_mine[:1])]
    h2_new, sums, *soon, h1_new = pl.pallas_call(
        functools.partial(layer_two, len(soon)),
        out_shape=(
            jax.ShapeDtypeStruct((k2, cells), F32),
            jax.ShapeDtypeStruct((k2 + 16, k1), F32),
            *(jax.ShapeDtypeStruct(x.shape, x.dtype) for x in soon),
            pltpu.HBM(h1.shape, F32),
        ),
        in_specs=[vmem] * 3 + [hbm] * len(soon),
        out_specs=[vmem] * (2 + len(soon)) + [hbm],
        scratch_shapes=[pltpu.SemaphoreType.DMA((len(soon) + 1,))],
        compiler_params=params(),
        name="layer_two",
    )(h1_late, w2t, h2, *soon)
    low2 = (h1_low2, h1_low2_other)
    if line:
        sums_in = cell(sums, bit=1)
        v_far, d_lo, d_hi = soon
        d_lo, d_hi = second(((d_lo, d_hi, v_far, v_other[3]),), rows, low2, ((False, False),))
        sums, sums_in, d_lo = after((sums, sums_in, d_lo))
        few = k2 // 2 + PAD
        with_sums = coded(t + few, k1)
        d_lo, d_hi = plain(
            functools.partial(pack, k2), (with_sums, with_sums), d_lo, d_hi, sums, sums_in, name="pack"
        )
        y_in, x_in = cell(d_lo, bit=2), cell(d_hi, bit=4)
        w_x, d_lo = after((w_x, d_lo))
        near = ((Later(w_x), on_mine[1], v_other[1]), (Later(w_y), on_mine[2], v_other[2]))
        x_lo, x_hi, y_lo, y_hi = second(near, rows, low2, ((True, False), (False, True)))
        x_lo_in, y_hi_in = cell(x_lo, bit=2), cell(y_hi, bit=4)
        sums_only = jax.ShapeDtypeStruct((few, k1), jnp.int16)
        x_hi, y_lo, x_sums, y_sums = plain(
            functools.partial(relay_add, k2), (with_sums, with_sums, sums_only, sums_only),
            x_hi, x_in, y_lo, y_in, d_lo, d_hi, name="relay_add",
        )
        x_hi_in, y_lo_in = cell(x_hi, bit=2), cell(y_lo, bit=4)
        w1_late, x_hi, x_lo_in, y_hi_in = after((w1, x_hi, x_lo_in, y_hi_in))
        (own,) = second(((Later(w1_late), on_mine[0], v_other[0]),), rows, low2, ((False,),))
        base, w1_late, w2t = plain(
            early_sum, tuple(jax.ShapeDtypeStruct(*x) for x in (((rows, k1), F32), (w1.shape, BF16), (w2t.shape, F32))),
            own, x_lo_in, y_hi_in, w1, w2t, name="early_sum",
        )
        w1_new, w2_new = plain(
            last_update, (jax.ShapeDtypeStruct((rows, k1), BF16), jax.ShapeDtypeStruct((k2, k1), F32)),
            base, x_hi_in, y_lo_in, x_sums, y_sums, w1_late, w2t, name="last_update",
        )
        w2_new = w2_new.T
    else:
        found = []
        for i in range(0, chips, each):
            some = tuple((halves[0][j], v_mine[j], v_other[j]) for j in range(i, i + each))
            found += second(some, rows, low2, ((False,),) * each)
        w1_num = lax.psum_scatter(
            jnp.concatenate(found), "cell", scatter_dimension=0, tiled=True, axis_index_groups=groups
        )
        sums = lax.psum(sums, "cell")
        w2_new = (w2t * sums[:k2] / sums[k2 + 8, :k2, None]).T
        w1_new = (w1.astype(F32) * w1_num / sums[k2 : k2 + 1]).astype(BF16)
    return (w1_new, h1_new, w2_new, h2_new)


def solution(mesh):
    placed = (P("gene", "cell"), P(("gene", "cell"), None), P(None, "cell"), P(), P(None, "cell"))
    return jax.shard_map(
        functools.partial(on_device, mesh.shape["gene"], mesh.shape["cell"]),
        mesh=mesh,
        in_specs=placed,
        out_specs=(P(("gene", "cell"), None), P(None, "cell"), P(), P(None, "cell")),
        check_vma=False,
    )
```

```python
import functools

import jax
import jax.numpy as jnp
from jax import lax
from jax.experimental import pallas as pl
from jax.experimental.pallas import tpu as pltpu
from jax.sharding import PartitionSpec as P

F32 = jnp.float32
BF16 = jnp.bfloat16
PAD = 16
CHUNKS = 2


def params(mib=16):
    return pltpu.CompilerParams(vmem_limit_bytes=mib * 1024 * 1024)


def mm(a, b, dims):
    return lax.dot_general(a, b, ((dims[:1], dims[1:]), ((), ())), preferred_element_type=F32)


def power_of(x):
    return jnp.ceil(jnp.log2(jnp.maximum(x, 1e-30)))


def encode(x, out_ref, extra=None, singles=(), at=0):
    rows, cols = x.shape
    power = power_of(jnp.max(x, axis=0, keepdims=True))
    q = jnp.minimum(x * (jnp.exp2(-power) * 65535.0) + 0.5, 65535.0)
    out_ref[at : at + rows, :] = (q.astype(jnp.int32) - 32768).astype(jnp.int16)
    lines = [power]
    if extra is not None:
        whole = jnp.floor(extra)
        for y in (whole, jnp.floor((extra - whole) * 32768.0 + 0.25)):
            lines += [y[:, i : i + cols] for i in range(0, y.shape[1], cols)]
    for y in singles:
        own = power_of(y)
        y = y * (jnp.exp2(-own) * 32767.0)
        whole = jnp.floor(y)
        lines += [own, whole, jnp.floor((y - whole) * 32768.0)]
    lines.append(jnp.zeros((PAD - len(lines), cols), F32))
    out_ref[at + rows : at + rows + PAD, :] = jnp.concatenate(lines, axis=0).astype(jnp.int32).astype(jnp.int16)


def pad_rows(ref, end):
    return ref[end - PAD : end, :].astype(jnp.int32).astype(F32)


def decode_extra(ref, width):
    n = width // ref.shape[1]
    lines = pad_rows(ref, ref.shape[0])
    lines = [lines[1 + i : 2 + i] for i in range(2 * n)]
    return jnp.concatenate(lines[:n], axis=1) + jnp.concatenate(lines[n:], axis=1) * (1.0 / 32768.0)


def decode_singles(ref, n, end):
    lines = pad_rows(ref, end)
    found = []
    for i in range(1, 1 + 3 * n, 3):
        unit = jnp.exp2(lines[i : i + 1]) * (1.0 / 32767.0)
        found.append((lines[i + 1 : i + 2] + lines[i + 2 : i + 3] * (1.0 / 32768.0)) * unit)
    return found


def decode(ref, rows=None, at=0):
    rows = ref.shape[0] - PAD if rows is None else rows
    unit = jnp.exp2(pad_rows(ref, at + rows + PAD)[:1]) * (1.0 / 65535.0)
    return (ref[at : at + rows, :].astype(jnp.int32) + 32768).astype(F32) * unit


def coded(rows, cols):
    return jax.ShapeDtypeStruct((rows + PAD, cols), jnp.int16)


def quotient(v, approx):
    return (v.astype(jnp.int32).astype(F32) / approx).astype(BF16)


def counts_body(chips, rows, at, v, *refs):
    outs, held, low, sems = refs[: 2 * chips], *refs[2 * chips :]
    copies = []
    for q in range(chips):
        start = pl.multiple_of((at[0] ^ q) * 2 * rows, 2 * rows)
        both = pl.ds(q * 2 * rows, 2 * rows)
        copies.append(pltpu.make_async_copy(v.at[pl.ds(start, 2 * rows), :], held.at[both, :], sems.at[q]))
        copies[-1].start()
    for q in range(chips):
        copies[q].wait()
        for slot, core in ((q, at[1]), (chips + q, 1 - at[1])):
            some = held[pl.ds(pl.multiple_of((2 * q + core) * rows, rows), rows), :]
            low[slot] = some.astype(jnp.int16)
            copies.append(pltpu.make_async_copy(low.at[slot], outs[slot], sems.at[chips + slot]))
            copies[-1].start()
    for copy in copies[chips:]:
        copy.wait()


def split_counts(at, counts, chips, rows):
    cells = counts.shape[1]
    out = pltpu.HBM((rows, cells), jnp.int16)
    smem, hbm = pl.BlockSpec(memory_space=pltpu.SMEM), pl.BlockSpec(memory_space=pltpu.HBM)
    outs = pl.pallas_call(
        functools.partial(counts_body, chips, rows),
        out_shape=(out,) * (2 * chips),
        in_specs=[smem, hbm],
        out_specs=[hbm] * (2 * chips),
        scratch_shapes=[
            pltpu.VMEM(counts.shape, counts.dtype),
            pltpu.VMEM((2 * chips, rows, cells), jnp.int16),
            pltpu.SemaphoreType.DMA((3 * chips,)),
        ],
        compiler_params=params(),
        name="split_counts",
    )(at, pltpu.with_memory_space_constraint(counts, pltpu.HBM))
    return outs[:chips], outs[chips:]


class Later:
    def __init__(self, array):
        self.array = array


def fetching(refs, later, scratch):
    sems, slots, found = scratch[-1] if later else None, iter(scratch), []
    for i, ref in enumerate(refs):
        copy = None
        if i in later:
            slot = next(slots)
            copy = pltpu.make_async_copy(ref, slot, sems.at[later.index(i)])
            copy.start()
            ref = slot
        found.append((ref, copy))
    return found


def ready(operand):
    ref, copy = operand
    if copy is not None:
        copy.wait()
    return ref[...]


def joined(operands):
    return jnp.concatenate([ready(x) for x in operands], axis=0) if len(operands) > 1 else ready(operands[0])


def ahead(sources, outs, sems):
    copies = [pltpu.make_async_copy(x, out, sems.at[i]) for i, (x, out) in enumerate(zip(sources, outs))]
    for copy in copies:
        copy.start()
    return copies


def fetch_body(n, *refs):
    for copy in ahead(refs[:n], refs[n : 2 * n], refs[-1]):
        copy.wait()


def plain_fetch(arrays):
    n = len(arrays)
    vmem, hbm = pl.BlockSpec(memory_space=pltpu.VMEM), pl.BlockSpec(memory_space=pltpu.HBM)
    return pl.pallas_call(
        functools.partial(fetch_body, n),
        out_shape=[jax.ShapeDtypeStruct(x.shape, x.dtype) for x in arrays],
        in_specs=[hbm] * n,
        out_specs=[vmem] * n,
        scratch_shapes=[pltpu.SemaphoreType.DMA((n,))],
        compiler_params=params(),
        name="fetch",
    )(*(pltpu.with_memory_space_constraint(x, pltpu.HBM) for x in arrays))


def first_body(groups, later, n_ahead, has_acc, h, *refs):
    n, n_later = sum(groups) + len(groups), len(later)
    refs, sems = (refs[:-1], refs[-1:]) if n_ahead else (refs, ())
    refs, scratch = (refs[:-n_later - 1] + sems, refs[-n_later - 1 :]) if later else (refs + sems, ())
    operands = fetching(refs[:n], later, scratch)
    copies, refs = (), refs[n:]
    if n_ahead:
        copies, refs = ahead(refs[:n_ahead], refs[-1 - n_ahead : -1], refs[-1]), refs[n_ahead : -1 - n_ahead]
    num_ref, col_ref = refs[-2:]
    total, col = (refs[0][...], refs[1][...]) if has_acc else (0.0, 0.0)
    for n in groups:
        w, v = joined(operands[:n]), operands[n]
        operands = operands[n + 1 :]
        approx = mm(w, h[...], (1, 0))
        total += mm(w, quotient(ready(v), approx), (0, 0))
        col += jnp.sum(w.astype(F32), axis=0, keepdims=True)
    num_ref[...] = total
    col_ref[...] = jnp.broadcast_to(col, col_ref.shape)
    for copy in copies:
        copy.wait()


def second_body(groups, later, n_ahead, codes, ha, hb, *refs):
    n, n_later = sum(groups) + 2 * len(groups), len(later)
    refs, scratch = (refs[:-n_later - 1], refs[-n_later - 1 :]) if later else (refs, ())
    operands, outs = fetching(refs[:n], later, scratch), refs[n:]
    for n, code in zip(groups, codes):
        pieces, v, operands = operands[:n], operands[n : n + 2], operands[n + 2 :]
        w = joined(pieces)
        total = 0.0
        for h, some in ((hb, v[1]), (ha, v[0])):
            low = h[...]
            approx = mm(w, low, (1, 0))
            total += mm(quotient(ready(some), approx), low, (1, 1))
        t = w.shape[0] // len(code)
        for k, coding in enumerate(code):
            out, outs = outs[0], outs[1:]
            part = total[k * t : (k + 1) * t]
            if coding:
                encode(part, out)
            else:
                out[...] = part


def products(body, flag, outs, groups, h, acc, name, fetch=()):
    n_h = len(h)
    sizes = tuple(len(g) - n_h for g in groups)
    flat = [x for g in groups for x in g]
    later = tuple(i for i, x in enumerate(flat) if isinstance(x, Later))
    vmem, hbm = pl.BlockSpec(memory_space=pltpu.VMEM), pl.BlockSpec(memory_space=pltpu.HBM)
    specs = [hbm if i in later else vmem for i in range(len(flat))]
    flat = [pltpu.with_memory_space_constraint(x.array, pltpu.HBM) if isinstance(x, Later) else x for x in flat]
    scratch = [pltpu.VMEM(flat[i].shape, flat[i].dtype) for i in later]
    if later:
        scratch.append(pltpu.SemaphoreType.DMA((len(later),)))
    fetch = [pltpu.with_memory_space_constraint(x, pltpu.HBM) for x in fetch]
    if fetch:
        scratch.append(pltpu.SemaphoreType.DMA((len(fetch),)))
    outs = (*outs, *(jax.ShapeDtypeStruct(x.shape, x.dtype) for x in fetch))
    args = [*h, *flat, *fetch, *acc]
    work = 2 * sum(x.shape[0] for x in flat) * h[0].shape[1]
    return pl.pallas_call(
        functools.partial(body, sizes, later, len(fetch), flag),
        out_shape=outs,
        in_specs=[vmem] * n_h + specs + [hbm] * len(fetch) + [vmem] * len(acc),
        out_specs=[vmem] * len(outs),
        scratch_shapes=scratch,
        input_output_aliases={len(args) - len(acc) + i: i for i in range(len(acc))},
        compiler_params=params(),
        cost_estimate=pl.CostEstimate(flops=2 * work * h[0].shape[0], bytes_accessed=work, transcendentals=0),
        name=name,
    )(*args)


def first(groups, h, acc=(), fetch=()):
    k1, cells = h.shape
    outs = (jax.ShapeDtypeStruct((k1, cells), F32), jax.ShapeDtypeStruct((8, k1), F32))
    return products(first_body, bool(acc), outs, groups, (h,), acc, "first_products", fetch)


def second(groups, rows, h, codes):
    k1 = h[0].shape[0]
    outs = []
    for code in codes:
        t = rows // len(code)
        outs += [coded(t, k1) if c else jax.ShapeDtypeStruct((t, k1), F32) for c in code]
    return products(second_body, codes, tuple(outs), groups, h, (), "second_products")


def plain(body, outs, *args, name, flag=None):
    vmem = pl.BlockSpec(memory_space=pltpu.VMEM)
    specs = [vmem] * len(args)
    if flag is not None:
        specs, args = [pl.BlockSpec(memory_space=pltpu.SMEM)] + specs, (flag, *args)
    out_specs = (vmem,) * len(outs) if isinstance(outs, tuple) else vmem
    return pl.pallas_call(
        body, out_shape=outs, in_specs=specs, out_specs=out_specs, compiler_params=params(), name=name
    )(*args)


def flip(x, axis, size, bit):
    return lax.ppermute(x, axis, [(i, i ^ bit) for i in range(size)])


def split_num(flag, num, col, keep_ref, *sends):
    inner = flag[0] == 1
    half = num.shape[1] // 2
    keep_ref[...] = jnp.where(inner, num[:, half:], num[:, :half])
    width = half // len(sends)
    for i, send in enumerate(sends):
        lo = num[:, i * width : (i + 1) * width]
        hi = num[:, half + i * width : half + (i + 1) * width]
        encode(jnp.where(inner, lo, hi), send, None if i else col[:1, :])


def add_kept(i, keep, other, *refs):
    width, k1 = other.shape[1], keep.shape[0]
    extra = None if i else decode_extra(refs[0], k1) + decode_extra(other, k1)
    encode(keep[:, i * width : (i + 1) * width] + decode(other), refs[-1], extra)


def add_coded(one, other, out_ref, *col_ref):
    encode(decode(one) + decode(other), out_ref)
    for ref in col_ref:
        k1 = ref.shape[1]
        ref[...] = jnp.broadcast_to(decode_extra(one, k1) + decode_extra(other, k1), ref.shape)


def h1_update(n, flag, *refs):
    mine, theirs, (h1_ref, col_ref, low_ref, late_ref) = refs[:n], refs[n : 2 * n], refs[2 * n :]
    inner = flag[0] == 1
    half = h1_ref.shape[1] // 2
    width = half // n
    col = col_ref[...].T[:, :1]
    for i in range(n):
        a, b = decode(mine[i]), decode(theirs[i])
        for at, num in ((i * width, jnp.where(inner, b, a)), (half + i * width, jnp.where(inner, a, b))):
            new = h1_ref[:, at : at + width] * num / col
            late_ref[:, at : at + width] = new
            low_ref[:, at : at + width] = new.astype(BF16)


def h1_update_plain(num, h1_ref, col_ref, new_ref, low_ref):
    new = h1_ref[...] * num[...] / col_ref[:, :1]
    new_ref[...] = new
    low_ref[...] = new.astype(BF16)


def cut_halves(a_ref, b_ref, lo_ref, hi_ref):
    t = lo_ref.shape[0]
    lo_ref[...] = a_ref[:t, :]
    hi_ref[...] = b_ref[t:, :]


def pack(k2, lo, hi, sums, sums_in, lo_ref, hi_ref):
    total = sums[...] + sums_in[...]
    t, half = lo.shape[0], k2 // 2
    encode(lo[...], lo_ref)
    encode(total[:half], lo_ref, singles=(total[k2 : k2 + 1], total[k2 + 8 : k2 + 9]), at=t + PAD)
    encode(hi[...], hi_ref)
    encode(total[half:k2], hi_ref, at=t + PAD)


def relay_add(k2, x, x_in, y, y_in, lo, hi, x_ref, y_ref, x_sums, y_sums):
    rows = x.shape[0]
    at, few = rows + PAD, k2 // 2
    encode(x[...] + decode(x_in, rows), x_ref)
    encode(y[...] + decode(y_in, rows), y_ref)
    one = [a + b for a, b in zip(decode_singles(lo, 2, lo.shape[0]), decode_singles(y_in, 2, lo.shape[0]))]
    encode(decode(lo, few, at) + decode(y_in, few, at), y_sums, singles=one)
    encode(decode(hi, few, at) + decode(x_in, few, at), x_sums)
    x_ref[at:, :] = x_sums[...]
    y_ref[at:, :] = y_sums[...]


def early_sum(own, x_lo, y_hi, w_ref, w2t_ref, out_ref, w_out, w2t_out):
    w_out[...], w2t_out[...] = w_ref[...], w2t_ref[...]
    t = x_lo.shape[0] - PAD
    out_ref[:t, :] = own[:t, :] + decode(x_lo)
    out_ref[t:, :] = own[t:, :] + decode(y_hi)


def last_update(base, x_hi, y_lo, x_sums, y_sums, w_ref, w2t_ref, w1_ref, w2_ref):
    t, few = base.shape[0] // 2, x_sums.shape[0] - PAD
    singles = zip(decode_singles(y_sums, 2, few + PAD), decode_singles(y_lo, 2, y_lo.shape[0]))
    row, h2_row = [a + b for a, b in singles]
    for at, late in ((0, y_lo), (t, x_hi)):
        rows = slice(at, at + t)
        total = base[rows, :] + decode(late, t)
        w1_ref[rows, :] = (w_ref[rows, :].astype(F32) * total / row).astype(BF16)
    h2_col = jnp.broadcast_to(h2_row, (8, h2_row.shape[1])).T[: 2 * few, :1]
    low = decode(y_sums, few) + decode(y_lo, few, t + PAD)
    high = decode(x_sums, few) + decode(x_hi, few, t + PAD)
    w2_ref[...] = w2t_ref[...] * jnp.concatenate([low, high], axis=0) / h2_col


def parts(x):
    hi = x.astype(BF16)
    return hi, (x - hi.astype(F32)).astype(BF16)


def mm3(a, b, dims):
    (ah, al), (bh, bl) = a, b
    if ah.shape[dims[0]] <= 64:
        one, other = (jnp.concatenate(x, axis=d) for x, d in (((ah, ah, al), dims[0]), ((bh, bl, bh), dims[1])))
        return mm(one, other, dims)
    m = ah.shape[1 - dims[0]]
    if m <= 64:
        both = mm(jnp.concatenate((ah, al), axis=1 - dims[0]), bh, dims)
        return both[:m] + (both[m:] + mm(ah, bl, dims))
    return mm(ah, bh, dims) + (mm(ah, bl, dims) + mm(al, bh, dims))


def layer_two(n_ahead, h1_ref, w2t_ref, h2_ref, *refs):
    new_ref, sums_ref = refs[n_ahead : n_ahead + 2]
    copies = ahead((*refs[:n_ahead], h1_ref), refs[n_ahead + 2 : -1], refs[-1])
    h1, w2t, h2 = h1_ref[...], w2t_ref[...], h2_ref[...]
    k2, k1 = w2t.shape
    w2p = parts(w2t)
    ratio3 = h1 / mm3(w2p, parts(h2), (0, 0))
    h2_new = h2 * mm3(w2p, parts(ratio3), (1, 0)) / jnp.sum(w2t, axis=1, keepdims=True)
    new_ref[...] = h2_new
    h2p = parts(h2_new)
    ratio4 = h1 / mm3(w2p, h2p, (0, 0))
    sums_ref[:k2, :] = mm3(h2p, parts(ratio4), (1, 1))
    cells = h1.shape[1]
    row = jnp.ones((8, cells), BF16)
    sums_ref[k2 : k2 + 8, :] = sum(mm(row, x, (1, 1)) for x in parts(h1))
    sums_ref[k2 + 8 :, :] = jnp.zeros((8, k1), F32)
    sums_ref[k2 + 8 :, :k2] = sum(mm(row, x, (1, 1)) for x in h2p)
    for copy in copies:
        copy.wait()


def on_device(n_gene, n_cell, counts, w1, h1, w2, h2):
    genes, cells = counts.shape
    rows, k1 = w1.shape
    k2 = w2.shape[1]
    chips = n_cell // 2
    me = lax.axis_index("cell")
    core, chip = me % 2, me // 2
    line = n_cell == 8 and n_gene == 4 and genes * 4 < 32768
    cell = functools.partial(flip, axis="cell", size=n_cell)
    gene = functools.partial(flip, axis="gene", size=n_gene)
    after = lax.optimization_barrier
    at = jnp.stack([chip, core]).astype(jnp.int32)

    h1_low = h1.astype(BF16)
    new_shapes = (jax.ShapeDtypeStruct((k1, cells), F32), jax.ShapeDtypeStruct((k1, cells), BF16))
    if line:
        t = rows // 2
        w_x, w_y = cell(w1, bit=2), cell(w1, bit=4)
        w_0 = cell(w1, bit=1)

        v_mine, v_theirs = split_counts(at, counts, chips, rows)
        v_other = [cell(v, bit=1) for v in v_theirs]
        on_mine, on_theirs = ([Later(v) for v in some] for some in (v_mine, v_theirs))
        acc = first(((Later(w1), on_mine[0]), (w_0, on_theirs[0])), h1_low)
        w_x, w_y, *acc = after((w_x, w_y, *acc))
        half = jax.ShapeDtypeStruct((t, k1), BF16)
        y_lo, x_hi = plain(cut_halves, (half, half), w_y, w_x, name="cut_halves")
        d_lo, d_hi = cell(y_lo, bit=2), cell(x_hi, bit=4)
        x_0, y_0 = cell(w_x, bit=1), cell(w_y, bit=1)
        near = ((w_x, on_mine[1]), (w_y, on_mine[2]), (x_0, on_theirs[1]), (y_0, on_theirs[2]))
        acc = first(near, h1_low, acc)
        d_lo, d_hi, *acc = after((d_lo, d_hi, *acc))
        far = [Later(cell(d, bit=1)) for d in (d_lo, d_hi)]
        *v_far, own_lo, own_hi = plain_fetch(after((v_mine[3], v_theirs[3], d_lo, d_hi, *acc))[:4])
        num, col = first(((own_lo, own_hi, v_far[0]), (*far, v_far[1])), h1_low, acc)

        z = lax.axis_index("gene")
        inner = jnp.where((z == 1) | (z == 2), 1, 0).astype(jnp.int32)[None]
        chunks = tuple(range(CHUNKS))
        piece = coded(k1, cells // 2 // CHUNKS)
        keep, *sent = plain(
            split_num, (jax.ShapeDtypeStruct((k1, cells // 2), F32),) + (piece,) * CHUNKS,
            num, col, flag=inner, name="split_num",
        )

        pair = []
        for i, x in enumerate(sent):
            got = gene(x, bit=1)
            extra = () if i else (x,)
            pair.append(plain(functools.partial(add_kept, i), piece, keep, got, *extra, name="add_pair"))
        mine = []
        for i, x in enumerate(pair):
            outs = piece if i else (piece, jax.ShapeDtypeStruct((8, k1), F32))
            mine.append(plain(add_coded, outs, x, gene(x, bit=3), name="add_cross"))
        (first_mine, col), *mine = mine
        mine = [first_mine, *mine]
        theirs = [gene(x, bit=1) for x in mine]
        h1_low2, h1_late = plain(
            functools.partial(h1_update, CHUNKS), new_shapes[::-1], *mine, *theirs, h1, col,
            flag=inner, name="h1_update",
        )
        h1_low2_other = cell(h1_low2, bit=1)
    else:
        col = None
        groups = [list(range(c, n_cell, 2)) for c in (0, 1)]
        w_half = lax.all_gather(w1, "cell", axis=0, tiled=True, axis_index_groups=groups)
        v_mine, v_theirs = split_counts(at * jnp.array([0, 1], jnp.int32), counts, chips, rows)
        v_other = [cell(v, bit=1) for v in v_theirs]
        halves = [[w[j * rows : (j + 1) * rows] for j in range(chips)] for w in (w_half, cell(w_half, bit=1))]
        each = min(chips, max(1, 512 // rows))
        acc = ()
        for i in range(0, chips, each):
            for w, v in zip(halves, (v_mine, v_theirs)):
                acc = first(tuple((w[j], v[j]) for j in range(i, i + each)), h1_low, acc)
        num, col = lax.psum(tuple(acc), "gene")
        col = jnp.broadcast_to(col[0][:, None], (k1, 128))
        h1_new, h1_low2 = plain(h1_update_plain, new_shapes, num, h1, col, name="h1_update")
        h1_low2_other, h1_late = cell(h1_low2, bit=1), h1_new

    w2t = w2.T
    vmem, hbm = pl.BlockSpec(memory_space=pltpu.VMEM), pl.BlockSpec(memory_space=pltpu.HBM)
    soon = [pltpu.with_memory_space_constraint(x, pltpu.HBM) for x in ((v_mine[3], d_lo, d_hi) if line else v_mine[:1])]
    h2_new, sums, *soon, h1_new = pl.pallas_call(
        functools.partial(layer_two, len(soon)),
        out_shape=(
            jax.ShapeDtypeStruct((k2, cells), F32),
            jax.ShapeDtypeStruct((k2 + 16, k1), F32),
            *(jax.ShapeDtypeStruct(x.shape, x.dtype) for x in soon),
            pltpu.HBM(h1.shape, F32),
        ),
        in_specs=[vmem] * 3 + [hbm] * len(soon),
        out_specs=[vmem] * (2 + len(soon)) + [hbm],
        scratch_shapes=[pltpu.SemaphoreType.DMA((len(soon) + 1,))],
        compiler_params=params(),
        name="layer_two",
    )(h1_late, w2t, h2, *soon)
    low2 = (h1_low2, h1_low2_other)
    if line:
        sums_in = cell(sums, bit=1)
        v_far, d_lo, d_hi = soon
        d_lo, d_hi = second(((d_lo, d_hi, v_far, v_other[3]),), rows, low2, ((False, False),))
        sums, sums_in, d_lo = after((sums, sums_in, d_lo))
        few = k2 // 2 + PAD
        with_sums = coded(t + few, k1)
        d_lo, d_hi = plain(
            functools.partial(pack, k2), (with_sums, with_sums), d_lo, d_hi, sums, sums_in, name="pack"
        )
        y_in, x_in = cell(d_lo, bit=2), cell(d_hi, bit=4)
        w_x, d_lo = after((w_x, d_lo))
        near = ((Later(w_x), on_mine[1], v_other[1]), (Later(w_y), on_mine[2], v_other[2]))
        x_lo, x_hi, y_lo, y_hi = second(near, rows, low2, ((True, False), (False, True)))
        x_lo_in, y_hi_in = cell(x_lo, bit=2), cell(y_hi, bit=4)
        sums_only = jax.ShapeDtypeStruct((few, k1), jnp.int16)
        x_hi, y_lo, x_sums, y_sums = plain(
            functools.partial(relay_add, k2), (with_sums, with_sums, sums_only, sums_only),
            x_hi, x_in, y_lo, y_in, d_lo, d_hi, name="relay_add",
        )
        x_hi_in, y_lo_in = cell(x_hi, bit=2), cell(y_lo, bit=4)
        w1_late, x_hi, x_lo_in, y_hi_in = after((w1, x_hi, x_lo_in, y_hi_in))
        (own,) = second(((Later(w1_late), on_mine[0], v_other[0]),), rows, low2, ((False,),))
        base, w1_late, w2t = plain(
            early_sum, tuple(jax.ShapeDtypeStruct(*x) for x in (((rows, k1), F32), (w1.shape, BF16), (w2t.shape, F32))),
            own, x_lo_in, y_hi_in, w1, w2t, name="early_sum",
        )
        w1_new, w2_new = plain(
            last_update, (jax.ShapeDtypeStruct((rows, k1), BF16), jax.ShapeDtypeStruct((k2, k1), F32)),
            base, x_hi_in, y_lo_in, x_sums, y_sums, w1_late, w2t, name="last_update",
        )
        w2_new = w2_new.T
    else:
        found = []
        for i in range(0, chips, each):
            some = tuple((halves[0][j], v_mine[j], v_other[j]) for j in range(i, i + each))
            found += second(some, rows, low2, ((False,),) * each)
        w1_num = lax.psum_scatter(
            jnp.concatenate(found), "cell", scatter_dimension=0, tiled=True, axis_index_groups=groups
        )
        sums = lax.psum(sums, "cell")
        w2_new = (w2t * sums[:k2] / sums[k2 + 8, :k2, None]).T
        w1_new = (w1.astype(F32) * w1_num / sums[k2 : k2 + 1]).astype(BF16)
    return (w1_new, h1_new, w2_new, h2_new)


def solution(mesh):
    placed = (P("gene", "cell"), P(("gene", "cell"), None), P(None, "cell"), P(), P(None, "cell"))
    return jax.shard_map(
        functools.partial(on_device, mesh.shape["gene"], mesh.shape["cell"]),
        mesh=mesh,
        in_specs=placed,
        out_specs=(P(("gene", "cell"), None), P(None, "cell"), P(), P(None, "cell")),
        check_vma=False,
    )
```

```python
import functools

import jax
import jax.numpy as jnp
from jax import lax
from jax.experimental import pallas as pl
from jax.experimental.pallas import tpu as pltpu
from jax.sharding import PartitionSpec as P

F32 = jnp.float32
BF16 = jnp.bfloat16
PAD = 16
CHUNKS = 2


def params(mib=16):
    return pltpu.CompilerParams(vmem_limit_bytes=mib * 1024 * 1024)


def mm(a, b, dims):
    return lax.dot_general(a, b, ((dims[:1], dims[1:]), ((), ())), preferred_element_type=F32)


def power_of(x):
    return jnp.ceil(jnp.log2(jnp.maximum(x, 1e-30)))


def encode(x, out_ref, extra=None, singles=(), at=0):
    rows, cols = x.shape
    power = power_of(jnp.max(x, axis=0, keepdims=True))
    q = jnp.minimum(x * (jnp.exp2(-power) * 65535.0) + 0.5, 65535.0)
    out_ref[at : at + rows, :] = (q.astype(jnp.int32) - 32768).astype(jnp.int16)
    lines = [power]
    if extra is not None:
        whole = jnp.floor(extra)
        for y in (whole, jnp.floor((extra - whole) * 32768.0 + 0.25)):
            lines += [y[:, i : i + cols] for i in range(0, y.shape[1], cols)]
    for y in singles:
        own = power_of(y)
        y = y * (jnp.exp2(-own) * 32767.0)
        whole = jnp.floor(y)
        lines += [own, whole, jnp.floor((y - whole) * 32768.0)]
    lines.append(jnp.zeros((PAD - len(lines), cols), F32))
    out_ref[at + rows : at + rows + PAD, :] = jnp.concatenate(lines, axis=0).astype(jnp.int32).astype(jnp.int16)


def pad_rows(ref, end):
    return ref[end - PAD : end, :].astype(jnp.int32).astype(F32)


def decode_extra(ref, width):
    n = width // ref.shape[1]
    lines = pad_rows(ref, ref.shape[0])
    lines = [lines[1 + i : 2 + i] for i in range(2 * n)]
    return jnp.concatenate(lines[:n], axis=1) + jnp.concatenate(lines[n:], axis=1) * (1.0 / 32768.0)


def decode_singles(ref, n, end):
    lines = pad_rows(ref, end)
    found = []
    for i in range(1, 1 + 3 * n, 3):
        unit = jnp.exp2(lines[i : i + 1]) * (1.0 / 32767.0)
        found.append((lines[i + 1 : i + 2] + lines[i + 2 : i + 3] * (1.0 / 32768.0)) * unit)
    return found


def decode(ref, rows=None, at=0):
    rows = ref.shape[0] - PAD if rows is None else rows
    unit = jnp.exp2(pad_rows(ref, at + rows + PAD)[:1]) * (1.0 / 65535.0)
    return (ref[at : at + rows, :].astype(jnp.int32) + 32768).astype(F32) * unit


def coded(rows, cols):
    return jax.ShapeDtypeStruct((rows + PAD, cols), jnp.int16)


def quotient(v, approx):
    return (v.astype(jnp.int32).astype(F32) / approx).astype(BF16)


def counts_body(chips, rows, at, v, *refs):
    outs, held, low, sems = refs[: 2 * chips], *refs[2 * chips :]
    copies = []
    for q in range(chips):
        start = pl.multiple_of((at[0] ^ q) * 2 * rows, 2 * rows)
        both = pl.ds(q * 2 * rows, 2 * rows)
        copies.append(pltpu.make_async_copy(v.at[pl.ds(start, 2 * rows), :], held.at[both, :], sems.at[q]))
        copies[-1].start()
    for q in range(chips):
        copies[q].wait()
        for slot, core in ((q, at[1]), (chips + q, 1 - at[1])):
            some = held[pl.ds(pl.multiple_of((2 * q + core) * rows, rows), rows), :]
            low[slot] = some.astype(jnp.int16)
            copies.append(pltpu.make_async_copy(low.at[slot], outs[slot], sems.at[chips + slot]))
            copies[-1].start()
    for copy in copies[chips:]:
        copy.wait()


def split_counts(at, counts, chips, rows):
    cells = counts.shape[1]
    out = pltpu.HBM((rows, cells), jnp.int16)
    smem, hbm = pl.BlockSpec(memory_space=pltpu.SMEM), pl.BlockSpec(memory_space=pltpu.HBM)
    outs = pl.pallas_call(
        functools.partial(counts_body, chips, rows),
        out_shape=(out,) * (2 * chips),
        in_specs=[smem, hbm],
        out_specs=[hbm] * (2 * chips),
        scratch_shapes=[
            pltpu.VMEM(counts.shape, counts.dtype),
            pltpu.VMEM((2 * chips, rows, cells), jnp.int16),
            pltpu.SemaphoreType.DMA((3 * chips,)),
        ],
        compiler_params=params(),
        name="split_counts",
    )(at, pltpu.with_memory_space_constraint(counts, pltpu.HBM))
    return outs[:chips], outs[chips:]


class Later:
    def __init__(self, array):
        self.array = array


def fetching(refs, later, scratch):
    sems, slots, found = scratch[-1] if later else None, iter(scratch), []
    for i, ref in enumerate(refs):
        copy = None
        if i in later:
            slot = next(slots)
            copy = pltpu.make_async_copy(ref, slot, sems.at[later.index(i)])
            copy.start()
            ref = slot
        found.append((ref, copy))
    return found


def ready(operand):
    ref, copy = operand
    if copy is not None:
        copy.wait()
    return ref[...]


def joined(operands):
    return jnp.concatenate([ready(x) for x in operands], axis=0) if len(operands) > 1 else ready(operands[0])


def ahead(sources, outs, sems):
    copies = [pltpu.make_async_copy(x, out, sems.at[i]) for i, (x, out) in enumerate(zip(sources, outs))]
    for copy in copies:
        copy.start()
    return copies


def fetch_body(n, *refs):
    for copy in ahead(refs[:n], refs[n : 2 * n], refs[-1]):
        copy.wait()


def plain_fetch(arrays):
    n = len(arrays)
    vmem, hbm = pl.BlockSpec(memory_space=pltpu.VMEM), pl.BlockSpec(memory_space=pltpu.HBM)
    return pl.pallas_call(
        functools.partial(fetch_body, n),
        out_shape=[jax.ShapeDtypeStruct(x.shape, x.dtype) for x in arrays],
        in_specs=[hbm] * n,
        out_specs=[vmem] * n,
        scratch_shapes=[pltpu.SemaphoreType.DMA((n,))],
        compiler_params=params(),
        name="fetch",
    )(*(pltpu.with_memory_space_constraint(x, pltpu.HBM) for x in arrays))


def first_body(groups, later, n_ahead, has_acc, h, *refs):
    n, n_later = sum(groups) + len(groups), len(later)
    refs, sems = (refs[:-1], refs[-1:]) if n_ahead else (refs, ())
    refs, scratch = (refs[:-n_later - 1] + sems, refs[-n_later - 1 :]) if later else (refs + sems, ())
    operands = fetching(refs[:n], later, scratch)
    copies, refs = (), refs[n:]
    if n_ahead:
        copies, refs = ahead(refs[:n_ahead], refs[-1 - n_ahead : -1], refs[-1]), refs[n_ahead : -1 - n_ahead]
    num_ref, col_ref = refs[-2:]
    total, col = (refs[0][...], refs[1][...]) if has_acc else (0.0, 0.0)
    for n in groups:
        w, v = joined(operands[:n]), operands[n]
        operands = operands[n + 1 :]
        approx = mm(w, h[...], (1, 0))
        total += mm(w, quotient(ready(v), approx), (0, 0))
        col += jnp.sum(w.astype(F32), axis=0, keepdims=True)
    num_ref[...] = total
    col_ref[...] = jnp.broadcast_to(col, col_ref.shape)
    for copy in copies:
        copy.wait()


def second_body(groups, later, n_ahead, codes, ha, hb, *refs):
    n, n_later = sum(groups) + 2 * len(groups), len(later)
    refs, scratch = (refs[:-n_later - 1], refs[-n_later - 1 :]) if later else (refs, ())
    operands, outs = fetching(refs[:n], later, scratch), refs[n:]
    for n, code in zip(groups, codes):
        pieces, v, operands = operands[:n], operands[n : n + 2], operands[n + 2 :]
        w = joined(pieces)
        total = 0.0
        for h, some in ((hb, v[1]), (ha, v[0])):
            low = h[...]
            approx = mm(w, low, (1, 0))
            total += mm(quotient(ready(some), approx), low, (1, 1))
        t = w.shape[0] // len(code)
        for k, coding in enumerate(code):
            out, outs = outs[0], outs[1:]
            part = total[k * t : (k + 1) * t]
            if coding:
                encode(part, out)
            else:
                out[...] = part


def products(body, flag, outs, groups, h, acc, name, fetch=()):
    n_h = len(h)
    sizes = tuple(len(g) - n_h for g in groups)
    flat = [x for g in groups for x in g]
    later = tuple(i for i, x in enumerate(flat) if isinstance(x, Later))
    vmem, hbm = pl.BlockSpec(memory_space=pltpu.VMEM), pl.BlockSpec(memory_space=pltpu.HBM)
    specs = [hbm if i in later else vmem for i in range(len(flat))]
    flat = [pltpu.with_memory_space_constraint(x.array, pltpu.HBM) if isinstance(x, Later) else x for x in flat]
    scratch = [pltpu.VMEM(flat[i].shape, flat[i].dtype) for i in later]
    if later:
        scratch.append(pltpu.SemaphoreType.DMA((len(later),)))
    fetch = [pltpu.with_memory_space_constraint(x, pltpu.HBM) for x in fetch]
    if fetch:
        scratch.append(pltpu.SemaphoreType.DMA((len(fetch),)))
    outs = (*outs, *(jax.ShapeDtypeStruct(x.shape, x.dtype) for x in fetch))
    args = [*h, *flat, *fetch, *acc]
    work = 2 * sum(x.shape[0] for x in flat) * h[0].shape[1]
    return pl.pallas_call(
        functools.partial(body, sizes, later, len(fetch), flag),
        out_shape=outs,
        in_specs=[vmem] * n_h + specs + [hbm] * len(fetch) + [vmem] * len(acc),
        out_specs=[vmem] * len(outs),
        scratch_shapes=scratch,
        input_output_aliases={len(args) - len(acc) + i: i for i in range(len(acc))},
        compiler_params=params(),
        cost_estimate=pl.CostEstimate(flops=2 * work * h[0].shape[0], bytes_accessed=work, transcendentals=0),
        name=name,
    )(*args)


def first(groups, h, acc=(), fetch=()):
    k1, cells = h.shape
    outs = (jax.ShapeDtypeStruct((k1, cells), F32), jax.ShapeDtypeStruct((8, k1), F32))
    return products(first_body, bool(acc), outs, groups, (h,), acc, "first_products", fetch)


def second(groups, rows, h, codes):
    k1 = h[0].shape[0]
    outs = []
    for code in codes:
        t = rows // len(code)
        outs += [coded(t, k1) if c else jax.ShapeDtypeStruct((t, k1), F32) for c in code]
    return products(second_body, codes, tuple(outs), groups, h, (), "second_products")


def plain(body, outs, *args, name, flag=None):
    vmem = pl.BlockSpec(memory_space=pltpu.VMEM)
    specs = [vmem] * len(args)
    if flag is not None:
        specs, args = [pl.BlockSpec(memory_space=pltpu.SMEM)] + specs, (flag, *args)
    out_specs = (vmem,) * len(outs) if isinstance(outs, tuple) else vmem
    return pl.pallas_call(
        body, out_shape=outs, in_specs=specs, out_specs=out_specs, compiler_params=params(), name=name
    )(*args)


def flip(x, axis, size, bit):
    return lax.ppermute(x, axis, [(i, i ^ bit) for i in range(size)])


def split_num(flag, num, col, keep_ref, *sends):
    inner = flag[0] == 1
    half = num.shape[1] // 2
    keep_ref[...] = jnp.where(inner, num[:, half:], num[:, :half])
    width = half // len(sends)
    for i, send in enumerate(sends):
        lo = num[:, i * width : (i + 1) * width]
        hi = num[:, half + i * width : half + (i + 1) * width]
        encode(jnp.where(inner, lo, hi), send, None if i else col[:1, :])


def first_and_split(groups, h, acc, flag, outs):
    sizes = tuple(len(g) - 1 for g in groups)
    flat = [x for g in groups for x in g]
    later = tuple(i for i, x in enumerate(flat) if isinstance(x, Later))
    n, n_outs, n_later = len(flat), len(outs), len(later)
    flat = [pltpu.with_memory_space_constraint(x.array, pltpu.HBM) if isinstance(x, Later) else x for x in flat]
    vmem, hbm = pl.BlockSpec(memory_space=pltpu.VMEM), pl.BlockSpec(memory_space=pltpu.HBM)

    def body(flag_ref, h_ref, *refs):
        inputs, out_refs, scratch = refs[: n + 2], refs[n + 2 : n + 2 + n_outs], refs[n + 2 + n_outs :]
        num, col = scratch[-2:]
        first_body(sizes, later, 0, True, h_ref, *inputs, num, col, *scratch[:-2])
        split_num(flag_ref, num, col, *out_refs)

    scratch = [pltpu.VMEM(flat[i].shape, flat[i].dtype) for i in later]
    if later:
        scratch.append(pltpu.SemaphoreType.DMA((n_later,)))
    return pl.pallas_call(
        body,
        out_shape=outs,
        in_specs=[pl.BlockSpec(memory_space=pltpu.SMEM), vmem] + [hbm if i in later else vmem for i in range(n)] + [vmem] * 2,
        out_specs=[vmem] * n_outs,
        scratch_shapes=scratch + [pltpu.VMEM(x.shape, x.dtype) for x in acc],
        compiler_params=params(),
        cost_estimate=pl.CostEstimate(
            flops=8 * flat[0].shape[0] * h.shape[0] * h.shape[1], bytes_accessed=4 * h.size, transcendentals=0
        ),
        name="first_and_split",
    )(flag, h, *flat, *acc)


def add_kept(i, keep, other, *refs):
    width, k1 = other.shape[1], keep.shape[0]
    extra = None if i else decode_extra(refs[0], k1) + decode_extra(other, k1)
    encode(keep[:, i * width : (i + 1) * width] + decode(other), refs[-1], extra)


def add_coded(one, other, out_ref, *col_ref):
    encode(decode(one) + decode(other), out_ref)
    for ref in col_ref:
        k1 = ref.shape[1]
        ref[...] = jnp.broadcast_to(decode_extra(one, k1) + decode_extra(other, k1), ref.shape)


def h1_update(n, flag, *refs):
    mine, theirs, (h1_ref, col_ref, low_ref, late_ref) = refs[:n], refs[n : 2 * n], refs[2 * n :]
    inner = flag[0] == 1
    half = h1_ref.shape[1] // 2
    width = half // n
    col = col_ref[...].T[:, :1]
    for i in range(n):
        a, b = decode(mine[i]), decode(theirs[i])
        for at, num in ((i * width, jnp.where(inner, b, a)), (half + i * width, jnp.where(inner, a, b))):
            new = h1_ref[:, at : at + width] * num / col
            late_ref[:, at : at + width] = new
            low_ref[:, at : at + width] = new.astype(BF16)


def h1_update_plain(num, h1_ref, col_ref, new_ref, low_ref):
    new = h1_ref[...] * num[...] / col_ref[:, :1]
    new_ref[...] = new
    low_ref[...] = new.astype(BF16)


def cut_halves(a_ref, b_ref, lo_ref, hi_ref):
    t = lo_ref.shape[0]
    lo_ref[...] = a_ref[:t, :]
    hi_ref[...] = b_ref[t:, :]


def pack(k2, lo, hi, sums, sums_in, lo_ref, hi_ref):
    total = sums[...] + sums_in[...]
    t, half = lo.shape[0], k2 // 2
    encode(lo[...], lo_ref)
    encode(total[:half], lo_ref, singles=(total[k2 : k2 + 1], total[k2 + 8 : k2 + 9]), at=t + PAD)
    encode(hi[...], hi_ref)
    encode(total[half:k2], hi_ref, at=t + PAD)


def relay_add(k2, x, x_in, y, y_in, lo, hi, x_ref, y_ref, x_sums, y_sums):
    rows = x.shape[0]
    at, few = rows + PAD, k2 // 2
    encode(x[...] + decode(x_in, rows), x_ref)
    encode(y[...] + decode(y_in, rows), y_ref)
    one = [a + b for a, b in zip(decode_singles(lo, 2, lo.shape[0]), decode_singles(y_in, 2, lo.shape[0]))]
    encode(decode(lo, few, at) + decode(y_in, few, at), y_sums, singles=one)
    encode(decode(hi, few, at) + decode(x_in, few, at), x_sums)
    x_ref[at:, :] = x_sums[...]
    y_ref[at:, :] = y_sums[...]


def early_sum(own, x_lo, y_hi, w_ref, w2t_ref, out_ref, w_out, w2t_out):
    w_out[...], w2t_out[...] = w_ref[...], w2t_ref[...]
    t = x_lo.shape[0] - PAD
    out_ref[:t, :] = own[:t, :] + decode(x_lo)
    out_ref[t:, :] = own[t:, :] + decode(y_hi)


def last_update(base, x_hi, y_lo, x_sums, y_sums, w_ref, w2t_ref, w1_ref, w2_ref):
    t, few = base.shape[0] // 2, x_sums.shape[0] - PAD
    singles = zip(decode_singles(y_sums, 2, few + PAD), decode_singles(y_lo, 2, y_lo.shape[0]))
    row, h2_row = [a + b for a, b in singles]
    for at, late in ((0, y_lo), (t, x_hi)):
        rows = slice(at, at + t)
        total = base[rows, :] + decode(late, t)
        w1_ref[rows, :] = (w_ref[rows, :].astype(F32) * total / row).astype(BF16)
    h2_col = jnp.broadcast_to(h2_row, (8, h2_row.shape[1])).T[: 2 * few, :1]
    low = decode(y_sums, few) + decode(y_lo, few, t + PAD)
    high = decode(x_sums, few) + decode(x_hi, few, t + PAD)
    w2_ref[...] = w2t_ref[...] * jnp.concatenate([low, high], axis=0) / h2_col


def parts(x):
    hi = x.astype(BF16)
    return hi, (x - hi.astype(F32)).astype(BF16)


def mm3(a, b, dims):
    (ah, al), (bh, bl) = a, b
    if ah.shape[dims[0]] <= 64:
        one, other = (jnp.concatenate(x, axis=d) for x, d in (((ah, ah, al), dims[0]), ((bh, bl, bh), dims[1])))
        return mm(one, other, dims)
    m = ah.shape[1 - dims[0]]
    if m <= 64:
        both = mm(jnp.concatenate((ah, al), axis=1 - dims[0]), bh, dims)
        return both[:m] + (both[m:] + mm(ah, bl, dims))
    return mm(ah, bh, dims) + (mm(ah, bl, dims) + mm(al, bh, dims))


def layer_two(n_ahead, h1_ref, w2t_ref, h2_ref, *refs):
    new_ref, sums_ref = refs[n_ahead : n_ahead + 2]
    copies = ahead((*refs[:n_ahead], h1_ref), refs[n_ahead + 2 : -1], refs[-1])
    h1, w2t, h2 = h1_ref[...], w2t_ref[...], h2_ref[...]
    k2, k1 = w2t.shape
    w2p = parts(w2t)
    ratio3 = h1 / mm3(w2p, parts(h2), (0, 0))
    h2_new = h2 * mm3(w2p, parts(ratio3), (1, 0)) / jnp.sum(w2t, axis=1, keepdims=True)
    new_ref[...] = h2_new
    h2p = parts(h2_new)
    ratio4 = h1 / mm3(w2p, h2p, (0, 0))
    sums_ref[:k2, :] = mm3(h2p, parts(ratio4), (1, 1))
    cells = h1.shape[1]
    row = jnp.ones((8, cells), BF16)
    sums_ref[k2 : k2 + 8, :] = sum(mm(row, x, (1, 1)) for x in parts(h1))
    sums_ref[k2 + 8 :, :] = jnp.zeros((8, k1), F32)
    sums_ref[k2 + 8 :, :k2] = sum(mm(row, x, (1, 1)) for x in h2p)
    for copy in copies:
        copy.wait()


def on_device(n_gene, n_cell, counts, w1, h1, w2, h2):
    genes, cells = counts.shape
    rows, k1 = w1.shape
    k2 = w2.shape[1]
    chips = n_cell // 2
    me = lax.axis_index("cell")
    core, chip = me % 2, me // 2
    line = n_cell == 8 and n_gene == 4 and genes * 4 < 32768
    cell = functools.partial(flip, axis="cell", size=n_cell)
    gene = functools.partial(flip, axis="gene", size=n_gene)
    after = lax.optimization_barrier
    at = jnp.stack([chip, core]).astype(jnp.int32)

    h1_low = h1.astype(BF16)
    new_shapes = (jax.ShapeDtypeStruct((k1, cells), F32), jax.ShapeDtypeStruct((k1, cells), BF16))
    if line:
        t = rows // 2
        w_x, w_y = cell(w1, bit=2), cell(w1, bit=4)
        w_0 = cell(w1, bit=1)

        v_mine, v_theirs = split_counts(at, counts, chips, rows)
        v_other = [cell(v, bit=1) for v in v_theirs]
        on_mine, on_theirs = ([Later(v) for v in some] for some in (v_mine, v_theirs))
        acc = first(((Later(w1), on_mine[0]), (w_0, on_theirs[0])), h1_low)
        w_x, w_y, *acc = after((w_x, w_y, *acc))
        half = jax.ShapeDtypeStruct((t, k1), BF16)
        y_lo, x_hi = plain(cut_halves, (half, half), w_y, w_x, name="cut_halves")
        d_lo, d_hi = cell(y_lo, bit=2), cell(x_hi, bit=4)
        w_x, w_y, x_hi, y_lo = after((w_x, w_y, x_hi, y_lo))
        x_0, y_0 = cell(w_x, bit=1), cell(w_y, bit=1)
        near = ((w_x, on_mine[1]), (w_y, on_mine[2]), (x_0, on_theirs[1]), (y_0, on_theirs[2]))
        acc = first(near, h1_low, acc)
        d_lo, d_hi, *acc = after((d_lo, d_hi, *acc))
        far = [cell(d, bit=1) for d in (d_lo, d_hi)]
        *v_far, own_lo, own_hi = plain_fetch(after((v_mine[3], v_theirs[3], d_lo, d_hi, *acc))[:4])
        z = lax.axis_index("gene")
        inner = jnp.where((z == 1) | (z == 2), 1, 0).astype(jnp.int32)[None]
        chunks = tuple(range(CHUNKS))
        piece = coded(k1, cells // 2 // CHUNKS)
        keep, *sent = first_and_split(
            ((own_lo, own_hi, v_far[0]), (*far, v_far[1])), h1_low, acc, inner,
            (jax.ShapeDtypeStruct((k1, cells // 2), F32),) + (piece,) * CHUNKS,
        )
        pair = []
        for i, x in enumerate(sent):
            got = gene(x, bit=1)
            extra = () if i else (x,)
            pair.append(plain(functools.partial(add_kept, i), piece, keep, got, *extra, name="add_pair"))
        mine = []
        for i, x in enumerate(pair):
            outs = piece if i else (piece, jax.ShapeDtypeStruct((8, k1), F32))
            mine.append(plain(add_coded, outs, x, gene(x, bit=3), name="add_cross"))
        (first_mine, col), *mine = mine
        mine = [first_mine, *mine]
        theirs = [gene(x, bit=1) for x in mine]
        h1_low2, h1_late = plain(
            functools.partial(h1_update, CHUNKS), new_shapes[::-1], *mine, *theirs, h1, col,
            flag=inner, name="h1_update",
        )
        h1_low2_other = cell(h1_low2, bit=1)
    else:
        col = None
        groups = [list(range(c, n_cell, 2)) for c in (0, 1)]
        w_half = lax.all_gather(w1, "cell", axis=0, tiled=True, axis_index_groups=groups)
        v_mine, v_theirs = split_counts(at * jnp.array([0, 1], jnp.int32), counts, chips, rows)
        v_other = [cell(v, bit=1) for v in v_theirs]
        halves = [[w[j * rows : (j + 1) * rows] for j in range(chips)] for w in (w_half, cell(w_half, bit=1))]
        each = min(chips, max(1, 512 // rows))
        acc = ()
        for i in range(0, chips, each):
            for w, v in zip(halves, (v_mine, v_theirs)):
                acc = first(tuple((w[j], v[j]) for j in range(i, i + each)), h1_low, acc)
        num, col = lax.psum(tuple(acc), "gene")
        col = jnp.broadcast_to(col[0][:, None], (k1, 128))
        h1_new, h1_low2 = plain(h1_update_plain, new_shapes, num, h1, col, name="h1_update")
        h1_low2_other, h1_late = cell(h1_low2, bit=1), h1_new

    w2t = w2.T
    vmem, hbm = pl.BlockSpec(memory_space=pltpu.VMEM), pl.BlockSpec(memory_space=pltpu.HBM)
    soon = [pltpu.with_memory_space_constraint(x, pltpu.HBM) for x in ((v_mine[3], d_lo, d_hi) if line else v_mine[:1])]
    h2_new, sums, *soon, h1_new = pl.pallas_call(
        functools.partial(layer_two, len(soon)),
        out_shape=(
            jax.ShapeDtypeStruct((k2, cells), F32),
            jax.ShapeDtypeStruct((k2 + 16, k1), F32),
            *(jax.ShapeDtypeStruct(x.shape, x.dtype) for x in soon),
            pltpu.HBM(h1.shape, F32),
        ),
        in_specs=[vmem] * 3 + [hbm] * len(soon),
        out_specs=[vmem] * (2 + len(soon)) + [hbm],
        scratch_shapes=[pltpu.SemaphoreType.DMA((len(soon) + 1,))],
        compiler_params=params(),
        name="layer_two",
    )(h1_late, w2t, h2, *soon)
    low2 = (h1_low2, h1_low2_other)
    if line:
        sums_in = cell(sums, bit=1)
        v_far, d_lo, d_hi = soon
        d_lo, d_hi = second(((d_lo, d_hi, v_far, v_other[3]),), rows, low2, ((False, False),))
        sums, sums_in, d_lo = after((sums, sums_in, d_lo))
        few = k2 // 2 + PAD
        with_sums = coded(t + few, k1)
        d_lo, d_hi = plain(
            functools.partial(pack, k2), (with_sums, with_sums), d_lo, d_hi, sums, sums_in, name="pack"
        )
        y_in, x_in = cell(d_lo, bit=2), cell(d_hi, bit=4)
        w_x, d_lo = after((w_x, d_lo))
        near = ((Later(w_x), on_mine[1], v_other[1]), (Later(w_y), on_mine[2], v_other[2]))
        x_lo, x_hi, y_lo, y_hi = second(near, rows, low2, ((True, False), (False, True)))
        x_lo_in, y_hi_in = cell(x_lo, bit=2), cell(y_hi, bit=4)
        sums_only = jax.ShapeDtypeStruct((few, k1), jnp.int16)
        x_hi, y_lo, x_sums, y_sums = plain(
            functools.partial(relay_add, k2), (with_sums, with_sums, sums_only, sums_only),
            x_hi, x_in, y_lo, y_in, d_lo, d_hi, name="relay_add",
        )
        x_hi_in, y_lo_in = cell(x_hi, bit=2), cell(y_lo, bit=4)
        w1_late, x_hi, x_lo_in, y_hi_in = after((w1, x_hi, x_lo_in, y_hi_in))
        (own,) = second(((Later(w1_late), on_mine[0], v_other[0]),), rows, low2, ((False,),))
        base, w1_late, w2t = plain(
            early_sum, tuple(jax.ShapeDtypeStruct(*x) for x in (((rows, k1), F32), (w1.shape, BF16), (w2t.shape, F32))),
            own, x_lo_in, y_hi_in, w1, w2t, name="early_sum",
        )
        w1_new, w2_new = plain(
            last_update, (jax.ShapeDtypeStruct((rows, k1), BF16), jax.ShapeDtypeStruct((k2, k1), F32)),
            base, x_hi_in, y_lo_in, x_sums, y_sums, w1_late, w2t, name="last_update",
        )
        w2_new = w2_new.T
    else:
        found = []
        for i in range(0, chips, each):
            some = tuple((halves[0][j], v_mine[j], v_other[j]) for j in range(i, i + each))
            found += second(some, rows, low2, ((False,),) * each)
        w1_num = lax.psum_scatter(
            jnp.concatenate(found), "cell", scatter_dimension=0, tiled=True, axis_index_groups=groups
        )
        sums = lax.psum(sums, "cell")
        w2_new = (w2t * sums[:k2] / sums[k2 + 8, :k2, None]).T
        w1_new = (w1.astype(F32) * w1_num / sums[k2 : k2 + 1]).astype(BF16)
    return (w1_new, h1_new, w2_new, h2_new)


def solution(mesh):
    placed = (P("gene", "cell"), P(("gene", "cell"), None), P(None, "cell"), P(), P(None, "cell"))
    return jax.shard_map(
        functools.partial(on_device, mesh.shape["gene"], mesh.shape["cell"]),
        mesh=mesh,
        in_specs=placed,
        out_specs=(P(("gene", "cell"), None), P(None, "cell"), P(), P(None, "cell")),
        check_vma=False,
    )
```

```python
import functools

import jax
import jax.numpy as jnp
from jax import lax
from jax.experimental import pallas as pl
from jax.experimental.pallas import tpu as pltpu
from jax.sharding import PartitionSpec as P

F32 = jnp.float32
BF16 = jnp.bfloat16
PAD = 16
CHUNKS = 2


def params(mib=16):
    return pltpu.CompilerParams(vmem_limit_bytes=mib * 1024 * 1024)


def mm(a, b, dims):
    return lax.dot_general(a, b, ((dims[:1], dims[1:]), ((), ())), preferred_element_type=F32)


def power_of(x):
    return jnp.ceil(jnp.log2(jnp.maximum(x, 1e-30)))


def encode(x, out_ref, extra=None, singles=(), at=0):
    rows, cols = x.shape
    power = power_of(jnp.max(x, axis=0, keepdims=True))
    q = jnp.minimum(x * (jnp.exp2(-power) * 65535.0) + 0.5, 65535.0)
    out_ref[at : at + rows, :] = (q.astype(jnp.int32) - 32768).astype(jnp.int16)
    lines = [power]
    if extra is not None:
        whole = jnp.floor(extra)
        for y in (whole, jnp.floor((extra - whole) * 32768.0 + 0.25)):
            lines += [y[:, i : i + cols] for i in range(0, y.shape[1], cols)]
    for y in singles:
        own = power_of(y)
        y = y * (jnp.exp2(-own) * 32767.0)
        whole = jnp.floor(y)
        lines += [own, whole, jnp.floor((y - whole) * 32768.0)]
    lines.append(jnp.zeros((PAD - len(lines), cols), F32))
    out_ref[at + rows : at + rows + PAD, :] = jnp.concatenate(lines, axis=0).astype(jnp.int32).astype(jnp.int16)


def pad_rows(ref, end):
    return ref[end - PAD : end, :].astype(jnp.int32).astype(F32)


def decode_extra(ref, width):
    n = width // ref.shape[1]
    lines = pad_rows(ref, ref.shape[0])
    lines = [lines[1 + i : 2 + i] for i in range(2 * n)]
    return jnp.concatenate(lines[:n], axis=1) + jnp.concatenate(lines[n:], axis=1) * (1.0 / 32768.0)


def decode_singles(ref, n, end):
    lines = pad_rows(ref, end)
    found = []
    for i in range(1, 1 + 3 * n, 3):
        unit = jnp.exp2(lines[i : i + 1]) * (1.0 / 32767.0)
        found.append((lines[i + 1 : i + 2] + lines[i + 2 : i + 3] * (1.0 / 32768.0)) * unit)
    return found


def decode(ref, rows=None, at=0):
    rows = ref.shape[0] - PAD if rows is None else rows
    unit = jnp.exp2(pad_rows(ref, at + rows + PAD)[:1]) * (1.0 / 65535.0)
    return (ref[at : at + rows, :].astype(jnp.int32) + 32768).astype(F32) * unit


def coded(rows, cols):
    return jax.ShapeDtypeStruct((rows + PAD, cols), jnp.int16)


def quotient(v, approx):
    return (v.astype(jnp.int32).astype(F32) / approx).astype(BF16)


def counts_body(chips, rows, at, v, *refs):
    outs, held, low, sems = refs[: 2 * chips], *refs[2 * chips :]
    copies = []
    for q in range(chips):
        start = pl.multiple_of((at[0] ^ q) * 2 * rows, 2 * rows)
        both = pl.ds(q * 2 * rows, 2 * rows)
        copies.append(pltpu.make_async_copy(v.at[pl.ds(start, 2 * rows), :], held.at[both, :], sems.at[q]))
        copies[-1].start()
    for q in range(chips):
        copies[q].wait()
        for slot, core in ((q, at[1]), (chips + q, 1 - at[1])):
            some = held[pl.ds(pl.multiple_of((2 * q + core) * rows, rows), rows), :]
            low[slot] = some.astype(jnp.int16)
            copies.append(pltpu.make_async_copy(low.at[slot], outs[slot], sems.at[chips + slot]))
            copies[-1].start()
    for copy in copies[chips:]:
        copy.wait()


def split_counts(at, counts, chips, rows):
    cells = counts.shape[1]
    out = pltpu.HBM((rows, cells), jnp.int16)
    smem, hbm = pl.BlockSpec(memory_space=pltpu.SMEM), pl.BlockSpec(memory_space=pltpu.HBM)
    outs = pl.pallas_call(
        functools.partial(counts_body, chips, rows),
        out_shape=(out,) * (2 * chips),
        in_specs=[smem, hbm],
        out_specs=[hbm] * (2 * chips),
        scratch_shapes=[
            pltpu.VMEM(counts.shape, counts.dtype),
            pltpu.VMEM((2 * chips, rows, cells), jnp.int16),
            pltpu.SemaphoreType.DMA((3 * chips,)),
        ],
        compiler_params=params(),
        name="split_counts",
    )(at, pltpu.with_memory_space_constraint(counts, pltpu.HBM))
    return outs[:chips], outs[chips:]


class Later:
    def __init__(self, array):
        self.array = array


def fetching(refs, later, scratch):
    sems, slots, found = scratch[-1] if later else None, iter(scratch), []
    for i, ref in enumerate(refs):
        copy = None
        if i in later:
            slot = next(slots)
            copy = pltpu.make_async_copy(ref, slot, sems.at[later.index(i)])
            copy.start()
            ref = slot
        found.append((ref, copy))
    return found


def ready(operand):
    ref, copy = operand
    if copy is not None:
        copy.wait()
    return ref[...]


def joined(operands):
    return jnp.concatenate([ready(x) for x in operands], axis=0) if len(operands) > 1 else ready(operands[0])


def ahead(sources, outs, sems):
    copies = [pltpu.make_async_copy(x, out, sems.at[i]) for i, (x, out) in enumerate(zip(sources, outs))]
    for copy in copies:
        copy.start()
    return copies


def fetch_body(n, *refs):
    for copy in ahead(refs[:n], refs[n : 2 * n], refs[-1]):
        copy.wait()


def plain_fetch(arrays):
    n = len(arrays)
    vmem, hbm = pl.BlockSpec(memory_space=pltpu.VMEM), pl.BlockSpec(memory_space=pltpu.HBM)
    return pl.pallas_call(
        functools.partial(fetch_body, n),
        out_shape=[jax.ShapeDtypeStruct(x.shape, x.dtype) for x in arrays],
        in_specs=[hbm] * n,
        out_specs=[vmem] * n,
        scratch_shapes=[pltpu.SemaphoreType.DMA((n,))],
        compiler_params=params(),
        name="fetch",
    )(*(pltpu.with_memory_space_constraint(x, pltpu.HBM) for x in arrays))


def first_body(groups, later, n_ahead, has_acc, h, *refs):
    n, n_later = sum(groups) + len(groups), len(later)
    refs, sems = (refs[:-1], refs[-1:]) if n_ahead else (refs, ())
    refs, scratch = (refs[:-n_later - 1] + sems, refs[-n_later - 1 :]) if later else (refs + sems, ())
    operands = fetching(refs[:n], later, scratch)
    copies, refs = (), refs[n:]
    if n_ahead:
        copies, refs = ahead(refs[:n_ahead], refs[-1 - n_ahead : -1], refs[-1]), refs[n_ahead : -1 - n_ahead]
    num_ref, col_ref = refs[-2:]
    total, col = (refs[0][...], refs[1][...]) if has_acc else (0.0, 0.0)
    for n in groups:
        w, v = joined(operands[:n]), operands[n]
        operands = operands[n + 1 :]
        approx = mm(w, h[...], (1, 0))
        total += mm(w, quotient(ready(v), approx), (0, 0))
        col += jnp.sum(w.astype(F32), axis=0, keepdims=True)
    num_ref[...] = total
    col_ref[...] = jnp.broadcast_to(col, col_ref.shape)
    for copy in copies:
        copy.wait()


def second_body(groups, later, n_ahead, codes, ha, hb, *refs):
    n, n_later = sum(groups) + 2 * len(groups), len(later)
    refs, scratch = (refs[:-n_later - 1], refs[-n_later - 1 :]) if later else (refs, ())
    operands, outs = fetching(refs[:n], later, scratch), refs[n:]
    for n, code in zip(groups, codes):
        pieces, v, operands = operands[:n], operands[n : n + 2], operands[n + 2 :]
        w = joined(pieces)
        total = 0.0
        for h, some in ((hb, v[1]), (ha, v[0])):
            low = h[...]
            approx = mm(w, low, (1, 0))
            total += mm(quotient(ready(some), approx), low, (1, 1))
        t = w.shape[0] // len(code)
        for k, coding in enumerate(code):
            out, outs = outs[0], outs[1:]
            part = total[k * t : (k + 1) * t]
            if coding:
                encode(part, out)
            else:
                out[...] = part


def products(body, flag, outs, groups, h, acc, name, fetch=()):
    n_h = len(h)
    sizes = tuple(len(g) - n_h for g in groups)
    flat = [x for g in groups for x in g]
    later = tuple(i for i, x in enumerate(flat) if isinstance(x, Later))
    vmem, hbm = pl.BlockSpec(memory_space=pltpu.VMEM), pl.BlockSpec(memory_space=pltpu.HBM)
    specs = [hbm if i in later else vmem for i in range(len(flat))]
    flat = [pltpu.with_memory_space_constraint(x.array, pltpu.HBM) if isinstance(x, Later) else x for x in flat]
    scratch = [pltpu.VMEM(flat[i].shape, flat[i].dtype) for i in later]
    if later:
        scratch.append(pltpu.SemaphoreType.DMA((len(later),)))
    fetch = [pltpu.with_memory_space_constraint(x, pltpu.HBM) for x in fetch]
    if fetch:
        scratch.append(pltpu.SemaphoreType.DMA((len(fetch),)))
    outs = (*outs, *(jax.ShapeDtypeStruct(x.shape, x.dtype) for x in fetch))
    args = [*h, *flat, *fetch, *acc]
    work = 2 * sum(x.shape[0] for x in flat) * h[0].shape[1]
    return pl.pallas_call(
        functools.partial(body, sizes, later, len(fetch), flag),
        out_shape=outs,
        in_specs=[vmem] * n_h + specs + [hbm] * len(fetch) + [vmem] * len(acc),
        out_specs=[vmem] * len(outs),
        scratch_shapes=scratch,
        input_output_aliases={len(args) - len(acc) + i: i for i in range(len(acc))},
        compiler_params=params(),
        cost_estimate=pl.CostEstimate(flops=2 * work * h[0].shape[0], bytes_accessed=work, transcendentals=0),
        name=name,
    )(*args)


def first(groups, h, acc=(), fetch=()):
    k1, cells = h.shape
    outs = (jax.ShapeDtypeStruct((k1, cells), F32), jax.ShapeDtypeStruct((8, k1), F32))
    return products(first_body, bool(acc), outs, groups, (h,), acc, "first_products", fetch)


def second(groups, rows, h, codes):
    k1 = h[0].shape[0]
    outs = []
    for code in codes:
        t = rows // len(code)
        outs += [coded(t, k1) if c else jax.ShapeDtypeStruct((t, k1), F32) for c in code]
    return products(second_body, codes, tuple(outs), groups, h, (), "second_products")


def plain(body, outs, *args, name, flag=None):
    vmem = pl.BlockSpec(memory_space=pltpu.VMEM)
    specs = [vmem] * len(args)
    if flag is not None:
        specs, args = [pl.BlockSpec(memory_space=pltpu.SMEM)] + specs, (flag, *args)
    out_specs = (vmem,) * len(outs) if isinstance(outs, tuple) else vmem
    return pl.pallas_call(
        body, out_shape=outs, in_specs=specs, out_specs=out_specs, compiler_params=params(), name=name
    )(*args)


def flip(x, axis, size, bit):
    return lax.ppermute(x, axis, [(i, i ^ bit) for i in range(size)])


def split_num(flag, num, col, keep_ref, *sends):
    inner = flag[0] == 1
    half = num.shape[1] // 2
    keep_ref[...] = jnp.where(inner, num[:, half:], num[:, :half])
    width = half // len(sends)
    for i, send in enumerate(sends):
        lo = num[:, i * width : (i + 1) * width]
        hi = num[:, half + i * width : half + (i + 1) * width]
        encode(jnp.where(inner, lo, hi), send, None if i else col[:1, :])


def first_and_split(groups, h, acc, flag, outs):
    sizes = tuple(len(g) - 1 for g in groups)
    flat = [x for g in groups for x in g]
    later = tuple(i for i, x in enumerate(flat) if isinstance(x, Later))
    n, n_outs, n_later = len(flat), len(outs), len(later)
    flat = [pltpu.with_memory_space_constraint(x.array, pltpu.HBM) if isinstance(x, Later) else x for x in flat]
    vmem, hbm = pl.BlockSpec(memory_space=pltpu.VMEM), pl.BlockSpec(memory_space=pltpu.HBM)

    def body(flag_ref, h_ref, *refs):
        inputs, out_refs, scratch = refs[: n + 2], refs[n + 2 : n + 2 + n_outs], refs[n + 2 + n_outs :]
        num, col = scratch[-2:]
        first_body(sizes, later, 0, True, h_ref, *inputs, num, col, *scratch[:-2])
        split_num(flag_ref, num, col, *out_refs)

    scratch = [pltpu.VMEM(flat[i].shape, flat[i].dtype) for i in later]
    if later:
        scratch.append(pltpu.SemaphoreType.DMA((n_later,)))
    return pl.pallas_call(
        body,
        out_shape=outs,
        in_specs=[pl.BlockSpec(memory_space=pltpu.SMEM), vmem] + [hbm if i in later else vmem for i in range(n)] + [vmem] * 2,
        out_specs=[vmem] * n_outs,
        scratch_shapes=scratch + [pltpu.VMEM(x.shape, x.dtype) for x in acc],
        compiler_params=params(),
        cost_estimate=pl.CostEstimate(
            flops=8 * flat[0].shape[0] * h.shape[0] * h.shape[1], bytes_accessed=4 * h.size, transcendentals=0
        ),
        name="first_and_split",
    )(flag, h, *flat, *acc)


def add_kept(i, keep, other, *refs):
    width, k1 = other.shape[1], keep.shape[0]
    extra = None if i else decode_extra(refs[0], k1) + decode_extra(other, k1)
    encode(keep[:, i * width : (i + 1) * width] + decode(other), refs[-1], extra)


def add_coded(one, other, out_ref, *col_ref):
    encode(decode(one) + decode(other), out_ref)
    for ref in col_ref:
        k1 = ref.shape[1]
        ref[...] = jnp.broadcast_to(decode_extra(one, k1) + decode_extra(other, k1), ref.shape)


def h1_update(n, flag, *refs):
    mine, theirs, (h1_ref, col_ref, low_ref, late_ref) = refs[:n], refs[n : 2 * n], refs[2 * n :]
    inner = flag[0] == 1
    half = h1_ref.shape[1] // 2
    width = half // n
    col = col_ref[...].T[:, :1]
    for i in range(n):
        a, b = decode(mine[i]), decode(theirs[i])
        for at, num in ((i * width, jnp.where(inner, b, a)), (half + i * width, jnp.where(inner, a, b))):
            new = h1_ref[:, at : at + width] * num / col
            late_ref[:, at : at + width] = new
            low_ref[:, at : at + width] = new.astype(BF16)


def h1_update_plain(num, h1_ref, col_ref, new_ref, low_ref):
    new = h1_ref[...] * num[...] / col_ref[:, :1]
    new_ref[...] = new
    low_ref[...] = new.astype(BF16)


def cut_halves(a_ref, b_ref, lo_ref, hi_ref):
    t = lo_ref.shape[0]
    lo_ref[...] = a_ref[:t, :]
    hi_ref[...] = b_ref[t:, :]


def pack(k2, lo, hi, sums, sums_in, lo_ref, hi_ref):
    total = sums[...] + sums_in[...]
    t, half = lo.shape[0], k2 // 2
    encode(lo[...], lo_ref)
    encode(total[:half], lo_ref, singles=(total[k2 : k2 + 1], total[k2 + 8 : k2 + 9]), at=t + PAD)
    encode(hi[...], hi_ref)
    encode(total[half:k2], hi_ref, at=t + PAD)


def relay_add(k2, x, x_in, y, y_in, lo, hi, x_ref, y_ref, x_sums, y_sums):
    rows = x.shape[0]
    at, few = rows + PAD, k2 // 2
    encode(x[...] + decode(x_in, rows), x_ref)
    encode(y[...] + decode(y_in, rows), y_ref)
    one = [a + b for a, b in zip(decode_singles(lo, 2, lo.shape[0]), decode_singles(y_in, 2, lo.shape[0]))]
    encode(decode(lo, few, at) + decode(y_in, few, at), y_sums, singles=one)
    encode(decode(hi, few, at) + decode(x_in, few, at), x_sums)
    x_ref[at:, :] = x_sums[...]
    y_ref[at:, :] = y_sums[...]


def early_sum(own, x_lo, y_hi, w_ref, w2t_ref, out_ref, w_out, w2t_out):
    w_out[...], w2t_out[...] = w_ref[...], w2t_ref[...]
    t = x_lo.shape[0] - PAD
    out_ref[:t, :] = own[:t, :] + decode(x_lo)
    out_ref[t:, :] = own[t:, :] + decode(y_hi)


def last_update(base, x_hi, y_lo, x_sums, y_sums, w_ref, w2t_ref, w1_ref, w2_ref):
    t, few = base.shape[0] // 2, x_sums.shape[0] - PAD
    singles = zip(decode_singles(y_sums, 2, few + PAD), decode_singles(y_lo, 2, y_lo.shape[0]))
    row, h2_row = [a + b for a, b in singles]
    for at, late in ((0, y_lo), (t, x_hi)):
        rows = slice(at, at + t)
        total = base[rows, :] + decode(late, t)
        w1_ref[rows, :] = (w_ref[rows, :].astype(F32) * total / row).astype(BF16)
    h2_col = jnp.broadcast_to(h2_row, (8, h2_row.shape[1])).T[: 2 * few, :1]
    low = decode(y_sums, few) + decode(y_lo, few, t + PAD)
    high = decode(x_sums, few) + decode(x_hi, few, t + PAD)
    w2_ref[...] = w2t_ref[...] * jnp.concatenate([low, high], axis=0) / h2_col


def parts(x):
    hi = x.astype(BF16)
    return hi, (x - hi.astype(F32)).astype(BF16)


def mm3(a, b, dims):
    (ah, al), (bh, bl) = a, b
    if ah.shape[dims[0]] <= 64:
        one, other = (jnp.concatenate(x, axis=d) for x, d in (((ah, ah, al), dims[0]), ((bh, bl, bh), dims[1])))
        return mm(one, other, dims)
    m = ah.shape[1 - dims[0]]
    if m <= 64:
        both = mm(jnp.concatenate((ah, al), axis=1 - dims[0]), bh, dims)
        return both[:m] + (both[m:] + mm(ah, bl, dims))
    return mm(ah, bh, dims) + (mm(ah, bl, dims) + mm(al, bh, dims))


def layer_two(n_ahead, h1_ref, w2t_ref, h2_ref, *refs):
    new_ref, sums_ref = refs[n_ahead : n_ahead + 2]
    copies = ahead((*refs[:n_ahead], h1_ref), refs[n_ahead + 2 : -1], refs[-1])
    h1, w2t, h2 = h1_ref[...], w2t_ref[...], h2_ref[...]
    k2, k1 = w2t.shape
    w2p = parts(w2t)
    ratio3 = h1 / mm3(w2p, parts(h2), (0, 0))
    h2_new = h2 * mm3(w2p, parts(ratio3), (1, 0)) / jnp.sum(w2t, axis=1, keepdims=True)
    new_ref[...] = h2_new
    h2p = parts(h2_new)
    ratio4 = h1 / mm3(w2p, h2p, (0, 0))
    sums_ref[:k2, :] = mm3(h2p, parts(ratio4), (1, 1))
    cells = h1.shape[1]
    row = jnp.ones((8, cells), BF16)
    sums_ref[k2 : k2 + 8, :] = sum(mm(row, x, (1, 1)) for x in parts(h1))
    sums_ref[k2 + 8 :, :] = jnp.zeros((8, k1), F32)
    sums_ref[k2 + 8 :, :k2] = sum(mm(row, x, (1, 1)) for x in h2p)
    for copy in copies:
        copy.wait()


def on_device(n_gene, n_cell, counts, w1, h1, w2, h2):
    genes, cells = counts.shape
    rows, k1 = w1.shape
    k2 = w2.shape[1]
    chips = n_cell // 2
    me = lax.axis_index("cell")
    core, chip = me % 2, me // 2
    line = n_cell == 8 and n_gene == 4 and genes * 4 < 32768
    cell = functools.partial(flip, axis="cell", size=n_cell)
    gene = functools.partial(flip, axis="gene", size=n_gene)
    after = lax.optimization_barrier
    at = jnp.stack([chip, core]).astype(jnp.int32)

    h1_low = h1.astype(BF16)
    new_shapes = (jax.ShapeDtypeStruct((k1, cells), F32), jax.ShapeDtypeStruct((k1, cells), BF16))
    if line:
        t = rows // 2
        w_x, w_y = cell(w1, bit=2), cell(w1, bit=4)
        w_0 = cell(w1, bit=1)

        v_mine, v_theirs = split_counts(at, counts, chips, rows)
        v_other = [cell(v, bit=1) for v in v_theirs]
        on_mine, on_theirs = ([Later(v) for v in some] for some in (v_mine, v_theirs))
        acc = first(((Later(w1), on_mine[0]), (w_0, on_theirs[0])), h1_low)
        w_x, w_y, *acc = after((w_x, w_y, *acc))
        half = jax.ShapeDtypeStruct((t, k1), BF16)
        y_lo, x_hi = plain(cut_halves, (half, half), w_y, w_x, name="cut_halves")
        d_lo, d_hi = cell(y_lo, bit=2), cell(x_hi, bit=4)
        x_0, y_0 = cell(w_x, bit=1), cell(w_y, bit=1)
        near = ((w_x, on_mine[1]), (w_y, on_mine[2]), (x_0, on_theirs[1]), (y_0, on_theirs[2]))
        acc = first(near, h1_low, acc)
        d_lo, d_hi, *acc = after((d_lo, d_hi, *acc))
        far = [cell(d, bit=1) for d in (d_lo, d_hi)]
        *v_far, own_lo, own_hi = plain_fetch(after((v_mine[3], v_theirs[3], d_lo, d_hi, *acc))[:4])
        z = lax.axis_index("gene")
        inner = jnp.where((z == 1) | (z == 2), 1, 0).astype(jnp.int32)[None]
        chunks = tuple(range(CHUNKS))
        piece = coded(k1, cells // 2 // CHUNKS)
        keep, *sent = first_and_split(
            ((own_lo, own_hi, v_far[0]), (*far, v_far[1])), h1_low, acc, inner,
            (jax.ShapeDtypeStruct((k1, cells // 2), F32),) + (piece,) * CHUNKS,
        )
        pair = []
        for i, x in enumerate(sent):
            got = gene(x, bit=1)
            extra = () if i else (x,)
            pair.append(plain(functools.partial(add_kept, i), piece, keep, got, *extra, name="add_pair"))
        mine = []
        for i, x in enumerate(pair):
            outs = piece if i else (piece, jax.ShapeDtypeStruct((8, k1), F32))
            mine.append(plain(add_coded, outs, x, gene(x, bit=3), name="add_cross"))
        (first_mine, col), *mine = mine
        mine = [first_mine, *mine]
        theirs = [gene(x, bit=1) for x in mine]
        h1_low2, h1_late = plain(
            functools.partial(h1_update, CHUNKS), new_shapes[::-1], *mine, *theirs, h1, col,
            flag=inner, name="h1_update",
        )
        h1_low2_other = cell(h1_low2, bit=1)
    else:
        col = None
        groups = [list(range(c, n_cell, 2)) for c in (0, 1)]
        w_half = lax.all_gather(w1, "cell", axis=0, tiled=True, axis_index_groups=groups)
        v_mine, v_theirs = split_counts(at * jnp.array([0, 1], jnp.int32), counts, chips, rows)
        v_other = [cell(v, bit=1) for v in v_theirs]
        halves = [[w[j * rows : (j + 1) * rows] for j in range(chips)] for w in (w_half, cell(w_half, bit=1))]
        each = min(chips, max(1, 512 // rows))
        acc = ()
        for i in range(0, chips, each):
            for w, v in zip(halves, (v_mine, v_theirs)):
                acc = first(tuple((w[j], v[j]) for j in range(i, i + each)), h1_low, acc)
        num, col = lax.psum(tuple(acc), "gene")
        col = jnp.broadcast_to(col[0][:, None], (k1, 128))
        h1_new, h1_low2 = plain(h1_update_plain, new_shapes, num, h1, col, name="h1_update")
        h1_low2_other, h1_late = cell(h1_low2, bit=1), h1_new

    w2t = w2.T
    vmem, hbm = pl.BlockSpec(memory_space=pltpu.VMEM), pl.BlockSpec(memory_space=pltpu.HBM)
    soon = [pltpu.with_memory_space_constraint(x, pltpu.HBM) for x in ((v_mine[3], d_lo, d_hi) if line else v_mine[:1])]
    h2_new, sums, *soon, h1_new = pl.pallas_call(
        functools.partial(layer_two, len(soon)),
        out_shape=(
            jax.ShapeDtypeStruct((k2, cells), F32),
            jax.ShapeDtypeStruct((k2 + 16, k1), F32),
            *(jax.ShapeDtypeStruct(x.shape, x.dtype) for x in soon),
            pltpu.HBM(h1.shape, F32),
        ),
        in_specs=[vmem] * 3 + [hbm] * len(soon),
        out_specs=[vmem] * (2 + len(soon)) + [hbm],
        scratch_shapes=[pltpu.SemaphoreType.DMA((len(soon) + 1,))],
        compiler_params=params(),
        name="layer_two",
    )(h1_late, w2t, h2, *soon)
    low2 = (h1_low2, h1_low2_other)
    if line:
        sums_in = cell(sums, bit=1)
        v_far, d_lo, d_hi = soon
        d_lo, d_hi = second(((d_lo, d_hi, v_far, v_other[3]),), rows, low2, ((False, False),))
        sums, sums_in, d_lo = after((sums, sums_in, d_lo))
        few = k2 // 2 + PAD
        with_sums = coded(t + few, k1)
        d_lo, d_hi = plain(
            functools.partial(pack, k2), (with_sums, with_sums), d_lo, d_hi, sums, sums_in, name="pack"
        )
        y_in, x_in = cell(d_lo, bit=2), cell(d_hi, bit=4)
        w_x, d_lo = after((w_x, d_lo))
        near = ((Later(w_x), on_mine[1], v_other[1]), (Later(w_y), on_mine[2], v_other[2]))
        x_lo, x_hi, y_lo, y_hi = second(near, rows, low2, ((True, False), (False, True)))
        x_lo_in, y_hi_in = cell(x_lo, bit=2), cell(y_hi, bit=4)
        sums_only = jax.ShapeDtypeStruct((few, k1), jnp.int16)
        x_hi, y_lo, x_sums, y_sums = plain(
            functools.partial(relay_add, k2), (with_sums, with_sums, sums_only, sums_only),
            x_hi, x_in, y_lo, y_in, d_lo, d_hi, name="relay_add",
        )
        x_hi_in, y_lo_in = cell(x_hi, bit=2), cell(y_lo, bit=4)
        w1_late, x_hi, x_lo_in, y_hi_in = after((w1, x_hi, x_lo_in, y_hi_in))
        (own,) = second(((Later(w1_late), on_mine[0], v_other[0]),), rows, low2, ((False,),))
        base, w1_late, w2t = plain(
            early_sum, tuple(jax.ShapeDtypeStruct(*x) for x in (((rows, k1), F32), (w1.shape, BF16), (w2t.shape, F32))),
            own, x_lo_in, y_hi_in, w1, w2t, name="early_sum",
        )
        w1_new, w2_new = plain(
            last_update, (jax.ShapeDtypeStruct((rows, k1), BF16), jax.ShapeDtypeStruct((k2, k1), F32)),
            base, x_hi_in, y_lo_in, x_sums, y_sums, w1_late, w2t, name="last_update",
        )
        w2_new = w2_new.T
    else:
        found = []
        for i in range(0, chips, each):
            some = tuple((halves[0][j], v_mine[j], v_other[j]) for j in range(i, i + each))
            found += second(some, rows, low2, ((False,),) * each)
        w1_num = lax.psum_scatter(
            jnp.concatenate(found), "cell", scatter_dimension=0, tiled=True, axis_index_groups=groups
        )
        sums = lax.psum(sums, "cell")
        w2_new = (w2t * sums[:k2] / sums[k2 + 8, :k2, None]).T
        w1_new = (w1.astype(F32) * w1_num / sums[k2 : k2 + 1]).astype(BF16)
    return (w1_new, h1_new, w2_new, h2_new)


def solution(mesh):
    placed = (P("gene", "cell"), P(("gene", "cell"), None), P(None, "cell"), P(), P(None, "cell"))
    return jax.shard_map(
        functools.partial(on_device, mesh.shape["gene"], mesh.shape["cell"]),
        mesh=mesh,
        in_specs=placed,
        out_specs=(P(("gene", "cell"), None), P(None, "cell"), P(), P(None, "cell")),
        check_vma=False,
    )
```
